32 devices in a mesh: section: 2 (over core), ctx: 4 (over y, x), fsdp: 4 (over z).
Axes of the slice: x: 2, y: 2, z: 4, core: 2. Of those that a mesh axis runs over, the one named last changes fastest.
Arguments:
- tokens: bfloat16 [8, 1024, 1024], P('fsdp', 'ctx'), may hold values from -6 to 6
- cotangent: bfloat16 [8, 1024, 1024], P('fsdp', 'ctx'), may hold values from -6 to 6
- segment_ids: int32 [8, 1024], P('fsdp'), may hold values from 0 to 3, never falling along the last dimension, each value on 1 to 512 neighbouring positions
- w_qkv: float32 [2, 1024, 3072], P('section', 'fsdp'), may hold values from -0.1875 to 0.1875
- w_out: float32 [2, 1024, 1024], P('section', 'fsdp'), may hold values from -1 to 1
- w_up: float32 [2, 1024, 4096], P('section', 'fsdp'), may hold values from -0.1875 to 0.1875
- w_down: float32 [2, 4096, 1024], P('section', 'fsdp'), may hold values from -0.09375 to 0.09375
- gain_attn: float32 [2, 1024], P('section', 'fsdp'), may hold values from 0.5 to 1.5
- gain_mlp: float32 [2, 1024], P('section', 'fsdp'), may hold values from 0.5 to 1.5
- row_qkv: float32 [2, 1024], P('section', 'fsdp'), may hold values from 29.4912 to 4259.84
- col_qkv: float32 [2, 3072], P('section'), may hold values from 106.496 to 983.04
- row_out: float32 [2, 1024], P('section', 'fsdp'), may hold values from 2.21184 to 319.488
- col_out: float32 [2, 1024], P('section'), may hold values from 8.192 to 81.92
- row_up: float32 [2, 1024], P('section', 'fsdp'), may hold values from 32.768 to 4751.36
- col_up: float32 [2, 4096], P('section'), may hold values from 122.88 to 1105.92
- row_down: float32 [2, 4096], P('section', 'fsdp'), may hold values from 110.592 to 15728.64
- col_down: float32 [2, 1024], P('section'), may hold values from 409.6 to 3686.4
- var_attn: float32 [2, 1024], P('section', 'fsdp'), may hold values from 819.2 to 8192
- var_mlp: float32 [2, 1024], P('section', 'fsdp'), may hold values from 819.2 to 8192
Outputs:
- hidden: bfloat16 [2, 8, 1024, 1024], P('section', 'fsdp', 'ctx')
- input_grads: bfloat16 [2, 8, 1024, 1024], P('section', 'fsdp', 'ctx')
- grad_qkv: float32 [2, 1024, 3072], P('section', 'fsdp')
- grad_out: float32 [2, 1024, 1024], P('section', 'fsdp')
- grad_up: float32 [2, 1024, 4096], P('section', 'fsdp')
- grad_down: float32 [2, 4096, 1024], P('section', 'fsdp')
- grad_gain_attn: float32 [2, 1024], P('section', 'fsdp')
- grad_gain_mlp: float32 [2, 1024], P('section', 'fsdp')
- new_qkv: float32 [2, 1024, 3072], P('section', 'fsdp')
- new_out: float32 [2, 1024, 1024], P('section', 'fsdp')
- new_up: float32 [2, 1024, 4096], P('section', 'fsdp')
- new_down: float32 [2, 4096, 1024], P('section', 'fsdp')
- new_gain_attn: float32 [2, 1024], P('section', 'fsdp')
- new_gain_mlp: float32 [2, 1024], P('section', 'fsdp')
- new_row_qkv: float32 [2, 1024], P('section', 'fsdp')
- new_col_qkv: float32 [2, 3072], P('section')
- new_row_out: float32 [2, 1024], P('section', 'fsdp')
- new_col_out: float32 [2, 1024], P('section')
- new_row_up: float32 [2, 1024], P('section', 'fsdp')
- new_col_up: float32 [2, 4096], P('section')
- new_row_down: float32 [2, 4096], P('section', 'fsdp')
- new_col_down: float32 [2, 1024], P('section')
- new_var_attn: float32 [2, 1024], P('section', 'fsdp')
- new_var_mlp: float32 [2, 1024], P('section', 'fsdp')
- clip_ratio: float32 [2, 6], P('section')
The draws below stay inside these ranges and needn't reach their ends.
Inputs may be any that keep to these rules, and one draw needn't show every extreme that they name: `segment_ids`: within a sequence the ids never fall; each id covers 1 to 512 positions of its sequence and one covers exactly 512.
All inputs are finite; a program needn't handle non-finite values.
Results may differ from the reference program's by a relative error of at most 0.025.
Values may be sent and summed in bfloat16 or wider, within the bound.
No kernel may reach another device: no remote copies, remote signals or barrier semaphores. Data moves between devices by JAX's collectives and lax.ppermute only.
A program may use at most 384 MiB of HBM per device.

```python
import math
import jax
import jax.numpy as jnp
import numpy as np
from jax import lax

D = 1024
HEADS = 16
FF = 4096
LEN = 1024
NSEQ = 8
TOKENS = 8192


def ramp_state(key, row_count, base_scale):
    position = jnp.arange(row_count, dtype=jnp.float32) / max(row_count - 1, 1)
    upper_end, lower_end = (5.0, 0.2)
    factor = jnp.exp(jax.random.uniform(key, (2, row_count), jnp.float32, math.log(0.6), math.log(1.6)))
    ramp = jnp.exp(math.log(upper_end) + (math.log(lower_end) - math.log(upper_end)) * position)
    return (base_scale * factor * ramp[None, :]).astype(jnp.float32)


def draw_row_qkv(key, part):
    return ramp_state(jax.random.fold_in(key, 11), D, 0.04 * TOKENS)


def draw_row_out(key, part):
    return ramp_state(jax.random.fold_in(key, 12), D, 0.003 * TOKENS)


def draw_row_up(key, part):
    return ramp_state(jax.random.fold_in(key, 13), D, 0.045 * TOKENS)


def draw_row_down(key, part):
    return ramp_state(jax.random.fold_in(key, 14), FF, 0.15 * TOKENS)


def shard_levels(rng, extent, pieces, least, high):
    def one(axis_at, shards_of):
        heights = jax.random.uniform(jax.random.fold_in(jax.random.fold_in(rng, 6), axis_at), (shards_of,), jnp.float32, least / len(pieces), high / len(pieces))
        return jnp.repeat(jnp.exp(heights), extent[axis_at] // shards_of).reshape((-1,) + (1,) * (len(extent) - axis_at - 1))

    factor_of = one(*pieces[0])
    for cut in pieces[1:]:
        factor_of = factor_of * one(*cut)
    return factor_of


def length_profile(count, total, reach, skew):
    loads = [(1 << 20) // math.isqrt(standing ** skew) + 1 for standing in range(2, count + 1)]
    surplus, counts = total - reach - (count - 1), [1] * (count - 1)
    while surplus > 0:
        candidates = [i for i in range(count - 1) if counts[i] < reach]
        pool, left = sum([loads[i] for i in candidates]), surplus
        for i in candidates:
            more = min(reach - counts[i], max(1, left * loads[i] // pool), surplus)
            counts[i] = counts[i] + more
            surplus = surplus - more
    return np.array([reach] + counts)


def uneven(stream_key, amount, total, bound, skew):
    if amount == 2:
        one = jax.random.randint(stream_key, (), max(1, total - bound), min(bound, total - 1) + 1)
        return jnp.stack([one, total - one])
    tallies = jnp.asarray(length_profile(amount, total, bound, skew), jnp.int32)
    pairs = (amount - 1) // 2
    giver, receiver = tallies[1:1 + 2 * pairs:2], tallies[2:2 + 2 * pairs:2]
    margin = jnp.minimum(giver - 1, bound - receiver)
    shifted = jax.random.randint(jax.random.fold_in(stream_key, 1), (pairs,), 0, 1 << 20) % (margin + 1)
    tallies = tallies.at[1:1 + 2 * pairs:2].set(giver - shifted).at[2:2 + 2 * pairs:2].set(receiver + shifted)
    return tallies[jax.random.permutation(jax.random.fold_in(stream_key, 2), amount)]


def scatter_about(rng, shape, deviation, reach, pieces=(), held_as=jnp.bfloat16):
    level = shard_levels(rng, shape, pieces, -0.22, 0.18) if pieces else 1.0
    values = jax.random.normal(rng, shape, jnp.float32) * deviation * level
    return jnp.minimum(jnp.maximum(values, -reach), reach).astype(held_as)


def setup_inputs(seed: int = 0) -> dict:
    arg_keys = jax.random.split(jax.random.key(seed), 20)
    tokens = scatter_about(arg_keys[0], (NSEQ, LEN, D), 1.0, 6.0, ((0, 4), (1, 4)))
    cotangent = scatter_about(arg_keys[1], (NSEQ, LEN, D), 1.0, 6.0, ((0, 4), (1, 4)))
    segment_ids = jax.vmap(lambda own: jnp.searchsorted(jnp.cumsum(uneven(own, 4, LEN, LEN // 2, 0)), jnp.arange(LEN), side="right"))(jax.random.split(arg_keys[2], NSEQ)).reshape((NSEQ, LEN)).astype(jnp.int32)
    w_qkv = scatter_about(arg_keys[3], (2, D, 3 * D), D ** -0.5, 0.1875, ((0, 2), (1, 4)), jnp.float32)
    w_out = scatter_about(arg_keys[4], (2, D, D), (D // 32) ** -0.5, 1.0, ((0, 2), (1, 4)), jnp.float32)
    w_up = scatter_about(arg_keys[5], (2, D, FF), D ** -0.5, 0.1875, ((0, 2), (1, 4)), jnp.float32)
    w_down = scatter_about(arg_keys[6], (2, FF, D), FF ** -0.5, 0.09375, ((0, 2), (1, 4)), jnp.float32)
    gain_attn = jnp.clip(1.0 + 0.1 * jax.random.normal(arg_keys[7], (2, D), jnp.float32), 0.5, 1.5)
    gain_mlp = jnp.clip(1.0 + 0.1 * jax.random.normal(arg_keys[8], (2, D), jnp.float32), 0.5, 1.5)
    row_qkv = draw_row_qkv(jax.random.fold_in(arg_keys[19], 71), 0)
    col_qkv = jnp.clip(jnp.exp(math.log(983.04) - 2.2225423 * jax.random.uniform(arg_keys[10], (2, 3 * D), jnp.float32) ** shard_levels(arg_keys[10], (2, 3 * D), ((0, 2),), -0.2, 0.2)), 106.496, 983.04)
    row_out = draw_row_out(jax.random.fold_in(arg_keys[19], 71), 0)
    col_out = jnp.clip(jnp.exp(math.log(81.92) - 2.30258502 * jax.random.uniform(arg_keys[12], (2, D), jnp.float32) ** shard_levels(arg_keys[12], (2, D), ((0, 2),), -0.2, 0.2)), 8.192, 81.92)
    row_up = draw_row_up(jax.random.fold_in(arg_keys[19], 71), 0)
    col_up = jnp.clip(jnp.exp(math.log(1105.92) - 2.1972246 * jax.random.uniform(arg_keys[14], (2, FF), jnp.float32) ** shard_levels(arg_keys[14], (2, FF), ((0, 2),), -0.2, 0.2)), 122.88, 1105.92)
    row_down = draw_row_down(jax.random.fold_in(arg_keys[19], 71), 0)
    col_down = jnp.clip(jnp.exp(math.log(3686.4) - 2.1972245 * jax.random.uniform(arg_keys[16], (2, D), jnp.float32) ** shard_levels(arg_keys[16], (2, D), ((0, 2),), -0.2, 0.2)), 409.6, 3686.4)
    var_attn = jnp.clip(jnp.exp(math.log(8192.0) - 2.3025851 * jax.random.uniform(arg_keys[17], (2, D), jnp.float32) ** shard_levels(arg_keys[17], (2, D), ((0, 2), (1, 4)), -0.2, 0.2)), 819.2, 8192.0)
    var_mlp = jnp.clip(jnp.exp(math.log(8192.0) - 2.3025851 * jax.random.uniform(arg_keys[18], (2, D), jnp.float32) ** shard_levels(arg_keys[18], (2, D), ((0, 2), (1, 4)), -0.2, 0.2)), 819.2, 8192.0)
    return {"tokens": tokens, "cotangent": cotangent, "segment_ids": segment_ids, "w_qkv": w_qkv, "w_out": w_out, "w_up": w_up, "w_down": w_down, "gain_attn": gain_attn, "gain_mlp": gain_mlp, "row_qkv": row_qkv, "col_qkv": col_qkv, "row_out": row_out, "col_out": col_out, "row_up": row_up, "col_up": col_up, "row_down": row_down, "col_down": col_down, "var_attn": var_attn, "var_mlp": var_mlp}


decay_rate = 0.5
clip_level = 0.5
step_rate = 1.0
norm_eps = 1e-05
weight_eps = 1e-06
mask_fill = -1e+30
highest = lax.Precision.HIGHEST

@jax.custom_vjp
def low(v):
    return lax.optimization_barrier(v.astype(jnp.bfloat16)).astype(jnp.float32)

@jax.custom_vjp
def low_back(v):
    return v

def low_keep(v):
    return (low(v), None)

def low_pass(kept, grad):
    return (grad,)

def back_keep(v):
    return (v, None)

def back_low(kept, grad):
    return (low(grad),)
low.defvjp(low_keep, low_pass)
low_back.defvjp(back_keep, back_low)

def layer_norm(values, gain):
    center = values - lax.optimization_barrier(jnp.mean(values, axis=-1, keepdims=True))
    spread = lax.optimization_barrier(jnp.mean(center * center, axis=-1, keepdims=True))
    return center * lax.rsqrt(spread + norm_eps) * gain

def layer_group(inputs, segments, qkv_low, out_low, up_low, down_low, attn_gain, mlp_gain):
    group_size, seq_len, model_width = inputs.shape
    head_dim = model_width // HEADS
    scale_factor = head_dim ** (-0.5)
    projected = low_back(low(jnp.einsum('gld,de->gle', inputs, qkv_low, precision=highest)))
    queries = projected[:, :, :model_width].reshape(group_size, seq_len, HEADS, head_dim)
    key_rows = projected[:, :, model_width:2 * model_width].reshape(group_size, seq_len, HEADS, head_dim)
    value_rows = projected[:, :, 2 * model_width:].reshape(group_size, seq_len, HEADS, head_dim)
    scores = low_back(jnp.einsum('gqhd,gkhd->ghqk', queries, key_rows, precision=highest) * scale_factor)
    same_doc = segments[:, None, :, None] == segments[:, None, None, :]
    attn_weights = jax.nn.softmax(jnp.where(same_doc, scores, mask_fill), axis=-1)
    context = jnp.einsum('ghqk,gkhd->gqhd', low(attn_weights), value_rows, precision=highest)
    context = low_back(low(context.reshape(group_size, seq_len, model_width)))
    branch = low_back(jnp.einsum('gld,de->gle', context, out_low, precision=highest))
    normed = layer_norm(inputs + branch, attn_gain)
    upward = low_back(jnp.einsum('gld,df->glf', low(normed), up_low, precision=highest))
    activated = low(jax.nn.gelu(upward, approximate=False))
    downward = low_back(jnp.einsum('glf,fd->gld', activated, down_low, precision=highest))
    return layer_norm(normed + downward, mlp_gain)

def run_layer(inputs, segment_ids, qkv_master, out_master, up_master, down_master, attn_master, mlp_master):
    group_size = math.gcd(NSEQ, max(1, 4096 // LEN))
    qkv_low = low(qkv_master)
    out_low = low(out_master)
    up_low = low(up_master)
    down_low = low(down_master)
    attn_gain = low(attn_master)
    mlp_gain = low(mlp_master)
    grouped = inputs.reshape(NSEQ // group_size, group_size, LEN, D)
    grouped_ids = segment_ids.reshape(NSEQ // group_size, group_size, LEN)

    def apply_group(group_pair):
        return layer_group(group_pair[0], group_pair[1], qkv_low, out_low, up_low, down_low, attn_gain, mlp_gain)
    outputs = lax.map(jax.checkpoint(apply_group), (grouped, grouped_ids))
    return outputs.reshape(NSEQ, LEN, D)

def factored_update(master, gradient, row_old, col_old):
    square = gradient * gradient
    row_new = decay_rate * row_old + (1.0 - decay_rate) * lax.optimization_barrier(jnp.mean(square, axis=1))
    col_new = decay_rate * col_old + (1.0 - decay_rate) * lax.optimization_barrier(jnp.mean(square, axis=0))
    second_moment = row_new[:, None] * col_new[None, :] / jnp.mean(row_new)
    update = gradient * lax.rsqrt(second_moment)
    clip_ratio = jnp.sqrt(jnp.mean(update * update))
    weight_scale = jnp.sqrt(jnp.mean(master * master) + weight_eps)
    fresh_master = master - step_rate * weight_scale * update / jnp.maximum(1.0, clip_ratio / clip_level)
    return (fresh_master, row_new, col_new, clip_ratio)

def vector_update(master, gradient, moment_old):
    moment_new = decay_rate * moment_old + (1.0 - decay_rate) * gradient * gradient
    update = gradient * lax.rsqrt(moment_new)
    clip_ratio = jnp.sqrt(jnp.mean(update * update))
    weight_scale = jnp.sqrt(jnp.mean(master * master) + weight_eps)
    fresh_master = master - step_rate * weight_scale * update / jnp.maximum(1.0, clip_ratio / clip_level)
    return (fresh_master, moment_new, clip_ratio)

def reference(tokens, cotangent, segment_ids, w_qkv, w_out, w_up, w_down, gain_attn, gain_mlp, row_qkv, col_qkv, row_out, col_out, row_up, col_up, row_down, col_down, var_attn, var_mlp):

    def apply_layer(inputs, qkv_master, out_master, up_master, down_master, attn_master, mlp_master):
        return run_layer(inputs, segment_ids, qkv_master, out_master, up_master, down_master, attn_master, mlp_master)
    early_out, early_back = jax.vjp(apply_layer, tokens.astype(jnp.float32), w_qkv[0], w_out[0], w_up[0], w_down[0], gain_attn[0], gain_mlp[0])
    middle = early_out.astype(jnp.bfloat16)
    late_out, late_back = jax.vjp(apply_layer, middle.astype(jnp.float32), w_qkv[1], w_out[1], w_up[1], w_down[1], gain_attn[1], gain_mlp[1])
    late_grads = late_back(cotangent.astype(jnp.float32))
    middle_grad = late_grads[0].astype(jnp.bfloat16)
    early_grads = early_back(middle_grad.astype(jnp.float32))
    input_grad = early_grads[0].astype(jnp.bfloat16)
    hidden = jnp.stack([middle, late_out.astype(jnp.bfloat16)])
    input_grads = jnp.stack([input_grad, middle_grad])
    layer_grads = (early_grads, late_grads)
    collected = []
    for layer_pos in range(2):
        grads_here = layer_grads[layer_pos]
        qkv_new, row_qkv_new, col_qkv_new, ratio_qkv = factored_update(w_qkv[layer_pos], grads_here[1], row_qkv[layer_pos], col_qkv[layer_pos])
        out_new, row_out_new, col_out_new, ratio_out = factored_update(w_out[layer_pos], grads_here[2], row_out[layer_pos], col_out[layer_pos])
        up_new, row_up_new, col_up_new, ratio_up = factored_update(w_up[layer_pos], grads_here[3], row_up[layer_pos], col_up[layer_pos])
        down_new, row_down_new, col_down_new, ratio_down = factored_update(w_down[layer_pos], grads_here[4], row_down[layer_pos], col_down[layer_pos])
        attn_new, moment_attn, ratio_attn = vector_update(gain_attn[layer_pos], grads_here[5], var_attn[layer_pos])
        mlp_new, moment_mlp, ratio_mlp = vector_update(gain_mlp[layer_pos], grads_here[6], var_mlp[layer_pos])
        ratios = jnp.stack([ratio_qkv, ratio_out, ratio_up, ratio_down, ratio_attn, ratio_mlp])
        collected.append((grads_here[1], grads_here[2], grads_here[3], grads_here[4], grads_here[5], grads_here[6], qkv_new, out_new, up_new, down_new, attn_new, mlp_new, row_qkv_new, col_qkv_new, row_out_new, col_out_new, row_up_new, col_up_new, row_down_new, col_down_new, moment_attn, moment_mlp, ratios))
    stacked = [jnp.stack([collected[0][entry], collected[1][entry]]) for entry in range(23)]
    return (hidden, input_grads, stacked[0], stacked[1], stacked[2], stacked[3], stacked[4], stacked[5], stacked[6], stacked[7], stacked[8], stacked[9], stacked[10], stacked[11], stacked[12], stacked[13], stacked[14], stacked[15], stacked[16], stacked[17], stacked[18], stacked[19], stacked[20], stacked[21], stacked[22])
```

```python
import functools

import jax
import jax.numpy as jnp
from jax import lax
from jax.experimental import pallas as pl
from jax.experimental.pallas import tpu as pltpu
from jax.sharding import PartitionSpec as P

HEADS = 16


decay_rate = 0.5
clip_level = 0.5
step_rate = 1.0
norm_eps = 1e-05
weight_eps = 1e-06
mask_fill = -1e30

bf16 = jnp.bfloat16
f32 = jnp.float32
LANES = 128


def swap_core(value):
    return lax.ppermute(value, "section", [(0, 1), (1, 0)])


def swap_x(value):
    return lax.ppermute(value, "ctx", [(i, i ^ 1) for i in range(4)])


def swap_y(value):
    return lax.ppermute(value, "ctx", [(i, i ^ 2) for i in range(4)])


def dot(left, right):
    return jnp.dot(left, right, preferred_element_type=f32)


def times_transposed(left, right):
    return lax.dot_general(left, right, (((1,), (1,)), ((), ())), preferred_element_type=f32)


def rows_product(left, right):
    return lax.dot_general(left, right, (((0,), (0,)), ((), ())), preferred_element_type=f32)


def gather4(value):
    pair = jnp.concatenate([value, swap_x(value)], axis=0)
    return jnp.concatenate([pair, swap_core(pair)], axis=0)


def scatter4(partial):
    half = partial.shape[0] // 2
    rows = half // 2
    partial = partial.astype(bf16)
    mine, theirs = partial[:half], swap_core(partial[half:])
    across = (mine[rows:].astype(f32) + theirs[rows:].astype(f32)).astype(bf16)
    return mine[:rows].astype(f32) + theirs[:rows].astype(f32) + swap_x(across).astype(f32)


def norm_parts(values):
    center = values - jnp.mean(values, axis=-1, keepdims=True)
    spread = jnp.mean(center * center, axis=-1, keepdims=True)
    scale = lax.rsqrt(spread + norm_eps)
    return center * scale, scale


def norm_back(out_grad, unit, scale, gain):
    scaled = out_grad * gain
    mean_scaled = jnp.mean(scaled, axis=-1, keepdims=True)
    mean_unit = jnp.mean(scaled * unit, axis=-1, keepdims=True)
    return scale * (scaled - mean_scaled - unit * mean_unit), jnp.sum(out_grad * unit, axis=0)


def nt(left, right):
    return lax.dot_general(left, right, (((1,), (1,)), ((), ())), preferred_element_type=f32)


def attention_kernel(q_ref, k_ref, v_ref, qid_ref, kid_ref, out_ref, lse_ref, *, scale):
    queries = q_ref[...] * jnp.asarray(scale, bf16)
    keys, values_t = k_ref[...], v_ref[...].T
    same = kid_ref[...] == qid_ref[...]
    first = lax.broadcasted_iota(jnp.int32, queries.shape, 1) < queries.shape[1] // 2
    parts = []
    for head in range(2):
        own = jnp.where(first if head == 0 else ~first, queries, jnp.zeros_like(queries))
        scores = jnp.where(same, nt(keys, own), mask_fill)
        peak = jnp.max(scores, axis=0, keepdims=True)
        weights = jnp.exp(scores - peak)
        total = jnp.sum(weights, axis=0, keepdims=True)
        lse_ref[0, head : head + 1, :] = peak + jnp.log(total)
        parts.append(dot(values_t, weights.astype(bf16)) * (1.0 / total))
    width = values_t.shape[0] // 2
    stacked = jnp.concatenate([parts[0][:width], parts[1][width:]], axis=0)
    out_ref[...] = stacked.T.astype(bf16)


def attention_forward(projected, keys_values, query_ids, key_ids, scale):
    rows, seq_len = projected.shape[0], keys_values.shape[0]
    tile = min(256, rows)
    elems = 4 * rows * seq_len
    return pl.pallas_call(
        functools.partial(attention_kernel, scale=scale),
        grid=(2, rows // tile),
        in_specs=[
            pl.BlockSpec((tile, LANES), lambda p, i: (i, 3 * p)),
            pl.BlockSpec((seq_len, LANES), lambda p, i: (0, 3 * p + 1)),
            pl.BlockSpec((seq_len, LANES), lambda p, i: (0, 3 * p + 2)),
            pl.BlockSpec((1, tile), lambda p, i: (0, i)),
            pl.BlockSpec((seq_len, 1), lambda p, i: (0, 0)),
        ],
        out_specs=[
            pl.BlockSpec((tile, LANES), lambda p, i: (i, p)),
            pl.BlockSpec((1, 2, tile), lambda p, i: (p, 0, i)),
        ],
        out_shape=[
            jax.ShapeDtypeStruct((rows, 2 * LANES), bf16),
            jax.ShapeDtypeStruct((2, 2, rows), f32),
        ],
        compiler_params=pltpu.CompilerParams(vmem_limit_bytes=32 << 20),
        cost_estimate=pl.CostEstimate(
            flops=elems * 4 * 128, bytes_accessed=4 << 20, transcendentals=elems
        ),
        name="attention_forward",
    )(projected, keys_values, keys_values, query_ids, key_ids)


def attention_back_kernel(
    q_ref, k_ref, v_ref, g_ref, lse_ref, qid_ref, kid_ref, dq_ref, dk_ref, dv_ref, *, scale
):
    queries = q_ref[...] * jnp.asarray(scale, bf16)
    keys, values, grads = k_ref[...], v_ref[...], g_ref[...]
    keys_t = keys.T
    same = kid_ref[...] == qid_ref[...]
    first = lax.broadcasted_iota(jnp.int32, queries.shape, 1) < queries.shape[1] // 2

    @pl.when(pl.program_id(1) == 0)
    def _():
        dk_ref[...] = jnp.zeros_like(dk_ref)
        dv_ref[...] = jnp.zeros_like(dv_ref)

    parts = []
    for head in range(2):
        mine = first if head == 0 else ~first
        own = jnp.where(mine, queries, jnp.zeros_like(queries))
        own_grads = jnp.where(mine, grads, jnp.zeros_like(grads))
        scores = jnp.where(same, nt(keys, own), mask_fill)
        weights = jnp.exp(scores - lse_ref[0, head : head + 1, :])
        prob_grad = nt(values, own_grads)
        row_dot = jnp.sum(weights * prob_grad, axis=0, keepdims=True)
        score_grad = (weights * (prob_grad - row_dot)).astype(bf16)
        dv_ref[...] += dot(weights.astype(bf16), own_grads)
        dk_ref[...] += dot(score_grad, own)
        parts.append(dot(keys_t, score_grad))
    width = keys_t.shape[0] // 2
    stacked = jnp.concatenate([parts[0][:width], parts[1][width:]], axis=0)
    dq_ref[...] = (stacked.T * scale).astype(bf16)


def attention_backward(projected, keys_values, grads, lse, query_ids, key_ids, scale):
    rows, seq_len = projected.shape[0], keys_values.shape[0]
    tile = min(256, rows)
    elems = 4 * rows * seq_len
    return pl.pallas_call(
        functools.partial(attention_back_kernel, scale=scale),
        grid=(2, rows // tile),
        in_specs=[
            pl.BlockSpec((tile, LANES), lambda p, i: (i, 3 * p)),
            pl.BlockSpec((seq_len, LANES), lambda p, i: (0, 3 * p + 1)),
            pl.BlockSpec((seq_len, LANES), lambda p, i: (0, 3 * p + 2)),
            pl.BlockSpec((tile, LANES), lambda p, i: (i, p)),
            pl.BlockSpec((1, 2, tile), lambda p, i: (p, 0, i)),
            pl.BlockSpec((1, tile), lambda p, i: (0, i)),
            pl.BlockSpec((seq_len, 1), lambda p, i: (0, 0)),
        ],
        out_specs=[
            pl.BlockSpec((tile, LANES), lambda p, i: (i, p)),
            pl.BlockSpec((seq_len, LANES), lambda p, i: (0, p)),
            pl.BlockSpec((seq_len, LANES), lambda p, i: (0, p)),
        ],
        out_shape=[
            jax.ShapeDtypeStruct((rows, 2 * LANES), bf16),
            jax.ShapeDtypeStruct((seq_len, 2 * LANES), f32),
            jax.ShapeDtypeStruct((seq_len, 2 * LANES), f32),
        ],
        compiler_params=pltpu.CompilerParams(vmem_limit_bytes=32 << 20),
        cost_estimate=pl.CostEstimate(
            flops=elems * 10 * 128, bytes_accessed=6 << 20, transcendentals=elems
        ),
        name="attention_backward",
    )(projected, keys_values, keys_values, grads, lse, query_ids, key_ids)


def per_device(
    tokens,
    cotangent,
    segment_ids,
    w_qkv,
    w_out,
    w_up,
    w_down,
    gain_attn,
    gain_mlp,
    row_qkv,
    col_qkv,
    row_out,
    col_out,
    row_up,
    col_up,
    row_down,
    col_down,
    var_attn,
    var_mlp,
):
    core = lax.axis_index("section")
    chip = lax.axis_index("ctx")
    depth = lax.axis_index("fsdp")
    y, x = chip // 2, chip % 2
    fsdp_count = lax.axis_size("fsdp")
    assert lax.axis_size("section") == 2 and lax.axis_size("ctx") == 4
    _, block, width = tokens.shape
    half = block // 2
    rows = w_qkv.shape[1]
    hidden_width = w_up.shape[2]
    unit = hidden_width // fsdp_count // 8
    scale = (width // HEADS) ** (-0.5)
    wide = 2 * LANES
    even_out = width // fsdp_count == wide
    first_core, first_y, first_x = core == 0, y == 0, x == 0

    def flipped(when, value, axis=0):
        low, high = jnp.split(value, 2, axis)
        return jnp.where(when, jnp.concatenate([high, low], axis), value)

    def eighth(e, of_core):
        qkv = lax.dynamic_index_in_dim(w_qkv[0].reshape(rows, 3, 8, LANES), e, 2, keepdims=False)
        up = lax.dynamic_index_in_dim(
            w_up[0].reshape(rows, fsdp_count, 8, unit), e, 2, keepdims=False
        )
        down = lax.dynamic_slice_in_dim(w_down[0], e * unit, unit, 0)
        parts = [qkv.reshape(rows, 3 * LANES), up.reshape(rows, fsdp_count * unit), down]
        if even_out:
            parts.append(
                lax.dynamic_slice(w_out[0], (of_core * LANES, chip * wide), (LANES, wide))
            )
        return [part.astype(bf16) for part in parts]

    mine_parts = eighth(2 * chip + core, core)
    other_parts = [swap_core(part) for part in eighth(2 * chip + 1 - core, 1 - core)]
    layer_parts = [
        [jnp.where(first_core, a, b) for a, b in zip(mine_parts, other_parts)],
        [jnp.where(first_core, b, a) for a, b in zip(mine_parts, other_parts)],
    ]
    if not even_out:
        whole_out = lax.all_gather(w_out[0].astype(bf16), "fsdp", axis=0, tiled=True)
        other_out = swap_core(whole_out)
        outs = (
            jnp.where(first_core, whole_out, other_out),
            jnp.where(first_core, other_out, whole_out),
        )

    gains_own = lax.all_gather(
        jnp.concatenate([gain_attn, gain_mlp], axis=0).astype(bf16), "fsdp", axis=1, tiled=True
    )
    gains_other = swap_core(gains_own)
    gains = (
        jnp.where(first_core, gains_own, gains_other).astype(f32),
        jnp.where(first_core, gains_other, gains_own).astype(f32),
    )

    def gather_rows(value):
        return lax.all_gather(value, "fsdp", axis=0, tiled=True)

    def layer_weights(layer):
        parts = layer_parts[layer]
        qkv = gather_rows(parts[0])
        qkv = jnp.concatenate([qkv, swap_y(qkv)], axis=1)
        if even_out:
            cols = gather_rows(parts[3]).reshape(fsdp_count, LANES, wide)

            def pick(index):
                return lax.dynamic_index_in_dim(cols, index, 0, keepdims=False)

            keep = jnp.stack([pick(chip), pick(chip ^ 2)])
            give = jnp.stack([pick(chip ^ 1), pick(chip ^ 3)])
            pair = jnp.concatenate([keep, swap_x(give)], axis=2)
            pair = flipped(~first_x, pair, 2)
            far = swap_y(pair[::-1])
            out = flipped(~first_y, jnp.concatenate([pair, far], axis=2), 2).reshape(wide, width)
        else:
            blocks = outs[layer].reshape(4, 2, LANES, width)
            blocks = lax.dynamic_index_in_dim(blocks, core, 1, keepdims=False)
            out = jnp.concatenate(
                [
                    lax.dynamic_index_in_dim(blocks, chip, 0, keepdims=False),
                    lax.dynamic_index_in_dim(blocks, chip ^ 2, 0, keepdims=False),
                ],
                axis=0,
            )
        up = gather_rows(parts[1])
        up = jnp.concatenate([up, swap_y(up)], axis=1)
        down = gather_rows(parts[2])
        down = jnp.concatenate([down, swap_y(down)], axis=0)
        return qkv, out, up, down

    weights = [layer_weights(0), layer_weights(1)]

    def own_rows(value):
        near = lax.dynamic_slice(value, (y, core * half, 0), (1, half, width))[0]
        away = lax.dynamic_slice(value, (1 - y, core * half, 0), (1, half, width))[0]
        return [near, swap_y(away)]

    ids = lax.dynamic_index_in_dim(segment_ids, y, 0, keepdims=False).reshape(2, 2, 2, half)
    ids = flipped(~first_y, flipped(~first_x, flipped(~first_core, ids, 2), 1), 0)
    ids = ids.transpose(0, 2, 1, 3)
    key_ids = ids.reshape(8 * half, 1)
    query_ids = [ids[k].reshape(1, 4 * half) for k in range(2)]

    def forward(inputs, layer):
        qkv_w, out_w, up_w, down_w = weights[layer]
        attn_gain, mlp_gain = gains[layer][0], gains[layer][1]
        inputs_all = [gather4(value) for value in inputs]
        projected = [dot(value, qkv_w).astype(bf16) for value in inputs_all]
        keys_values = jnp.concatenate(projected, axis=0)
        kept, outputs = [], []
        for k in range(2):
            context, lse = attention_forward(
                projected[k], keys_values, query_ids[k], key_ids, scale
            )
            pre_attn = inputs[k].astype(f32) + scatter4(dot(context, out_w))
            unit_attn, scale_attn = norm_parts(pre_attn)
            normed = unit_attn * attn_gain
            normed_all = gather4(normed.astype(bf16))
            upward = dot(normed_all, up_w)
            phi_whole = 0.5 * (1.0 + lax.erf(upward * (0.5**0.5)))
            activated = (upward * phi_whole).astype(bf16)
            density = jnp.exp(-0.5 * upward * upward) * 0.3989422804014327
            slope = (phi_whole + upward * density).astype(bf16)
            pre_mlp = normed + scatter4(dot(activated, down_w))
            unit_mlp, scale_mlp = norm_parts(pre_mlp)
            outputs.append((unit_mlp * mlp_gain).astype(bf16))
            kept.append(
                (context, lse, unit_attn, scale_attn, normed_all, activated, slope, unit_mlp, scale_mlp)
            )
        return outputs, (inputs_all, projected, keys_values, kept)

    def backward(out_grads, saved, layer):
        qkv_w, out_w, up_w, down_w = weights[layer]
        attn_gain, mlp_gain = gains[layer][0], gains[layer][1]
        inputs_all, projected, keys_values, kept = saved
        attn_gain_grad, mlp_gain_grad, attn_in, query_grads = 0.0, 0.0, [], []
        key_grad, value_grad = 0.0, 0.0
        grad_out, grad_up, grad_down = 0.0, 0.0, 0.0
        for k in range(2):
            context, lse, unit_attn, scale_attn, normed_all, activated, slope, unit_mlp, scale_mlp = kept[k]
            mlp_in, gain_part = norm_back(out_grads[k].astype(f32), unit_mlp, scale_mlp, mlp_gain)
            mlp_gain_grad += gain_part
            down_all = gather4(mlp_in.astype(bf16))
            upward_grad = (times_transposed(down_all, down_w) * slope.astype(f32)).astype(bf16)
            normed_grad = mlp_in + scatter4(times_transposed(upward_grad, up_w))
            attn_grad, gain_part = norm_back(normed_grad, unit_attn, scale_attn, attn_gain)
            attn_gain_grad += gain_part
            attn_in.append(attn_grad)
            branch_all = gather4(attn_grad.astype(bf16))
            context_grad = times_transposed(branch_all, out_w).astype(bf16)
            dq, dk, dv = attention_backward(
                projected[k], keys_values, context_grad, lse, query_ids[k], key_ids, scale
            )
            query_grads.append(dq)
            key_grad += dk
            value_grad += dv
            grad_down += rows_product(activated, down_all)
            grad_up += rows_product(normed_all, upward_grad)
            grad_out += rows_product(context, branch_all)
        key_grad, value_grad = key_grad.astype(bf16), value_grad.astype(bf16)
        in_grads, grad_qkv = [], 0.0
        for k in range(2):
            part = slice(4 * half * k, 4 * half * (k + 1))
            stacked = jnp.concatenate(
                [
                    piece[:, LANES * p : LANES * (p + 1)]
                    for p in range(2)
                    for piece in (query_grads[k], key_grad[part], value_grad[part])
                ],
                axis=1,
            )
            in_grads.append(
                (attn_in[k] + scatter4(times_transposed(stacked, qkv_w))).astype(bf16)
            )
            grad_qkv += rows_product(inputs_all[k], stacked)
        whole = tuple(g.astype(bf16) for g in (grad_qkv, grad_out, grad_up, grad_down))
        return in_grads, whole, jnp.stack([attn_gain_grad, mlp_gain_grad])

    def fold_y(keep, give):
        return (keep.astype(f32) + swap_y(give).astype(f32)).astype(bf16)

    def scatter_rows(value):
        return lax.psum_scatter(value, "fsdp", scatter_dimension=0, tiled=True)

    def spread(value, y_first):
        if y_first:
            pair = jnp.stack([value, swap_y(value)])
            far = swap_x(pair)
            return jnp.stack([pair[0], far[0], pair[1], far[1]])
        pair = jnp.stack([value, swap_x(value)])
        return jnp.concatenate([pair, swap_y(pair)], axis=0)

    def reduce_gradients(whole):
        grad_qkv, grad_out, grad_up, grad_down = whole
        wide_qkv = grad_qkv.shape[1] // 2
        down = scatter_rows(fold_y(grad_down[: fsdp_count * unit], grad_down[fsdp_count * unit :]))
        up = scatter_rows(fold_y(grad_up[:, : fsdp_count * unit], grad_up[:, fsdp_count * unit :]))
        if even_out:
            blocks = grad_out.reshape(2, LANES, width)
            near_cols = flipped(~first_y, blocks, 2)
            pair = fold_y(near_cols[:, :, : width // 2], near_cols[::-1, :, width // 2 :])
            pair = flipped(~first_x, pair, 2)
            cross = swap_x(pair[:, :, wide:])
            keep = pair[:, :, :wide]
            four = jnp.stack([keep[0], keep[1], cross[0], cross[1]])
            order = jnp.stack([chip, chip ^ 2, chip ^ 1, chip ^ 3])
            placed = jnp.where(
                (order[None, :] == jnp.arange(4)[:, None])[:, :, None, None], four[None], 0
            ).sum(axis=1, dtype=bf16)
            out = scatter_rows(placed.reshape(4 * LANES, wide))
        else:
            blocks = grad_out.reshape(2, LANES, width)
            place = jnp.zeros((4, 2, LANES, width), bf16)
            place = lax.dynamic_update_slice(place, blocks[:1, None], (chip, core, 0, 0))
            place = lax.dynamic_update_slice(place, blocks[1:, None], (chip ^ 2, core, 0, 0))
            out = scatter_rows(lax.psum(place.reshape(width, width), ("section", "ctx")))
        qkv = scatter_rows(fold_y(grad_qkv[:, :wide_qkv], grad_qkv[:, wide_qkv:]))
        spread_out = spread(out, True) if even_out else out
        return [spread(qkv, False), spread_out, spread(up, False), spread(down, True)]

    inputs = own_rows(tokens)
    out_grads = own_rows(cotangent)
    hidden0, saved0 = forward(inputs, 0)
    hidden1, saved1 = forward(hidden0, 1)
    in_grads1, whole1, gain_grads1 = backward(out_grads, saved1, 1)
    pieces1 = reduce_gradients(whole1)
    in_grads0, whole0, gain_grads0 = backward(in_grads1, saved0, 0)
    pieces0 = reduce_gradients(whole0)

    def to_owner(layer0, layer1):
        pairs = [jnp.stack([runs[0], swap_y(runs[1])]) for runs in (layer0, layer1)]
        keep = jnp.where(first_core, pairs[0], pairs[1])
        take = swap_core(jnp.where(first_core, pairs[1], pairs[0]))
        both = flipped(~first_core, jnp.stack([keep, take], axis=1), 1)
        return flipped(~first_y, both, 0).reshape(2, block, width)

    hidden_out = to_owner(hidden0, hidden1)
    in_grads_out = to_owner(in_grads0, in_grads1)

    def own_layer(piece0, piece1):
        keep = jnp.where(first_core, piece0, piece1)
        take = swap_core(jnp.where(first_core, piece1, piece0))
        both = jnp.stack([keep, take], axis=1)
        shape = both.shape
        both = both.reshape((2, 2, 2) + shape[2:])
        both = flipped(~first_y, flipped(~first_x, flipped(~first_core, both, 2), 1), 0)
        return both.reshape((8,) + shape[2:])

    natural = own_layer(pieces0[0], pieces1[0]).reshape(8, rows, 3, LANES)
    shard_qkv = natural.transpose(1, 2, 0, 3).reshape(rows, 3 * width).astype(f32)
    if even_out:
        natural = own_layer(pieces0[1], pieces1[1]).reshape(4, 2, LANES, wide)
        shard_out = natural.transpose(1, 2, 0, 3).reshape(2 * LANES, width).astype(f32)
    else:
        shard_out = jnp.where(first_core, pieces0[1], pieces1[1]).astype(f32)
    natural = own_layer(pieces0[2], pieces1[2]).reshape(8, rows, fsdp_count, unit)
    shard_up = natural.transpose(1, 2, 0, 3).reshape(rows, hidden_width).astype(f32)
    shard_down = own_layer(pieces0[3], pieces1[3]).reshape(8 * unit, width).astype(f32)

    gain_all = lax.psum(jnp.stack([gain_grads0, gain_grads1]), ("section", "ctx", "fsdp"))
    gain_own = jnp.where(first_core, gain_all[0], gain_all[1])
    gain_shard = lax.dynamic_slice(gain_own, (0, depth * rows), (2, rows))
    shard_attn, shard_mlp = gain_shard[0], gain_shard[1]
    masters = (w_qkv[0], w_out[0], w_up[0], w_down[0])
    gradients = (shard_qkv, shard_out, shard_up, shard_down)
    rows_old = (row_qkv[0], row_out[0], row_up[0], row_down[0])
    cols_old = (col_qkv[0], col_out[0], col_up[0], col_down[0])
    squares = [gradient * gradient for gradient in gradients]
    rows_new = [
        decay_rate * old_row + (1.0 - decay_rate) * jnp.mean(square, axis=1)
        for old_row, square in zip(rows_old, squares)
    ]
    row_counts = [gradient.shape[0] * fsdp_count for gradient in gradients]
    col_partial = [jnp.sum(square, axis=0) for square in squares]
    row_totals = jnp.stack([jnp.sum(row_value) for row_value in rows_new])
    weight_totals = jnp.stack(
        [jnp.sum(master * master) for master in masters]
        + [jnp.sum(gain_attn[0] * gain_attn[0]), jnp.sum(gain_mlp[0] * gain_mlp[0])]
    )
    moment_attn = decay_rate * var_attn[0] + (1.0 - decay_rate) * shard_attn * shard_attn
    moment_mlp = decay_rate * var_mlp[0] + (1.0 - decay_rate) * shard_mlp * shard_mlp
    gain_updates = (shard_attn * lax.rsqrt(moment_attn), shard_mlp * lax.rsqrt(moment_mlp))
    vector_totals = jnp.stack([jnp.sum(gain_step * gain_step) for gain_step in gain_updates])
    totals = lax.psum(
        jnp.concatenate(col_partial + [row_totals, weight_totals, vector_totals]), "fsdp"
    )
    col_sums, start = [], 0
    for partial in col_partial:
        col_sums.append(totals[start : start + partial.shape[0]])
        start += partial.shape[0]
    row_all, weight_all, vector_all = (
        totals[start : start + 4],
        totals[start + 4 : start + 10],
        totals[start + 10 :],
    )
    cols_new = [
        decay_rate * cols_old[matrix_pos]
        + (1.0 - decay_rate) * col_sums[matrix_pos] / row_counts[matrix_pos]
        for matrix_pos in range(4)
    ]
    updates = [
        gradients[matrix_pos]
        * lax.rsqrt(
            rows_new[matrix_pos][:, None]
            * cols_new[matrix_pos][None, :]
            / (row_all[matrix_pos] / row_counts[matrix_pos])
        )
        for matrix_pos in range(4)
    ]
    update_all = lax.psum(jnp.stack([jnp.sum(update * update) for update in updates]), "fsdp")
    fresh_masters = []
    ratios = []
    for matrix_pos in range(4):
        entry_count = row_counts[matrix_pos] * gradients[matrix_pos].shape[1]
        clip_ratio = jnp.sqrt(update_all[matrix_pos] / entry_count)
        weight_scale = jnp.sqrt(weight_all[matrix_pos] / entry_count + weight_eps)
        fresh_masters.append(
            masters[matrix_pos]
            - step_rate
            * weight_scale
            * updates[matrix_pos]
            / jnp.maximum(1.0, clip_ratio / clip_level)
        )
        ratios.append(clip_ratio)
    gain_masters = (gain_attn[0], gain_mlp[0])
    gain_count = shard_attn.shape[0] * fsdp_count
    for gain_pos in range(2):
        clip_ratio = jnp.sqrt(vector_all[gain_pos] / gain_count)
        weight_scale = jnp.sqrt(weight_all[4 + gain_pos] / gain_count + weight_eps)
        fresh_masters.append(
            gain_masters[gain_pos]
            - step_rate
            * weight_scale
            * gain_updates[gain_pos]
            / jnp.maximum(1.0, clip_ratio / clip_level)
        )
        ratios.append(clip_ratio)
    return (
        hidden_out[None],
        in_grads_out[None],
        shard_qkv[None],
        shard_out[None],
        shard_up[None],
        shard_down[None],
        shard_attn[None],
        shard_mlp[None],
        fresh_masters[0][None],
        fresh_masters[1][None],
        fresh_masters[2][None],
        fresh_masters[3][None],
        fresh_masters[4][None],
        fresh_masters[5][None],
        rows_new[0][None],
        cols_new[0][None],
        rows_new[1][None],
        cols_new[1][None],
        rows_new[2][None],
        cols_new[2][None],
        rows_new[3][None],
        cols_new[3][None],
        moment_attn[None],
        moment_mlp[None],
        jnp.stack(ratios)[None],
    )


def solution(mesh):
    in_specs = (
        P("fsdp", "ctx", None),
        P("fsdp", "ctx", None),
        P("fsdp", None),
        P("section", "fsdp", None),
        P("section", "fsdp", None),
        P("section", "fsdp", None),
        P("section", "fsdp", None),
        P("section", "fsdp"),
        P("section", "fsdp"),
        P("section", "fsdp"),
        P("section", None),
        P("section", "fsdp"),
        P("section", None),
        P("section", "fsdp"),
        P("section", None),
        P("section", "fsdp"),
        P("section", None),
        P("section", "fsdp"),
        P("section", "fsdp"),
    )
    out_specs = (
        P("section", "fsdp", "ctx", None),
        P("section", "fsdp", "ctx", None),
        P("section", "fsdp", None),
        P("section", "fsdp", None),
        P("section", "fsdp", None),
        P("section", "fsdp", None),
        P("section", "fsdp"),
        P("section", "fsdp"),
        P("section", "fsdp", None),
        P("section", "fsdp", None),
        P("section", "fsdp", None),
        P("section", "fsdp", None),
        P("section", "fsdp"),
        P("section", "fsdp"),
        P("section", "fsdp"),
        P("section", None),
        P("section", "fsdp"),
        P("section", None),
        P("section", "fsdp"),
        P("section", None),
        P("section", "fsdp"),
        P("section", None),
        P("section", "fsdp"),
        P("section", "fsdp"),
        P("section", None),
    )
    return jax.shard_map(
        per_device, mesh=mesh, in_specs=in_specs, out_specs=out_specs, check_vma=False
    )
```

```python
import functools

import jax
import jax.numpy as jnp
from jax import lax
from jax.experimental import pallas as pl
from jax.experimental.pallas import tpu as pltpu
from jax.sharding import PartitionSpec as P

HEADS = 16


decay_rate = 0.5
clip_level = 0.5
step_rate = 1.0
norm_eps = 1e-05
weight_eps = 1e-06
mask_fill = -1e30

bf16 = jnp.bfloat16
f32 = jnp.float32
LANES = 128


def swap_core(value):
    return lax.ppermute(value, "section", [(0, 1), (1, 0)])


def swap_x(value):
    return lax.ppermute(value, "ctx", [(i, i ^ 1) for i in range(4)])


def swap_y(value):
    return lax.ppermute(value, "ctx", [(i, i ^ 2) for i in range(4)])


def dot(left, right):
    return jnp.dot(left, right, preferred_element_type=f32)


def times_transposed(left, right):
    return lax.dot_general(left, right, (((1,), (1,)), ((), ())), preferred_element_type=f32)


def rows_product(left, right):
    return lax.dot_general(left, right, (((0,), (0,)), ((), ())), preferred_element_type=f32)


def after(value, *tokens):
    return lax.optimization_barrier((value, *tokens))[0]


def gather4(value):
    pair = jnp.concatenate([value, swap_x(value)], axis=0)
    return jnp.concatenate([pair, swap_core(pair)], axis=0)


def fold_core(partial):
    half = partial.shape[0] // 2
    rows = half // 2
    partial = partial.astype(bf16)
    mine, theirs = partial[:half], swap_core(partial[half:])
    keep = mine[:rows].astype(f32) + theirs[:rows].astype(f32)
    return keep, (mine[rows:].astype(f32) + theirs[rows:].astype(f32)).astype(bf16)


def norm_parts(values):
    center = values - jnp.mean(values, axis=-1, keepdims=True)
    spread = jnp.mean(center * center, axis=-1, keepdims=True)
    scale = lax.rsqrt(spread + norm_eps)
    return center * scale, scale


def norm_back(out_grad, unit, scale, gain):
    scaled = out_grad * gain
    mean_scaled = jnp.mean(scaled, axis=-1, keepdims=True)
    mean_unit = jnp.mean(scaled * unit, axis=-1, keepdims=True)
    return scale * (scaled - mean_scaled - unit * mean_unit), jnp.sum(out_grad * unit, axis=0)


def nt(left, right):
    return lax.dot_general(left, right, (((1,), (1,)), ((), ())), preferred_element_type=f32)


def attention_kernel(q_ref, k_ref, v_ref, qid_ref, kid_ref, out_ref, lse_ref, *, scale):
    queries = q_ref[...] * jnp.asarray(scale, bf16)
    keys, values_t = k_ref[...], v_ref[...].T
    same = kid_ref[...] == qid_ref[...]
    first = lax.broadcasted_iota(jnp.int32, queries.shape, 1) < queries.shape[1] // 2
    parts = []
    for head in range(2):
        own = jnp.where(first if head == 0 else ~first, queries, jnp.zeros_like(queries))
        scores = jnp.where(same, nt(keys, own), mask_fill)
        peak = jnp.max(scores, axis=0, keepdims=True)
        weights = jnp.exp(scores - peak)
        total = jnp.sum(weights, axis=0, keepdims=True)
        lse_ref[0, head : head + 1, :] = peak + jnp.log(total)
        parts.append(dot(values_t, weights.astype(bf16)) * (1.0 / total))
    width = values_t.shape[0] // 2
    stacked = jnp.concatenate([parts[0][:width], parts[1][width:]], axis=0)
    out_ref[...] = stacked.T.astype(bf16)


def attention_forward(projected, keys_values, query_ids, key_ids, scale):
    rows, seq_len = projected.shape[0], keys_values.shape[0]
    tile = min(256, rows)
    elems = 4 * rows * seq_len
    return pl.pallas_call(
        functools.partial(attention_kernel, scale=scale),
        grid=(2, rows // tile),
        in_specs=[
            pl.BlockSpec((tile, LANES), lambda p, i: (i, 3 * p)),
            pl.BlockSpec((seq_len, LANES), lambda p, i: (0, 3 * p + 1)),
            pl.BlockSpec((seq_len, LANES), lambda p, i: (0, 3 * p + 2)),
            pl.BlockSpec((1, tile), lambda p, i: (0, i)),
            pl.BlockSpec((seq_len, 1), lambda p, i: (0, 0)),
        ],
        out_specs=[
            pl.BlockSpec((tile, LANES), lambda p, i: (i, p)),
            pl.BlockSpec((1, 2, tile), lambda p, i: (p, 0, i)),
        ],
        out_shape=[
            jax.ShapeDtypeStruct((rows, 2 * LANES), bf16),
            jax.ShapeDtypeStruct((2, 2, rows), f32),
        ],
        compiler_params=pltpu.CompilerParams(vmem_limit_bytes=32 << 20),
        cost_estimate=pl.CostEstimate(
            flops=elems * 4 * 128, bytes_accessed=4 << 20, transcendentals=elems
        ),
        name="attention_forward",
    )(projected, keys_values, keys_values, query_ids, key_ids)


def attention_back_kernel(
    q_ref, k_ref, v_ref, g_ref, lse_ref, qid_ref, kid_ref, dq_ref, dk_ref, dv_ref, *, scale
):
    queries = q_ref[...] * jnp.asarray(scale, bf16)
    keys, values, grads = k_ref[...], v_ref[...], g_ref[...]
    keys_t = keys.T
    same = kid_ref[...] == qid_ref[...]
    first = lax.broadcasted_iota(jnp.int32, queries.shape, 1) < queries.shape[1] // 2

    @pl.when(pl.program_id(1) == 0)
    def _():
        dk_ref[...] = jnp.zeros_like(dk_ref)
        dv_ref[...] = jnp.zeros_like(dv_ref)

    parts = []
    for head in range(2):
        mine = first if head == 0 else ~first
        own = jnp.where(mine, queries, jnp.zeros_like(queries))
        own_grads = jnp.where(mine, grads, jnp.zeros_like(grads))
        scores = jnp.where(same, nt(keys, own), mask_fill)
        weights = jnp.exp(scores - lse_ref[0, head : head + 1, :])
        prob_grad = nt(values, own_grads)
        row_dot = jnp.sum(weights * prob_grad, axis=0, keepdims=True)
        score_grad = (weights * (prob_grad - row_dot)).astype(bf16)
        dv_ref[...] += dot(weights.astype(bf16), own_grads)
        dk_ref[...] += dot(score_grad, own)
        parts.append(dot(keys_t, score_grad))
    width = keys_t.shape[0] // 2
    stacked = jnp.concatenate([parts[0][:width], parts[1][width:]], axis=0)
    dq_ref[...] = (stacked.T * scale).astype(bf16)


def attention_backward(projected, keys_values, grads, lse, query_ids, key_ids, scale):
    rows, seq_len = projected.shape[0], keys_values.shape[0]
    tile = min(256, rows)
    elems = 4 * rows * seq_len
    return pl.pallas_call(
        functools.partial(attention_back_kernel, scale=scale),
        grid=(2, rows // tile),
        in_specs=[
            pl.BlockSpec((tile, LANES), lambda p, i: (i, 3 * p)),
            pl.BlockSpec((seq_len, LANES), lambda p, i: (0, 3 * p + 1)),
            pl.BlockSpec((seq_len, LANES), lambda p, i: (0, 3 * p + 2)),
            pl.BlockSpec((tile, LANES), lambda p, i: (i, p)),
            pl.BlockSpec((1, 2, tile), lambda p, i: (p, 0, i)),
            pl.BlockSpec((1, tile), lambda p, i: (0, i)),
            pl.BlockSpec((seq_len, 1), lambda p, i: (0, 0)),
        ],
        out_specs=[
            pl.BlockSpec((tile, LANES), lambda p, i: (i, p)),
            pl.BlockSpec((seq_len, LANES), lambda p, i: (0, p)),
            pl.BlockSpec((seq_len, LANES), lambda p, i: (0, p)),
        ],
        out_shape=[
            jax.ShapeDtypeStruct((rows, 2 * LANES), bf16),
            jax.ShapeDtypeStruct((seq_len, 2 * LANES), f32),
            jax.ShapeDtypeStruct((seq_len, 2 * LANES), f32),
        ],
        compiler_params=pltpu.CompilerParams(vmem_limit_bytes=32 << 20),
        cost_estimate=pl.CostEstimate(
            flops=elems * 10 * 128, bytes_accessed=6 << 20, transcendentals=elems
        ),
        name="attention_backward",
    )(projected, keys_values, keys_values, grads, lse, query_ids, key_ids)


def whole(shape):
    return pl.BlockSpec(shape, lambda *_: (0,) * len(shape))


def cut_kernel(_, *refs, width):
    first, up, down = refs[:16], refs[16:24], refs[24:26]
    packed, far, ups, downs = refs[26:28], refs[28:30], refs[30:32], refs[32:34]
    rows = first[0].shape[1]
    for core in range(2):
        for i in range(3):
            lanes = slice(LANES * i, LANES * (i + 1))
            packed[core][:rows, lanes] = first[3 * core + i][0].astype(bf16)
            far[core][:, lanes] = first[6 + 3 * core + i][0].astype(bf16)
        out = first[12 + core][0].astype(bf16)
        packed[core][:LANES, 3 * LANES :] = out[:, :LANES]
        packed[core][LANES:rows, 3 * LANES :] = out[:, LANES:]
        gains = jnp.concatenate([first[14][...], first[15][...]], axis=1)
        top = lax.broadcasted_iota(jnp.int32, (16, 2 * rows), 0) == 0
        gains = jnp.where(top, jnp.broadcast_to(gains, (16, 2 * rows)), 0.0)
        packed[core][rows:, :] = gains.astype(bf16)
        for i in range(4):
            ups[core][:, LANES * i : LANES * (i + 1)] = up[4 * core + i][0].astype(bf16)
        downs[core][...] = down[core][0].astype(bf16)


def cut_weights(w_qkv, w_out, w_up, w_down, gain_attn, gain_mlp, at_eighth):
    rows, width = w_qkv.shape[1], w_out.shape[2]

    def column(i, flip):
        return pl.BlockSpec((1, rows, LANES), lambda g, at: (0, 0, 8 * i + (at[0] ^ flip)))

    specs = [column(i, flip) for flip in (0, 1, 4, 5) for i in range(3)]
    specs += [
        pl.BlockSpec(
            (1, LANES, 2 * LANES), lambda g, at, c=core: (0, (at[0] & 1) ^ c, at[0] >> 1)
        )
        for core in range(2)
    ]
    specs += [whole(gain_attn.shape), whole(gain_mlp.shape)]
    specs += [column(i, core) for core in range(2) for i in range(4)]
    specs += [
        pl.BlockSpec((1, LANES, width), lambda g, at, c=core: (0, at[0] ^ c, 0))
        for core in range(2)
    ]
    outs = [
        jax.ShapeDtypeStruct(shape, bf16)
        for shape in (
            (rows + 16, 4 * LANES),
            (rows, 3 * LANES),
            (rows, 4 * LANES),
            (LANES, width),
        )
        for _ in range(2)
    ]
    operands = [w_qkv] * 12 + [w_out] * 2 + [gain_attn, gain_mlp] + [w_up] * 8 + [w_down] * 2
    return pl.pallas_call(
        functools.partial(cut_kernel, width=width),
        grid_spec=pltpu.PrefetchScalarGridSpec(
            num_scalar_prefetch=1,
            grid=(1,),
            in_specs=specs,
            out_specs=[whole(out.shape) for out in outs],
        ),
        out_shape=outs,
        compiler_params=pltpu.CompilerParams(vmem_limit_bytes=56 << 20),
        name="cut_weights",
    )(at_eighth, *operands)


def place_kernel(at, *refs, fixed):
    qkv_ref, out_ref, gain_ref = refs[-3:]
    count = (len(refs) - 3) // 2
    rows, cols = refs[count].shape
    for k in range(count):
        slot = k if fixed else lax.rem(at[0] + count - k, count)
        packed, far = refs[k], refs[count + k]
        part = pl.ds(pl.multiple_of(slot * rows, rows), rows)
        qkv_ref[part, :cols] = packed[:rows, :cols]
        qkv_ref[part, cols:] = far[...]
        away = slot ^ at[1]
        away = 2 * (away & 1) + (away >> 1)
        out_ref[away, :, :LANES] = packed[:LANES, cols:]
        out_ref[away, :, LANES:] = packed[LANES:rows, cols:]
        part = pl.ds(pl.multiple_of(slot * rows, rows), rows)
        gains = packed[rows:, :].astype(f32)
        gain_ref[0:1, part] = gains[0:1, :rows]
        gain_ref[1:2, part] = gains[0:1, rows:]


def place(packed, far, depth, fixed):
    count = 4
    rows, cols = far[0].shape
    if fixed:
        rows = rows // count
    shapes = ((rows + 16, cols + LANES), (rows, cols))
    specs = [
        pl.BlockSpec(shape, (lambda g, at, k=k: (k, 0)) if fixed else (lambda g, at: (0, 0)))
        for shape in shapes
        for k in range(count)
    ]
    outs = [
        jax.ShapeDtypeStruct((rows * count, 2 * cols), bf16),
        jax.ShapeDtypeStruct((count, LANES, 2 * LANES), bf16),
        jax.ShapeDtypeStruct((2, rows * count), f32),
    ]
    return pl.pallas_call(
        functools.partial(place_kernel, fixed=fixed),
        grid_spec=pltpu.PrefetchScalarGridSpec(
            num_scalar_prefetch=1,
            grid=(1,),
            in_specs=specs,
            out_specs=[whole(out.shape) for out in outs],
        ),
        out_shape=outs,
        compiler_params=pltpu.CompilerParams(vmem_limit_bytes=24 << 20),
        name="place_rows",
    )(depth, *(list(packed) * (count if fixed else 1)), *(list(far) * (count if fixed else 1)))


def small_call(kernel, at, operands, outs, name):
    return pl.pallas_call(
        kernel,
        grid_spec=pltpu.PrefetchScalarGridSpec(
            num_scalar_prefetch=1,
            grid=(1,),
            in_specs=[whole(value.shape) for value in operands],
            out_specs=[whole(out.shape) for out in outs],
        ),
        out_shape=outs,
        compiler_params=pltpu.CompilerParams(vmem_limit_bytes=40 << 20),
        name=name,
    )(at, *operands)


def join_out_kernel(at, keep, came, far_keep, far_came, out_ref):
    for b in range(2):
        rows = slice(LANES * b, LANES * (b + 1))
        for away, value in enumerate((keep[b], came[b], far_keep[1 - b], far_came[1 - b])):
            size = value.shape[1]
            start = pl.multiple_of((at[0] ^ away) * size, size)
            out_ref[rows, pl.ds(start, size)] = value


def fold_out_kernel(at, keep, came, near_ref, give_ref):
    size = near_ref.shape[2]
    first_x = (at[0] & 1) == 0
    for b in range(2):
        value = keep[b].astype(f32) + came[1 - b].astype(f32)
        low, high = value[:, :size], value[:, size:]
        near_ref[b] = jnp.where(first_x, low, high).astype(bf16)
        give_ref[b] = jnp.where(first_x, high, low).astype(bf16)


def pack_kernel(at, keep, came, near, cross, gains, out_ref):
    cols = keep.shape[1]
    rows = keep.shape[0] // 4
    top = lax.broadcasted_iota(jnp.int32, (16, 2 * rows), 0) == 0
    for f in range(4):
        base = f * (rows + 16)
        part = slice(rows * f, rows * (f + 1))
        out_ref[base : base + rows, :cols] = (
            keep[part, :].astype(f32) + came[part, :].astype(f32)
        ).astype(bf16)
        gain = jnp.concatenate([gains[0:1, part], gains[1:2, part]], axis=1)
        gain = jnp.where(top, jnp.broadcast_to(gain, (16, 2 * rows)), 0.0)
        out_ref[base + rows : base + rows + 16, :] = gain.astype(bf16)
    for away, value in enumerate((near[0], cross[0], near[1], cross[1])):
        base = (at[0] ^ away) * (rows + 16)
        for half in range(2):
            start = pl.multiple_of(base + LANES * half, 16)
            out_ref[pl.ds(start, LANES), cols:] = value[:, LANES * half : LANES * (half + 1)]


def assemble_kernel(at, *refs, kind, shapes):
    groups = [refs[4 * i : 4 * i + 4] for i in range(4)]
    rows_old = refs[16 : 16 + len(shapes)]
    outs = refs[16 + len(shapes) :]
    grads, rows_new, sums_ref = outs[: len(shapes)], outs[len(shapes) : 2 * len(shapes)], outs[-1]
    first_core = at[1] == 0
    gain = 0.0
    for core in range(2):
        for chip in range(4):
            eighth = (2 * chip + core) ^ at[0]
            value = jnp.where(first_core, groups[core][chip][...], groups[2 + core][chip][...])
            value = value.astype(f32)
            if kind == "rows":
                rows = value.shape[0]
                grads[0][pl.ds(pl.multiple_of(eighth * rows, rows), rows), :] = value
            elif kind == "columns":
                for i in range(value.shape[1] // LANES):
                    start = pl.multiple_of((8 * i + eighth) * LANES, LANES)
                    grads[0][:, pl.ds(start, LANES)] = value[:, LANES * i : LANES * (i + 1)]
            else:
                rows = shapes[0][0]
                for i in range(3):
                    start = pl.multiple_of((8 * i + eighth) * LANES, LANES)
                    grads[0][:, pl.ds(start, LANES)] = value[:rows, LANES * i : LANES * (i + 1)]
                part = pl.ds(pl.multiple_of((eighth & 1) * LANES, LANES), LANES)
                for half in range(2):
                    start = pl.multiple_of((2 * (eighth >> 1) + half) * LANES, LANES)
                    block = value[half * LANES : (half + 1) * LANES, 3 * LANES :]
                    grads[1][part, pl.ds(start, LANES)] = block
                gain = gain + value[rows : rows + 1, :]
    if kind == "packed":
        outs[-2][...] = gain
    sums_ref[...] = jnp.zeros_like(sums_ref)
    lane = lax.broadcasted_iota(jnp.int32, (1, LANES), 1)
    begin = LANES
    for index, (total_rows, cols) in enumerate(shapes):
        grad_ref, row_ref, new_ref = grads[index], rows_old[index], rows_new[index]
        col_part = slice(begin, begin + cols)
        ratio_part = slice(begin + cols, begin + 2 * cols)
        begin += 2 * cols

        def body(i, total):
            part = pl.ds(pl.multiple_of(i * 64, 64), 64)
            values = grad_ref[part, :]
            square = values * values
            row_new = decay_rate * row_ref[part, :] + (1.0 - decay_rate) * (
                jnp.sum(square, axis=1, keepdims=True) / cols
            )
            new_ref[part, :] = row_new
            sums_ref[:, col_part] += jnp.sum(square, axis=0, keepdims=True)
            sums_ref[:, ratio_part] += jnp.sum(square * (1.0 / row_new), axis=0, keepdims=True)
            return total + jnp.sum(row_new, axis=0, keepdims=True)

        total = lax.fori_loop(0, total_rows // 64, body, jnp.zeros((1, 1), f32))
        sums_ref[:, :LANES] += jnp.where(lane == index, total, 0.0)


def assemble(near0, near1, far0, far1, rows_old, where, kind, shapes):
    outs = [jax.ShapeDtypeStruct(shape, f32) for shape in shapes]
    outs += [jax.ShapeDtypeStruct((shape[0], 1), f32) for shape in shapes]
    if kind == "packed":
        outs.append(jax.ShapeDtypeStruct((1, near0[0].shape[1]), f32))
    outs.append(
        jax.ShapeDtypeStruct((1, LANES + 2 * sum(shape[1] for shape in shapes)), f32)
    )
    return small_call(
        functools.partial(assemble_kernel, kind=kind, shapes=shapes),
        where,
        [*near0, *far0, *near1, *far1, *rows_old],
        outs,
        "assemble_" + kind,
    )


def per_device(
    tokens,
    cotangent,
    segment_ids,
    w_qkv,
    w_out,
    w_up,
    w_down,
    gain_attn,
    gain_mlp,
    row_qkv,
    col_qkv,
    row_out,
    col_out,
    row_up,
    col_up,
    row_down,
    col_down,
    var_attn,
    var_mlp,
):
    core = lax.axis_index("section")
    chip = lax.axis_index("ctx")
    depth = lax.axis_index("fsdp")
    y, x = chip // 2, chip % 2
    fsdp_count = lax.axis_size("fsdp")
    assert lax.axis_size("section") == 2 and lax.axis_size("ctx") == 4
    _, block, width = tokens.shape
    half = block // 2
    rows = w_qkv.shape[1]
    hidden_width = w_up.shape[2]
    unit = hidden_width // fsdp_count // 8
    scale = (width // HEADS) ** (-0.5)
    even = fsdp_count == 4 and rows == 2 * LANES and unit == LANES
    first_core, first_y, first_x = core == 0, y == 0, x == 0

    def flipped(when, value, axis=0):
        low, high = jnp.split(value, 2, axis)
        return jnp.where(when, jnp.concatenate([high, low], axis), value)

    at_eighth = 2 * chip + core

    def eighth(e):
        qkv = lax.dynamic_index_in_dim(w_qkv[0].reshape(rows, 3, 8, LANES), e, 2, keepdims=False)
        up = lax.dynamic_index_in_dim(
            w_up[0].reshape(rows, fsdp_count, 8, unit), e, 2, keepdims=False
        )
        down = lax.dynamic_slice_in_dim(w_down[0], e * unit, unit, 0)
        return [
            part.astype(bf16)
            for part in (qkv.reshape(rows, 3 * LANES), up.reshape(rows, fsdp_count * unit), down)
        ]

    def by_layer(mine, other):
        taken = swap_core(other)
        return jnp.where(first_core, mine, taken), jnp.where(first_core, taken, mine)

    def gather_rows(value):
        return lax.all_gather(value, "fsdp", axis=0, tiled=True)

    def rotations(value):
        return [value] + [
            lax.ppermute(
                value, "fsdp", [(i, (i + k) % fsdp_count) for i in range(fsdp_count)]
            )
            for k in range(1, fsdp_count)
        ]

    def with_far(value):
        return value, swap_y(value)

    chip_array = chip.reshape(1).astype(jnp.int32)

    def out_from_columns(columns):
        keep, came = columns[:2], swap_x(columns[2:])
        out = jax.ShapeDtypeStruct((2 * LANES, width), bf16)
        operands = [keep, came, swap_y(keep), swap_y(came)]
        return small_call(join_out_kernel, chip_array, operands, [out], "join_out")[0]

    weights, gains = [{}, {}], [None, None]
    depth_array = jnp.stack([depth, chip]).astype(jnp.int32)
    if even:
        cuts = cut_weights(
            w_qkv, w_out, w_up, w_down, gain_attn, gain_mlp, at_eighth.reshape(1).astype(jnp.int32)
        )
        packed_parts = by_layer(*cuts[:2])
        far_parts = by_layer(*cuts[2:4])
        up_parts = by_layer(*cuts[4:6])
        down_parts = by_layer(*cuts[6:])
        turns = rotations(packed_parts[0])
        fars = [swap_y(value[:rows, : 3 * LANES]) for value in turns[1:]]
        qkv, columns, gains[0] = place(turns, [far_parts[0]] + fars, depth_array, False)
        weights[0]["qkv"] = qkv
        weights[0]["out"] = out_from_columns(columns)
        up_gathered = [gather_rows(after(up_parts[0], *turns[1:])), gather_rows(up_parts[1])]
        down_gathered = [gather_rows(after(down_parts[0], *turns[1:])), gather_rows(down_parts[1])]
        packed_gathered = gather_rows(packed_parts[1])
    else:
        mine_parts, other_parts = eighth(at_eighth), eighth(at_eighth ^ 1)
        qkv_parts, up_parts, down_parts = [by_layer(a, b) for a, b in zip(mine_parts, other_parts)]
        whole_out = gather_rows(w_out[0].astype(bf16))
        out_parts = by_layer(whole_out, whole_out)
        gains_own = lax.all_gather(
            jnp.concatenate([gain_attn, gain_mlp], axis=0).astype(bf16), "fsdp", axis=1, tiled=True
        )
        gains = [part.astype(f32) for part in by_layer(gains_own, gains_own)]
        for layer in range(2):
            blocks = out_parts[layer].reshape(4, 2, LANES, width)
            blocks = lax.dynamic_index_in_dim(blocks, core, 1, keepdims=False)
            weights[layer] = dict(
                qkv=jnp.concatenate(with_far(gather_rows(qkv_parts[layer])), axis=1),
                out=jnp.concatenate(
                    [
                        lax.dynamic_index_in_dim(blocks, chip, 0, keepdims=False),
                        lax.dynamic_index_in_dim(blocks, chip ^ 2, 0, keepdims=False),
                    ],
                    axis=0,
                ),
                up=with_far(gather_rows(up_parts[layer])),
                down=with_far(gather_rows(down_parts[layer])),
            )

    def own_rows(value):
        near = lax.dynamic_slice(value, (y, core * half, 0), (1, half, width))[0]
        away = lax.dynamic_slice(value, (1 - y, core * half, 0), (1, half, width))[0]
        return [near, swap_y(away)]

    ids = lax.dynamic_index_in_dim(segment_ids, y, 0, keepdims=False).reshape(2, 2, 2, half)
    ids = flipped(~first_y, flipped(~first_x, flipped(~first_core, ids, 2), 1), 0)
    ids = ids.transpose(0, 2, 1, 3)
    key_ids = ids.reshape(8 * half, 1)
    query_ids = [ids[k].reshape(1, 4 * half) for k in range(2)]

    def forward(inputs, layer, hook):
        held = weights[layer]
        attn_gain, mlp_gain = gains[layer][0], gains[layer][1]
        inputs_all = [gather4(value) for value in inputs]
        first_in = hook("project", inputs_all[0])
        projected = [dot(value, held["qkv"]).astype(bf16) for value in (first_in, inputs_all[1])]
        keys_values = jnp.concatenate(projected, axis=0)

        def attend(k, queries):
            context, lse = attention_forward(queries, keys_values, query_ids[k], key_ids, scale)
            return context, lse, *fold_core(dot(context, held["out"]))

        context0, lse0, keep0, across0 = attend(0, hook("attend0", projected[0]))
        context1, lse1, keep1, across1 = attend(1, hook("attend1", after(projected[1], across0)))
        came0 = hook("norm0", after(swap_x(across0), across1))
        came1 = hook("norm1", swap_x(across1))
        unit_attn, scale_attn, normed, normed_all = [], [], [], []
        for k, (keep, came) in enumerate(((keep0, came0), (keep1, came1))):
            pre_attn = inputs[k].astype(f32) + keep + came.astype(f32)
            unit, factor = norm_parts(pre_attn)
            unit_attn.append(unit)
            scale_attn.append(factor)
            normed.append(unit * attn_gain)
        low = [value.astype(bf16) for value in normed]
        normed_all = [gather4(value) for value in low]

        def feed(value):
            activated, slope, partial = [], [], 0.0
            for half_up, half_down in zip(held["up"], held["down"]):
                upward = dot(value, half_up)
                phi_whole = 0.5 * (1.0 + lax.erf(upward * (0.5**0.5)))
                activated.append((upward * phi_whole).astype(bf16))
                density = jnp.exp(-0.5 * upward * upward) * 0.3989422804014327
                slope.append((phi_whole + upward * density).astype(bf16))
                partial += dot(activated[-1], half_down)
            return activated, slope, *fold_core(partial)

        activated0, slope0, keep0, across0 = feed(hook("feed0", after(normed_all[0], low[1])))
        activated1, slope1, keep1, across1 = feed(hook("feed1", after(normed_all[1], across0)))
        came0 = hook("last0", after(swap_x(across0), across1))
        came1 = swap_x(across1)
        unit_mlp, scale_mlp, outputs = [], [], []
        for k, (keep, came) in enumerate(((keep0, came0), (keep1, came1))):
            unit, factor = norm_parts(normed[k] + keep + came.astype(f32))
            unit_mlp.append(unit)
            scale_mlp.append(factor)
            outputs.append((unit * mlp_gain).astype(bf16))
        return outputs, dict(
            inputs_all=inputs_all,
            projected=projected,
            keys_values=keys_values,
            context=(context0, context1),
            lse=(lse0, lse1),
            unit_attn=unit_attn,
            scale_attn=scale_attn,
            normed_all=normed_all,
            activated=(activated0, activated1),
            slope=(slope0, slope1),
            unit_mlp=unit_mlp,
            scale_mlp=scale_mlp,
        )

    def backward(out_grads, kept, layer, hook):
        held = weights[layer]

        def over_tokens(left, right):
            return (rows_product(left[0], right[0]) + rows_product(left[1], right[1])).astype(bf16)

        def by_half(left, right):
            size = right[0].shape[1] // 2
            return [
                over_tokens(left, [value[:, at : at + size] for value in right])
                for at in (0, size)
            ]

        attn_gain, mlp_gain = gains[layer][0], gains[layer][1]
        mlp_in, mlp_gain_grad = [], 0.0
        for k in range(2):
            grad, gain_part = norm_back(
                out_grads[k].astype(f32), kept["unit_mlp"][k], kept["scale_mlp"][k], mlp_gain
            )
            mlp_in.append(grad)
            mlp_gain_grad += gain_part
        low = [value.astype(bf16) for value in mlp_in]
        down_all = [gather4(value) for value in low]

        def feed_back(k, value):
            grads, partial = [], 0.0
            for half_up, half_down, slope in zip(held["up"], held["down"], kept["slope"][k]):
                grad = times_transposed(value, half_down) * slope.astype(f32)
                grads.append(grad.astype(bf16))
                partial += times_transposed(grads[-1], half_up)
            return grads, *fold_core(partial)

        upward0, keep0, across0 = feed_back(0, hook("feed0", after(down_all[0], low[1])))
        upward1, keep1, across1 = feed_back(1, hook("feed1", after(down_all[1], across0)))
        came0 = hook(
            "norm0",
            after(swap_x(across0), across1),
            down=[over_tokens(left, down_all) for left in zip(*kept["activated"])],
        )
        came1 = swap_x(across1)
        upward_grad = (upward0, upward1)
        attn_in, attn_gain_grad = [], 0.0
        for k, (keep, came) in enumerate(((keep0, came0), (keep1, came1))):
            grad, gain_part = norm_back(
                mlp_in[k] + keep + came.astype(f32),
                kept["unit_attn"][k],
                kept["scale_attn"][k],
                attn_gain,
            )
            attn_in.append(grad)
            attn_gain_grad += gain_part
        low = [value.astype(bf16) for value in attn_in]
        branch_all = [gather4(value) for value in low]

        def attend_back(k, value):
            grads = times_transposed(value, held["out"]).astype(bf16)
            return attention_backward(
                kept["projected"][k],
                kept["keys_values"],
                grads,
                kept["lse"][k],
                query_ids[k],
                key_ids,
                scale,
            )

        grad_up = [over_tokens(kept["normed_all"], right) for right in zip(*upward_grad)]
        query0, key0, value0 = attend_back(
            0, hook("attend0", after(branch_all[0], low[1]), up=grad_up)
        )
        grad_out = over_tokens(kept["context"], branch_all)
        gain_grads = jnp.stack([attn_gain_grad, mlp_gain_grad])
        query1, key1, value1 = attend_back(
            1, hook("attend1", after(branch_all[1], query0), out=grad_out, gains=gain_grads)
        )
        key_grad, value_grad = (key0 + key1).astype(bf16), (value0 + value1).astype(bf16)
        stacked = []
        for k, query_grad in enumerate((query0, query1)):
            part = slice(4 * half * k, 4 * half * (k + 1))
            stacked.append(
                jnp.concatenate(
                    [
                        piece[:, LANES * p : LANES * (p + 1)]
                        for p in range(2)
                        for piece in (query_grad, key_grad[part], value_grad[part])
                    ],
                    axis=1,
                )
            )
        stacked[0] = hook("stacked", stacked[0])
        keep0, across0 = fold_core(times_transposed(stacked[0], held["qkv"]))
        stacked[1] = hook("stacked1", stacked[1])
        keep1, across1 = fold_core(times_transposed(stacked[1], held["qkv"]))
        came = (hook("last0", after(swap_x(across0), across1)), swap_x(across1))
        grad_qkv = by_half(kept["inputs_all"], stacked)
        in_grads = [
            (attn_in[k] + keep + came[k].astype(f32)).astype(bf16)
            for k, keep in enumerate((keep0, keep1))
        ]
        return in_grads, grad_qkv

    def scatter_rows(value):
        return lax.psum_scatter(value, "fsdp", scatter_dimension=0, tiled=True)

    def sync(value, *others):
        return lax.optimization_barrier((value, *others))

    def fold(keep, came):
        return (keep.astype(f32) + came.astype(f32)).astype(bf16)

    def halves(grad):
        return grad[0], swap_y(grad[1])

    def out_halves(grad_out):
        size = width // 2
        keep = lax.dynamic_slice_in_dim(grad_out, y * size, size, 1)
        give = lax.dynamic_slice_in_dim(grad_out, (1 - y) * size, size, 1)
        return keep.reshape(2, LANES, size), swap_y(give.reshape(2, LANES, size))

    def out_pair(keep, came):
        out = jax.ShapeDtypeStruct((2, LANES, 2 * LANES), bf16)
        near, give = small_call(fold_out_kernel, chip_array, [keep, came], [out, out], "fold_out")
        return near, swap_x(give)

    def pack(keep, came, near, cross, gain_grads):
        out = jax.ShapeDtypeStruct((4 * (rows + 16), 4 * LANES), bf16)
        operands = [keep, came, near, cross, gain_grads]
        return small_call(pack_kernel, chip_array, operands, [out], "pack_gradients")[0]

    def spread_start(value, y_first):
        return value, (swap_y if y_first else swap_x)(value)

    def spread_end(pair, y_first):
        value, first = pair
        if y_first:
            return [value, swap_x(value), first, swap_x(first)]
        return [value, first, swap_y(value), swap_y(first)]

    def spread(value, y_first):
        return spread_end(spread_start(value, y_first), y_first)

    def reduce_plain(grads, grad_qkv):
        keep, came = out_halves(grads["out"])
        both = fold(keep, came[::-1])
        placed = jnp.zeros((4, 2, LANES, width // 2), bf16)
        placed = lax.dynamic_update_slice(placed, both[:1, None], (chip, core, 0, 0))
        placed = lax.dynamic_update_slice(placed, both[1:, None], (chip ^ 2, core, 0, 0))
        gain_rows = grads["gains"].reshape(2, fsdp_count, rows).transpose(1, 0, 2)
        gain_rows = gain_rows.reshape(fsdp_count, 1, 2 * rows).astype(bf16)
        gain_rows = jnp.pad(gain_rows, ((0, 0), (0, 15), (0, width // 2 - 2 * rows)))
        packed = jnp.concatenate([placed.reshape(fsdp_count, rows, width // 2), gain_rows], axis=1)
        return [
            spread(scatter_rows(fold(*halves(grad_qkv))), False),
            spread(scatter_rows(packed.reshape(fsdp_count * (rows + 16), width // 2)), True),
            spread(scatter_rows(fold(*halves(grads["up"]))), False),
            spread(scatter_rows(fold(*halves(grads["down"]))), True),
        ]

    inputs = own_rows(tokens)
    out_grads = own_rows(cotangent)
    grads0, grads1 = {}, {}
    if even:
        down_got, up_got = {}, {}

        def hook_forward0(name, value):
            if name == "attend1":
                value, up, out_grads[1] = sync(value, up_gathered[0], out_grads[1])
                weights[0]["up"] = with_far(up)
            elif name == "norm0":
                value, far = sync(value, weights[0]["up"][1])
                weights[0]["up"] = weights[0]["up"][0], far
            elif name == "norm1":
                value, down = sync(value, down_gathered[0])
                weights[0]["down"] = with_far(down)
            elif name == "feed1":
                value, packed = sync(value, packed_gathered)
                near = packed.reshape(4, rows + 16, 4 * LANES)[:, :rows, : 3 * LANES]
                far = swap_y(near.reshape(4 * rows, 3 * LANES))
                qkv, columns, gains[1] = place([packed], [far], depth_array, True)
                weights[1].update(qkv=qkv, out=out_from_columns(columns))
            return value

        def hook_forward1(name, value):
            if name == "attend0":
                value, up = sync(value, up_gathered[1])
                weights[1]["up"] = with_far(up)
            elif name == "attend1":
                value, weights[1]["out"] = sync(value, weights[1]["out"])
            elif name == "norm0":
                value, far = sync(value, weights[1]["up"][1])
                weights[1]["up"] = weights[1]["up"][0], far
            elif name == "norm1":
                value, down = sync(value, down_gathered[1])
                weights[1]["down"] = with_far(down)
            return value

        def hook_backward1(name, value, **grads):
            if name == "norm0":
                value, *down = sync(value, *grads["down"])
                grads1["down"] = halves(down)
            elif name == "attend0":
                value, came, *up = sync(value, grads1["down"][1], *grads["up"])
                grads1["down"] = scatter_rows(fold(grads1["down"][0], came))
                grads1["up"] = halves(up)
            elif name == "attend1":
                value, grads1["whole_out"], grads1["gains"] = sync(
                    value, grads["out"], grads["gains"]
                )
            elif name == "stacked":
                value, came, *outputs = sync(value, grads1["up"][1], *hidden_away)
                grads1["up"] = scatter_rows(fold(grads1["up"][0], came))
                grads1["out"] = out_halves(grads1["whole_out"])
                hidden_away[:] = outputs
            elif name == "last0":
                value, came = sync(value, grads1["out"][1])
                grads1["out"] = out_pair(grads1["out"][0], came)
            return value

        def hook_backward0(name, value, **grads):
            if name == "feed0":
                value, down, out_came, *qkv = sync(
                    value, grads1["down"], grads1["out"][1], *grads1["qkv"]
                )
                grads1["out"] = grads1["out"][0], out_came
                grads1["qkv"] = halves(qkv)
                grads1["down"] = spread_start(down, True)
            elif name == "norm0":
                value, came, up1, hop, *down = sync(
                    value, grads1["qkv"][1], grads1["up"], grads1["down"][1], *grads["down"]
                )
                grads1["packed"] = scatter_rows(
                    pack(grads1["qkv"][0], came, *grads1["out"], grads1["gains"])
                )
                grads1["down"] = grads1["down"][0], hop
                grads1["up"] = up1
                grads0["down"] = halves(down)
            elif name == "attend0":
                value, came, *up = sync(value, grads0["down"][1], *grads["up"])
                grads0["down"] = scatter_rows(fold(grads0["down"][0], came))
                grads0["up"] = halves(up)
                grads1["up"] = spread_start(grads1["up"], False)
            elif name == "attend1":
                value, grads0["whole_out"], grads0["gains"], hop, packed1 = sync(
                    value, grads["out"], grads["gains"], grads1["up"][1], grads1["packed"]
                )
                grads1["up"] = grads1["up"][0], hop
                grads1["down"] = spread_end(grads1["down"], True)
                grads1["packed"] = spread_start(packed1, False)
            elif name == "stacked":
                value, came, hop, down, away, *ends = sync(
                    value,
                    grads0["up"][1],
                    grads1["packed"][1],
                    grads0["down"],
                    in_away[0],
                    *grads1["down"],
                )
                in_away[0] = away
                grads1["down"] = ends
                grads0["up"] = scatter_rows(fold(grads0["up"][0], came))
                grads0["out"] = out_halves(grads0["whole_out"])
                grads1["packed"] = grads1["packed"][0], hop
                grads0["down"] = spread_start(down, True)
                grads1["up"] = spread_end(grads1["up"], False)
            elif name == "last0":
                value, came = sync(value, grads0["out"][1])
                grads0["out"] = out_pair(grads0["out"][0], came)
            return value

    else:

        def hook_forward0(name, value):
            return value

        hook_forward1 = hook_forward0

        def hook_backward1(name, value, **grads):
            grads1.update(grads)
            return value

        def hook_backward0(name, value, **grads):
            grads0.update(grads)
            return value

    hidden0, saved0 = forward(inputs, 0, hook_forward0)
    hidden1, saved1 = forward(hidden0, 1, hook_forward1)
    hidden_away = [swap_y(hidden0[1]), swap_y(hidden1[1])]
    in_grads1, grad_qkv1 = backward(out_grads, saved1, 1, hook_backward1)
    grads1["qkv"] = grad_qkv1
    in_away = [swap_y(in_grads1[1])]
    in_grads0, grad_qkv0 = backward(in_grads1, saved0, 0, hook_backward0)
    if even:
        qkv_keep, qkv_came = halves(grad_qkv0)
        in_grads0[0], up0, hop = sync(in_grads0[0], grads0["up"], grads0["down"][1])
        grads0["down"] = grads0["down"][0], hop
        packed0 = scatter_rows(pack(qkv_keep, qkv_came, *grads0["out"], grads0["gains"]))
        near1 = [spread_end(grads1["packed"], False), grads1["up"], grads1["down"]]
        near0 = [spread(packed0, False), spread(up0, False), spread_end(grads0["down"], True)]
    else:
        near1, near0 = reduce_plain(grads1, grad_qkv1), reduce_plain(grads0, grad_qkv0)

    def to_owner(layer0, layer1, away):
        pairs = [jnp.stack([runs[0], far]) for runs, far in zip((layer0, layer1), away)]
        keep = jnp.where(first_core, pairs[0], pairs[1])
        take = swap_core(jnp.where(first_core, pairs[1], pairs[0]))
        both = flipped(~first_core, jnp.stack([keep, take], axis=1), 1)
        return flipped(~first_y, both, 0).reshape(2, block, width)

    hidden_out = to_owner(hidden0, hidden1, hidden_away)
    in_grads_out = to_owner(in_grads0, in_grads1, [swap_y(in_grads0[1]), in_away[0]])

    def natural(position):
        layers = jnp.stack(near0[position]), jnp.stack(near1[position])
        near = jnp.where(first_core, layers[0], layers[1])
        far = jnp.where(first_core, swap_core(layers[0]), swap_core(layers[1]))
        both = jnp.stack([near, far], axis=1)
        shape = both.shape
        both = both.reshape((2, 2, 2) + shape[2:])
        both = flipped(~first_y, flipped(~first_x, flipped(~first_core, both, 2), 1), 0)
        return both.reshape((8,) + shape[2:])

    rows_old = (row_qkv, row_out, row_up, row_down)
    if even:
        where = jnp.stack([at_eighth, core]).astype(jnp.int32)

        def build(position, kind, olds, shapes):
            return assemble(
                near0[position],
                near1[position],
                [swap_core(value) for value in near0[position]],
                [swap_core(value) for value in near1[position]],
                olds,
                where,
                kind,
                shapes,
            )

        def column(row):
            return row.reshape(-1, 1)

        down = build(2, "rows", [column(row_down)], ((8 * unit, width),))
        up = build(1, "columns", [column(row_up)], ((rows, hidden_width),))
        built = [None, None, up[:2], down[:2]]
        sums = {2: jnp.concatenate([up[2], down[2]], axis=1)}
        places = {2: (0, LANES), 3: (LANES + 2 * hidden_width, 2 * LANES + 2 * hidden_width)}
        places.update({0: (0, LANES), 1: (1, LANES + 6 * width)})

        def build_first(*tokens):
            first = build(
                0,
                "packed",
                [after(column(row_qkv), *tokens), column(row_out)],
                ((rows, 3 * width), (rows, width)),
            )
            built[:2] = (first[0], first[2]), (first[1], first[3])
            sums[0] = first[5]
            return first[4].reshape(2, rows)

    else:
        qkv = natural(0).reshape(8, rows, 3, LANES).transpose(1, 2, 0, 3).reshape(rows, 3 * width)
        out = natural(1).reshape(2, 4, rows + 16, width // 2).astype(f32).sum(axis=1)
        gain_shard = out[:, rows].sum(axis=0)[: 2 * rows].reshape(2, rows)
        out = out[:, :rows].transpose(1, 0, 2).reshape(rows, width)
        up = natural(2).reshape(8, rows, fsdp_count, unit).transpose(1, 2, 0, 3)
        up = up.reshape(rows, hidden_width)
        down = natural(3).reshape(8 * unit, width)
        built, parts = [], []
        for gradient, row_old in zip((qkv, out, up, down), rows_old):
            gradient = gradient.astype(f32)
            square = gradient * gradient
            row_new = decay_rate * row_old.reshape(-1, 1) + (1.0 - decay_rate) * jnp.mean(
                square, axis=1, keepdims=True
            )
            built.append((gradient, row_new))
            total_new = jnp.pad(jnp.sum(row_new).reshape(1, 1), ((0, 0), (0, LANES - 1)))
            parts.append(
                [
                    total_new,
                    jnp.sum(square, axis=0, keepdims=True),
                    jnp.sum(square / row_new, axis=0, keepdims=True),
                ]
            )
        blank = jnp.zeros_like(parts[0][0])
        sums = {
            2: jnp.concatenate(parts[2] + parts[3], axis=1),
            0: jnp.concatenate([blank] + parts[0] + parts[1], axis=1),
        }
        places = {2: (0, LANES), 3: (LANES + 2 * hidden_width, 2 * LANES + 2 * hidden_width)}
        places.update(
            {0: (LANES, 2 * LANES), 1: (2 * LANES + 6 * width, 3 * LANES + 6 * width)}
        )

        def build_first(*tokens):
            return gain_shard

    def sum_line(value):
        if fsdp_count != 4:
            return lax.psum(value, "fsdp")
        near, two, three = rotations(value)[1:]
        return (value + two) + (near + three)

    masters = (w_qkv[0], w_out[0], w_up[0], w_down[0])
    cols_old = (col_qkv, col_out, col_up, col_down)
    gain_masters = (gain_attn, gain_mlp)
    moments_old = (var_attn, var_mlp)

    def total(value):
        return jnp.sum(value).reshape(1, 1)

    new_rows, new_cols, ratios, new_masters = [None] * 4, [None] * 4, [None] * 4, [None] * 4

    def update(position, summed, weight_total):
        gradient, row_new = built[position]
        at_total, start = places[position]
        cols = gradient.shape[1]
        row_count = gradient.shape[0] * fsdp_count
        entry_count = row_count * cols
        col_all = summed[:, start : start + cols]
        ratio_all = summed[:, start + cols : start + 2 * cols]
        row_mean = summed[:, at_total : at_total + 1] / row_count
        new_rows[position] = row_new.reshape(1, -1)
        new_cols[position] = (
            decay_rate * cols_old[position] + (1.0 - decay_rate) * col_all / row_count
        )
        ratios[position] = jnp.sqrt(
            row_mean * total(ratio_all / new_cols[position]) / entry_count
        )
        weight_scale = jnp.sqrt(weight_total / entry_count + weight_eps)
        factor = step_rate * weight_scale / jnp.maximum(1.0, ratios[position] / clip_level)
        raw = gradient * lax.rsqrt(row_new * new_cols[position] / row_mean)
        new_masters[position] = masters[position] - factor * raw

    def lanes(values, start):
        row = jnp.concatenate(values, axis=1)
        return jnp.pad(row, ((0, 0), (start, LANES - start - row.shape[1])))

    def with_lanes(row, values):
        return jnp.concatenate([row[:, :LANES] + lanes(values, 2), row[:, LANES:]], axis=1)

    weight_totals = [total(master * master) for master in masters + gain_masters]
    summed = sum_line(with_lanes(sums[2], weight_totals))
    weight_all = [summed[:, 2 + i : 3 + i] for i in range(6)]
    for position in (2, 3):
        update(position, summed, weight_all[position])
    gain_shard = build_first(new_masters[2], new_masters[3])
    moments, gain_updates = [], []
    for gain_pos in range(2):
        grad = gain_shard[gain_pos : gain_pos + 1]
        moment = decay_rate * moments_old[gain_pos] + (1.0 - decay_rate) * grad * grad
        moments.append(moment)
        gain_updates.append(grad * lax.rsqrt(moment))
    summed = sum_line(with_lanes(sums[0], [total(step * step) for step in gain_updates]))
    for position in (0, 1):
        update(position, summed, weight_all[position])
    for gain_pos in range(2):
        clip_ratio = jnp.sqrt(summed[:, 2 + gain_pos : 3 + gain_pos] / width)
        weight_scale = jnp.sqrt(weight_all[4 + gain_pos] / width + weight_eps)
        factor = step_rate * weight_scale / jnp.maximum(1.0, clip_ratio / clip_level)
        new_masters.append(gain_masters[gain_pos] - factor * gain_updates[gain_pos])
        ratios.append(clip_ratio)
    return (
        hidden_out[None],
        in_grads_out[None],
        *[entry[0][None] for entry in built],
        gain_shard[:1],
        gain_shard[1:],
        *[master[None] for master in new_masters[:4]],
        new_masters[4],
        new_masters[5],
        new_rows[0],
        new_cols[0],
        new_rows[1],
        new_cols[1],
        new_rows[2],
        new_cols[2],
        new_rows[3],
        new_cols[3],
        moments[0],
        moments[1],
        jnp.concatenate(ratios, axis=1),
    )


def solution(mesh):
    in_specs = (
        P("fsdp", "ctx", None),
        P("fsdp", "ctx", None),
        P("fsdp", None),
        P("section", "fsdp", None),
        P("section", "fsdp", None),
        P("section", "fsdp", None),
        P("section", "fsdp", None),
        P("section", "fsdp"),
        P("section", "fsdp"),
        P("section", "fsdp"),
        P("section", None),
        P("section", "fsdp"),
        P("section", None),
        P("section", "fsdp"),
        P("section", None),
        P("section", "fsdp"),
        P("section", None),
        P("section", "fsdp"),
        P("section", "fsdp"),
    )
    out_specs = (
        P("section", "fsdp", "ctx", None),
        P("section", "fsdp", "ctx", None),
        P("section", "fsdp", None),
        P("section", "fsdp", None),
        P("section", "fsdp", None),
        P("section", "fsdp", None),
        P("section", "fsdp"),
        P("section", "fsdp"),
        P("section", "fsdp", None),
        P("section", "fsdp", None),
        P("section", "fsdp", None),
        P("section", "fsdp", None),
        P("section", "fsdp"),
        P("section", "fsdp"),
        P("section", "fsdp"),
        P("section", None),
        P("section", "fsdp"),
        P("section", None),
        P("section", "fsdp"),
        P("section", None),
        P("section", "fsdp"),
        P("section", None),
        P("section", "fsdp"),
        P("section", "fsdp"),
        P("section", None),
    )
    return jax.shard_map(
        per_device, mesh=mesh, in_specs=in_specs, out_specs=out_specs, check_vma=False
    )
```

```python
import functools
import types

import jax
import jax.numpy as jnp
from jax import lax
from jax.experimental import pallas as pl
from jax.experimental.pallas import tpu as pltpu
from jax.sharding import PartitionSpec as P

HEADS = 16


decay_rate = 0.5
clip_level = 0.5
step_rate = 1.0
norm_eps = 1e-05
weight_eps = 1e-06
mask_fill = -1e30

bf16 = jnp.bfloat16
f32 = jnp.float32
LANES = 128
SECTION, CTX, FSDP = "section", "ctx", "fsdp"
ROWS, COLUMNS, PACKED = range(3)


def swap_core(value):
    return lax.ppermute(value, SECTION, [(0, 1), (1, 0)])


def swap_x(value):
    return lax.ppermute(value, CTX, [(i, i ^ 1) for i in range(4)])


def swap_y(value):
    return lax.ppermute(value, CTX, [(i, i ^ 2) for i in range(4)])


def dot(left, right):
    return jnp.dot(left, right, preferred_element_type=f32)


def times_transposed(left, right):
    return lax.dot_general(left, right, (((1,), (1,)), ((), ())), preferred_element_type=f32)


def rows_product(left, right):
    return lax.dot_general(left, right, (((0,), (0,)), ((), ())), preferred_element_type=f32)


def after(value, *tokens):
    return lax.optimization_barrier((value, *tokens))[0]


def with_core(value):
    return jnp.concatenate([value, swap_core(value)], axis=0)


def gather_tiles(value):
    return [with_core(value), with_core(swap_x(value))]


def fold_core(partial):
    rows = partial.shape[0] // 2
    partial = partial.astype(bf16)
    return partial[:rows].astype(f32) + swap_core(partial[rows:]).astype(f32)


(PROJECT, ATTEND0, ATTEND1, STACKED, LAST, NORM, FEED0, FEED1) = range(8)


def norm_parts(values):
    center = values - jnp.mean(values, axis=-1, keepdims=True)
    spread = jnp.mean(center * center, axis=-1, keepdims=True)
    scale = lax.rsqrt(spread + norm_eps)
    return center * scale, scale


def norm_back(out_grad, unit, scale, gain):
    scaled = out_grad * gain
    mean_scaled = jnp.mean(scaled, axis=-1, keepdims=True)
    mean_unit = jnp.mean(scaled * unit, axis=-1, keepdims=True)
    return scale * (scaled - mean_scaled - unit * mean_unit), jnp.sum(out_grad * unit, axis=0)


def nt(left, right):
    return lax.dot_general(left, right, (((1,), (1,)), ((), ())), preferred_element_type=f32)


def attention_kernel(q_ref, k_ref, v_ref, qid_ref, kid_ref, out_ref, lse_ref, *, scale):
    queries = q_ref[...] * jnp.asarray(scale, bf16)
    keys, values_t = k_ref[...], v_ref[...].T
    same = kid_ref[...] == qid_ref[...]
    first = lax.broadcasted_iota(jnp.int32, queries.shape, 1) < queries.shape[1] // 2
    parts = []
    for head in range(2):
        own = jnp.where(first if head == 0 else ~first, queries, jnp.zeros_like(queries))
        scores = jnp.where(same, nt(keys, own), mask_fill)
        peak = jnp.max(scores, axis=0, keepdims=True)
        weights = jnp.exp(scores - peak)
        total = jnp.sum(weights, axis=0, keepdims=True)
        lse_ref[0, head : head + 1, :] = peak + jnp.log(total)
        parts.append(dot(values_t, weights.astype(bf16)) * (1.0 / total))
    width = values_t.shape[0] // 2
    stacked = jnp.concatenate([parts[0][:width], parts[1][width:]], axis=0)
    out_ref[...] = stacked.T.astype(bf16)


def attention_forward(projected, keys_values, query_ids, key_ids, scale):
    rows, seq_len = projected.shape[0], keys_values.shape[0]
    tile = min(256, rows)
    elems = 4 * rows * seq_len
    return pl.pallas_call(
        functools.partial(attention_kernel, scale=scale),
        grid=(2, rows // tile),
        in_specs=[
            pl.BlockSpec((tile, LANES), lambda p, i: (i, 3 * p)),
            pl.BlockSpec((seq_len, LANES), lambda p, i: (0, 3 * p + 1)),
            pl.BlockSpec((seq_len, LANES), lambda p, i: (0, 3 * p + 2)),
            pl.BlockSpec((1, tile), lambda p, i: (0, i)),
            pl.BlockSpec((seq_len, 1), lambda p, i: (0, 0)),
        ],
        out_specs=[
            pl.BlockSpec((tile, LANES), lambda p, i: (i, p)),
            pl.BlockSpec((1, 2, tile), lambda p, i: (p, 0, i)),
        ],
        out_shape=[
            jax.ShapeDtypeStruct((rows, 2 * LANES), bf16),
            jax.ShapeDtypeStruct((2, 2, rows), f32),
        ],
        compiler_params=pltpu.CompilerParams(vmem_limit_bytes=32 << 20),
        cost_estimate=pl.CostEstimate(
            flops=elems * 4 * 128, bytes_accessed=4 << 20, transcendentals=elems
        ),
    )(projected, keys_values, keys_values, query_ids, key_ids)


def attention_back_kernel(
    q_ref, k_ref, v_ref, g_ref, lse_ref, qid_ref, kid_ref, dq_ref, dk_ref, dv_ref, *, scale
):
    queries = q_ref[...] * jnp.asarray(scale, bf16)
    keys, values, grads = k_ref[...], v_ref[...], g_ref[...]
    keys_t = keys.T
    same = kid_ref[...] == qid_ref[...]
    first = lax.broadcasted_iota(jnp.int32, queries.shape, 1) < queries.shape[1] // 2

    @pl.when(pl.program_id(1) == 0)
    def _():
        dk_ref[...] = jnp.zeros_like(dk_ref)
        dv_ref[...] = jnp.zeros_like(dv_ref)

    parts = []
    for head in range(2):
        mine = first if head == 0 else ~first
        own = jnp.where(mine, queries, jnp.zeros_like(queries))
        own_grads = jnp.where(mine, grads, jnp.zeros_like(grads))
        scores = jnp.where(same, nt(keys, own), mask_fill)
        weights = jnp.exp(scores - lse_ref[0, head : head + 1, :])
        prob_grad = nt(values, own_grads)
        row_dot = jnp.sum(weights * prob_grad, axis=0, keepdims=True)
        score_grad = (weights * (prob_grad - row_dot)).astype(bf16)
        dv_ref[...] += dot(weights.astype(bf16), own_grads)
        dk_ref[...] += dot(score_grad, own)
        parts.append(dot(keys_t, score_grad))
    width = keys_t.shape[0] // 2
    stacked = jnp.concatenate([parts[0][:width], parts[1][width:]], axis=0)
    dq_ref[...] = (stacked.T * scale).astype(bf16)


def attention_backward(projected, keys_values, grads, lse, query_ids, key_ids, scale):
    rows, seq_len = projected.shape[0], keys_values.shape[0]
    tile = min(256, rows)
    elems = 4 * rows * seq_len
    return pl.pallas_call(
        functools.partial(attention_back_kernel, scale=scale),
        grid=(2, rows // tile),
        in_specs=[
            pl.BlockSpec((tile, LANES), lambda p, i: (i, 3 * p)),
            pl.BlockSpec((seq_len, LANES), lambda p, i: (0, 3 * p + 1)),
            pl.BlockSpec((seq_len, LANES), lambda p, i: (0, 3 * p + 2)),
            pl.BlockSpec((tile, LANES), lambda p, i: (i, p)),
            pl.BlockSpec((1, 2, tile), lambda p, i: (p, 0, i)),
            pl.BlockSpec((1, tile), lambda p, i: (0, i)),
            pl.BlockSpec((seq_len, 1), lambda p, i: (0, 0)),
        ],
        out_specs=[
            pl.BlockSpec((tile, LANES), lambda p, i: (i, p)),
            pl.BlockSpec((seq_len, LANES), lambda p, i: (0, p)),
            pl.BlockSpec((seq_len, LANES), lambda p, i: (0, p)),
        ],
        out_shape=[
            jax.ShapeDtypeStruct((rows, 2 * LANES), bf16),
            jax.ShapeDtypeStruct((seq_len, 2 * LANES), f32),
            jax.ShapeDtypeStruct((seq_len, 2 * LANES), f32),
        ],
        compiler_params=pltpu.CompilerParams(vmem_limit_bytes=32 << 20),
        cost_estimate=pl.CostEstimate(
            flops=elems * 10 * 128, bytes_accessed=6 << 20, transcendentals=elems
        ),
    )(projected, keys_values, keys_values, grads, lse, query_ids, key_ids)


def whole(shape):
    return pl.BlockSpec(shape, lambda *_: (0,) * len(shape))


def cut_kernel(_, *refs, width):
    first, up, down = refs[:16], refs[16:24], refs[24:26]
    packed, far, ups, downs = refs[26:28], refs[28:30], refs[30:32], refs[32:34]
    rows = first[0].shape[1]
    for core in range(2):
        for i in range(3):
            lanes = slice(LANES * i, LANES * (i + 1))
            packed[core][:rows, lanes] = first[3 * core + i][0].astype(bf16)
            far[core][:, lanes] = first[6 + 3 * core + i][0].astype(bf16)
        out = first[12 + core][0].astype(bf16)
        packed[core][:LANES, 3 * LANES :] = out[:, :LANES]
        packed[core][LANES:rows, 3 * LANES :] = out[:, LANES:]
        gains = jnp.concatenate([first[14][...], first[15][...]], axis=1)
        top = lax.broadcasted_iota(jnp.int32, (16, 2 * rows), 0) == 0
        gains = jnp.where(top, jnp.broadcast_to(gains, (16, 2 * rows)), 0.0)
        packed[core][rows:, :] = gains.astype(bf16)
        for i in range(4):
            ups[core][:, LANES * i : LANES * (i + 1)] = up[4 * core + i][0].astype(bf16)
        downs[core][...] = down[core][0].astype(bf16)


def cut_weights(w_qkv, w_out, w_up, w_down, gain_attn, gain_mlp, at_eighth):
    rows, width = w_qkv.shape[1], w_out.shape[2]

    def column(i, flip):
        return pl.BlockSpec((1, rows, LANES), lambda g, at: (0, 0, 8 * i + (at[0] ^ flip)))

    specs = [column(i, flip) for flip in (0, 1, 4, 5) for i in range(3)]
    specs += [
        pl.BlockSpec(
            (1, LANES, 2 * LANES), lambda g, at, c=core: (0, (at[0] & 1) ^ c, at[0] >> 1)
        )
        for core in range(2)
    ]
    specs += [whole(gain_attn.shape), whole(gain_mlp.shape)]
    specs += [column(i, core) for core in range(2) for i in range(4)]
    specs += [
        pl.BlockSpec((1, LANES, width), lambda g, at, c=core: (0, at[0] ^ c, 0))
        for core in range(2)
    ]
    outs = [
        jax.ShapeDtypeStruct(shape, bf16)
        for shape in (
            (rows + 16, 4 * LANES),
            (rows, 3 * LANES),
            (rows, 4 * LANES),
            (LANES, width),
        )
        for _ in range(2)
    ]
    operands = [w_qkv] * 12 + [w_out] * 2 + [gain_attn, gain_mlp] + [w_up] * 8 + [w_down] * 2
    return pl.pallas_call(
        functools.partial(cut_kernel, width=width),
        grid_spec=pltpu.PrefetchScalarGridSpec(
            num_scalar_prefetch=1,
            grid=(1,),
            in_specs=specs,
            out_specs=[whole(out.shape) for out in outs],
        ),
        out_shape=outs,
        compiler_params=pltpu.CompilerParams(vmem_limit_bytes=56 << 20),
    )(at_eighth, *operands)


def place_kernel(at, *refs, fixed):
    qkv_ref, out_ref, gain_ref = refs[-3:]
    count = (len(refs) - 3) // 2
    rows, cols = refs[count].shape
    for k in range(count):
        slot = k if fixed else lax.rem(at[0] + count - k, count)
        packed, far = refs[k], refs[count + k]
        part = pl.ds(pl.multiple_of(slot * rows, rows), rows)
        qkv_ref[part, :cols] = packed[:rows, :cols]
        qkv_ref[part, cols:] = far[...]
        away = slot ^ at[1]
        away = 2 * (away & 1) + (away >> 1)
        out_ref[away, :, :LANES] = packed[:LANES, cols:]
        out_ref[away, :, LANES:] = packed[LANES:rows, cols:]
        part = pl.ds(pl.multiple_of(slot * rows, rows), rows)
        gains = packed[rows:, :].astype(f32)
        gain_ref[0:1, part] = gains[0:1, :rows]
        gain_ref[1:2, part] = gains[0:1, rows:]


def place(packed, far, depth, fixed):
    count = 4
    rows, cols = far[0].shape
    if fixed:
        rows = rows // count
    shapes = ((rows + 16, cols + LANES), (rows, cols))
    specs = [
        pl.BlockSpec(shape, (lambda g, at, k=k: (k, 0)) if fixed else (lambda g, at: (0, 0)))
        for shape in shapes
        for k in range(count)
    ]
    outs = [
        jax.ShapeDtypeStruct((rows * count, 2 * cols), bf16),
        jax.ShapeDtypeStruct((count, LANES, 2 * LANES), bf16),
        jax.ShapeDtypeStruct((2, rows * count), f32),
    ]
    return pl.pallas_call(
        functools.partial(place_kernel, fixed=fixed),
        grid_spec=pltpu.PrefetchScalarGridSpec(
            num_scalar_prefetch=1,
            grid=(1,),
            in_specs=specs,
            out_specs=[whole(out.shape) for out in outs],
        ),
        out_shape=outs,
        compiler_params=pltpu.CompilerParams(vmem_limit_bytes=24 << 20),
    )(depth, *(list(packed) * (count if fixed else 1)), *(list(far) * (count if fixed else 1)))


def small_call(kernel, at, operands, outs):
    return pl.pallas_call(
        kernel,
        grid_spec=pltpu.PrefetchScalarGridSpec(
            num_scalar_prefetch=1,
            grid=(1,),
            in_specs=[whole(value.shape) for value in operands],
            out_specs=[whole(out.shape) for out in outs],
        ),
        out_shape=outs,
        compiler_params=pltpu.CompilerParams(vmem_limit_bytes=40 << 20),
    )(at, *operands)


def join_out_kernel(at, keep, came, far_keep, far_came, out_ref):
    for b in range(2):
        rows = slice(LANES * b, LANES * (b + 1))
        for away, value in enumerate((keep[b], came[b], far_keep[1 - b], far_came[1 - b])):
            size = value.shape[1]
            start = pl.multiple_of((at[0] ^ away) * size, size)
            out_ref[rows, pl.ds(start, size)] = value


def fold_out_kernel(at, keep, came, near_ref, give_ref):
    size = near_ref.shape[2]
    first_x = (at[0] & 1) == 0
    for b in range(2):
        value = keep[b].astype(f32) + came[1 - b].astype(f32)
        low, high = value[:, :size], value[:, size:]
        near_ref[b] = jnp.where(first_x, low, high).astype(bf16)
        give_ref[b] = jnp.where(first_x, high, low).astype(bf16)


def pack_kernel(at, keep, came, near, cross, gains, out_ref):
    cols = keep.shape[1]
    rows = keep.shape[0] // 4
    top = lax.broadcasted_iota(jnp.int32, (16, 2 * rows), 0) == 0
    for f in range(4):
        base = f * (rows + 16)
        part = slice(rows * f, rows * (f + 1))
        out_ref[base : base + rows, :cols] = (
            keep[part, :].astype(f32) + came[part, :].astype(f32)
        ).astype(bf16)
        gain = jnp.concatenate([gains[0:1, part], gains[1:2, part]], axis=1)
        gain = jnp.where(top, jnp.broadcast_to(gain, (16, 2 * rows)), 0.0)
        out_ref[base + rows : base + rows + 16, :] = gain.astype(bf16)
    for away, value in enumerate((near[0], cross[0], near[1], cross[1])):
        base = (at[0] ^ away) * (rows + 16)
        for half in range(2):
            start = pl.multiple_of(base + LANES * half, 16)
            out_ref[pl.ds(start, LANES), cols:] = value[:, LANES * half : LANES * (half + 1)]


def assemble_kernel(at, *refs, kind, shapes):
    groups = [refs[4 * i : 4 * i + 4] for i in range(4)]
    rows_old = refs[16 : 16 + len(shapes)]
    outs = refs[16 + len(shapes) :]
    grads, rows_new, sums_ref = outs[: len(shapes)], outs[len(shapes) : 2 * len(shapes)], outs[-1]
    first_core = at[1] == 0
    gain = 0.0
    for core in range(2):
        for chip in range(4):
            eighth = (2 * chip + core) ^ at[0]
            value = jnp.where(first_core, groups[core][chip][...], groups[2 + core][chip][...])
            value = value.astype(f32)
            if kind == ROWS:
                rows = value.shape[0]
                grads[0][pl.ds(pl.multiple_of(eighth * rows, rows), rows), :] = value
            elif kind == COLUMNS:
                for i in range(value.shape[1] // LANES):
                    start = pl.multiple_of((8 * i + eighth) * LANES, LANES)
                    grads[0][:, pl.ds(start, LANES)] = value[:, LANES * i : LANES * (i + 1)]
            else:
                rows = shapes[0][0]
                for i in range(3):
                    start = pl.multiple_of((8 * i + eighth) * LANES, LANES)
                    grads[0][:, pl.ds(start, LANES)] = value[:rows, LANES * i : LANES * (i + 1)]
                part = pl.ds(pl.multiple_of((eighth & 1) * LANES, LANES), LANES)
                for half in range(2):
                    start = pl.multiple_of((2 * (eighth >> 1) + half) * LANES, LANES)
                    block = value[half * LANES : (half + 1) * LANES, 3 * LANES :]
                    grads[1][part, pl.ds(start, LANES)] = block
                gain = gain + value[rows : rows + 1, :]
    if kind == PACKED:
        outs[-2][...] = gain
    sums_ref[...] = jnp.zeros_like(sums_ref)
    lane = lax.broadcasted_iota(jnp.int32, (1, LANES), 1)
    begin = LANES
    for index, (total_rows, cols) in enumerate(shapes):
        grad_ref, row_ref, new_ref = grads[index], rows_old[index], rows_new[index]
        col_part = slice(begin, begin + cols)
        ratio_part = slice(begin + cols, begin + 2 * cols)
        begin += 2 * cols

        def body(i, total):
            part = pl.ds(pl.multiple_of(i * 64, 64), 64)
            values = grad_ref[part, :]
            square = values * values
            row_new = decay_rate * row_ref[part, :] + (1.0 - decay_rate) * (
                jnp.sum(square, axis=1, keepdims=True) / cols
            )
            new_ref[part, :] = row_new
            sums_ref[:, col_part] += jnp.sum(square, axis=0, keepdims=True)
            sums_ref[:, ratio_part] += jnp.sum(square * (1.0 / row_new), axis=0, keepdims=True)
            return total + jnp.sum(row_new, axis=0, keepdims=True)

        total = lax.fori_loop(0, total_rows // 64, body, jnp.zeros((1, 1), f32))
        sums_ref[:, :LANES] += jnp.where(lane == index, total, 0.0)


def assemble(near0, near1, far0, far1, rows_old, where, kind, shapes):
    outs = [jax.ShapeDtypeStruct(shape, f32) for shape in shapes]
    outs += [jax.ShapeDtypeStruct((shape[0], 1), f32) for shape in shapes]
    if kind == PACKED:
        outs.append(jax.ShapeDtypeStruct((1, near0[0].shape[1]), f32))
    outs.append(
        jax.ShapeDtypeStruct((1, LANES + 2 * sum(shape[1] for shape in shapes)), f32)
    )
    return small_call(
        functools.partial(assemble_kernel, kind=kind, shapes=shapes),
        where,
        [*near0, *far0, *near1, *far1, *rows_old],
        outs,
    )


def per_device(
    tokens,
    cotangent,
    segment_ids,
    w_qkv,
    w_out,
    w_up,
    w_down,
    gain_attn,
    gain_mlp,
    row_qkv,
    col_qkv,
    row_out,
    col_out,
    row_up,
    col_up,
    row_down,
    col_down,
    var_attn,
    var_mlp,
):
    core = lax.axis_index(SECTION)
    chip = lax.axis_index(CTX)
    depth = lax.axis_index(FSDP)
    y, x = chip // 2, chip % 2
    fsdp_count = lax.axis_size(FSDP)
    assert lax.axis_size(SECTION) == 2 and lax.axis_size(CTX) == 4
    _, block, width = tokens.shape
    half = block // 2
    rows = w_qkv.shape[1]
    hidden_width = w_up.shape[2]
    unit = hidden_width // fsdp_count // 8
    scale = (width // HEADS) ** (-0.5)
    even = fsdp_count == 4 and rows == 2 * LANES and unit == LANES
    first_core, first_y, first_x = core == 0, y == 0, x == 0

    def flipped(when, value, axis=0):
        low, high = jnp.split(value, 2, axis)
        return jnp.where(when, jnp.concatenate([high, low], axis), value)

    at_eighth = 2 * chip + core

    def eighth(e):
        qkv = lax.dynamic_index_in_dim(w_qkv[0].reshape(rows, 3, 8, LANES), e, 2, keepdims=False)
        up = lax.dynamic_index_in_dim(
            w_up[0].reshape(rows, fsdp_count, 8, unit), e, 2, keepdims=False
        )
        down = lax.dynamic_slice_in_dim(w_down[0], e * unit, unit, 0)
        return [
            part.astype(bf16)
            for part in (qkv.reshape(rows, 3 * LANES), up.reshape(rows, fsdp_count * unit), down)
        ]

    def by_layer(mine, other):
        taken = swap_core(other)
        return jnp.where(first_core, mine, taken), jnp.where(first_core, taken, mine)

    def gather_rows(value):
        return lax.all_gather(value, FSDP, axis=0, tiled=True)

    def rotations(value):
        return [value] + [
            lax.ppermute(
                value, FSDP, [(i, (i + k) % fsdp_count) for i in range(fsdp_count)]
            )
            for k in range(1, fsdp_count)
        ]

    def with_far(value):
        return value, swap_y(value)

    chip_array = chip.reshape(1).astype(jnp.int32)

    def out_from_columns(columns):
        keep, came = columns[:2], swap_x(columns[2:])
        out = jax.ShapeDtypeStruct((2 * LANES, width), bf16)
        operands = [keep, came, swap_y(keep), swap_y(came)]
        return small_call(join_out_kernel, chip_array, operands, [out])[0]

    weights, gains = [types.SimpleNamespace(), types.SimpleNamespace()], [None, None]
    depth_array = jnp.stack([depth, chip]).astype(jnp.int32)
    if even:
        cuts = cut_weights(
            w_qkv, w_out, w_up, w_down, gain_attn, gain_mlp, at_eighth.reshape(1).astype(jnp.int32)
        )
        packed_parts = by_layer(*cuts[:2])
        far_parts = by_layer(*cuts[2:4])
        up_parts = by_layer(*cuts[4:6])
        down_parts = by_layer(*cuts[6:])
        turns = rotations(packed_parts[0])
        fars = [swap_y(value[:rows, : 3 * LANES]) for value in turns[1:]]
        qkv, columns, gains[0] = place(turns, [far_parts[0]] + fars, depth_array, False)
        weights[0].qkv = qkv
        weights[0].out = out_from_columns(columns)
        up_gathered = [gather_rows(after(up_parts[0], *turns[1:])), gather_rows(up_parts[1])]
        down_gathered = [gather_rows(after(down_parts[0], *turns[1:])), gather_rows(down_parts[1])]
        packed_gathered = gather_rows(packed_parts[1])
    else:
        mine_parts, other_parts = eighth(at_eighth), eighth(at_eighth ^ 1)
        qkv_parts, up_parts, down_parts = [by_layer(a, b) for a, b in zip(mine_parts, other_parts)]
        whole_out = gather_rows(w_out[0].astype(bf16))
        out_parts = by_layer(whole_out, whole_out)
        gains_own = lax.all_gather(
            jnp.concatenate([gain_attn, gain_mlp], axis=0).astype(bf16), FSDP, axis=1, tiled=True
        )
        gains = [part.astype(f32) for part in by_layer(gains_own, gains_own)]
        for layer in range(2):
            blocks = out_parts[layer].reshape(4, 2, LANES, width)
            blocks = lax.dynamic_index_in_dim(blocks, core, 1, keepdims=False)
            weights[layer] = types.SimpleNamespace(
                qkv=jnp.concatenate(with_far(gather_rows(qkv_parts[layer])), axis=1),
                out=jnp.concatenate(
                    [
                        lax.dynamic_index_in_dim(blocks, chip, 0, keepdims=False),
                        lax.dynamic_index_in_dim(blocks, chip ^ 2, 0, keepdims=False),
                    ],
                    axis=0,
                ),
                up=with_far(gather_rows(up_parts[layer])),
                down=with_far(gather_rows(down_parts[layer])),
            )

    def own_rows(value):
        near = lax.dynamic_slice(value, (y, core * half, 0), (1, half, width))[0]
        away = lax.dynamic_slice(value, (1 - y, core * half, 0), (1, half, width))[0]
        return jnp.concatenate([near, swap_y(away)], axis=0)

    ids = lax.dynamic_index_in_dim(segment_ids, y, 0, keepdims=False).reshape(2, 2, 2, half)
    ids = flipped(~first_y, flipped(~first_x, flipped(~first_core, ids, 2), 1), 0)
    ids = ids.transpose(1, 2, 0, 3)
    key_ids = ids.reshape(8 * half, 1)
    query_ids = [ids[k].reshape(1, 4 * half) for k in range(2)]

    def forward(inputs, layer, hook):
        held = weights[layer]
        attn_gain, mlp_gain = gains[layer][0], gains[layer][1]
        inputs_all = gather_tiles(inputs)
        projected = [dot(value, held.qkv).astype(bf16) for value in inputs_all]
        keys_values = jnp.concatenate(projected, axis=0)

        def attend(k, queries):
            context, lse = attention_forward(queries, keys_values, query_ids[k], key_ids, scale)
            return context, lse, fold_core(dot(context, held.out))

        context1, lse1, across = attend(1, hook(ATTEND0, projected[1]))
        across = across.astype(bf16)
        context0, lse0, keep = attend(0, hook(ATTEND1, after(projected[0], across)))
        came = hook(NORM, after(swap_x(across), keep))
        unit_attn, scale_attn = norm_parts(inputs.astype(f32) + keep + came.astype(f32))
        normed = unit_attn * attn_gain
        normed_all = gather_tiles(normed.astype(bf16))

        def feed(value):
            activated, slope, partial = [], [], 0.0
            for half_up, half_down in zip(held.up, held.down):
                upward = dot(value, half_up)
                phi_whole = 0.5 * (1.0 + lax.erf(upward * (0.5**0.5)))
                activated.append((upward * phi_whole).astype(bf16))
                density = jnp.exp(-0.5 * upward * upward) * 0.3989422804014327
                slope.append((phi_whole + upward * density).astype(bf16))
                partial += dot(activated[-1], half_down)
            return activated, slope, fold_core(partial)

        activated0, slope0, keep = feed(hook(FEED0, normed_all[0]))
        activated1, slope1, across = feed(hook(FEED1, after(normed_all[1], keep)))
        came = hook(LAST, swap_x(across.astype(bf16)))
        unit_mlp, scale_mlp = norm_parts(normed + keep + came.astype(f32))
        return (unit_mlp * mlp_gain).astype(bf16), types.SimpleNamespace(
            inputs_all=inputs_all,
            projected=projected,
            keys_values=keys_values,
            context=(context0, context1),
            lse=(lse0, lse1),
            unit_attn=unit_attn,
            scale_attn=scale_attn,
            normed_all=normed_all,
            activated=(activated0, activated1),
            slope=(slope0, slope1),
            unit_mlp=unit_mlp,
            scale_mlp=scale_mlp,
        )

    def backward(out_grads, kept, layer, hook):
        held = weights[layer]
        attn_gain, mlp_gain = gains[layer][0], gains[layer][1]

        def over_tokens(left, right):
            return (rows_product(left[0], right[0]) + rows_product(left[1], right[1])).astype(bf16)

        def by_half(left, right):
            size = right[0].shape[1] // 2
            return [
                over_tokens(left, [value[:, at : at + size] for value in right])
                for at in (0, size)
            ]

        mlp_in, mlp_gain_grad = norm_back(
            out_grads.astype(f32), kept.unit_mlp, kept.scale_mlp, mlp_gain
        )
        down_all = gather_tiles(mlp_in.astype(bf16))

        def feed_back(k, value):
            grads, partial = [], 0.0
            for half_up, half_down, slope in zip(held.up, held.down, kept.slope[k]):
                grad = times_transposed(value, half_down) * slope.astype(f32)
                grads.append(grad.astype(bf16))
                partial += times_transposed(grads[-1], half_up)
            return grads, fold_core(partial)

        upward0, keep = feed_back(0, hook(FEED0, down_all[0]))
        upward1, across = feed_back(1, hook(FEED1, after(down_all[1], keep)))
        grad_down = [over_tokens(left, down_all) for left in zip(*kept.activated)]
        came = hook(NORM, swap_x(across.astype(bf16)), grad_down)
        attn_in, attn_gain_grad = norm_back(
            mlp_in + keep + came.astype(f32), kept.unit_attn, kept.scale_attn, attn_gain
        )
        branch_all = gather_tiles(attn_in.astype(bf16))

        def attend_back(k, value):
            grads = times_transposed(value, held.out).astype(bf16)
            return attention_backward(
                kept.projected[k],
                kept.keys_values,
                grads,
                kept.lse[k],
                query_ids[k],
                key_ids,
                scale,
            )

        grad_up = [over_tokens(kept.normed_all, right) for right in zip(upward0, upward1)]
        query0, key0, value0 = attend_back(0, hook(ATTEND0, branch_all[0], grad_up))
        query1, key1, value1 = attend_back(1, hook(ATTEND1, after(branch_all[1], query0)))
        key_grad, value_grad = (key0 + key1).astype(bf16), (value0 + value1).astype(bf16)
        stacked = []
        for k, query_grad in enumerate((query0, query1)):
            part = slice(4 * half * k, 4 * half * (k + 1))
            stacked.append(
                jnp.concatenate(
                    [
                        piece[:, LANES * p : LANES * (p + 1)]
                        for p in range(2)
                        for piece in (query_grad, key_grad[part], value_grad[part])
                    ],
                    axis=1,
                )
            )
        stacked[1] = hook(STACKED, stacked[1])
        across = fold_core(times_transposed(stacked[1], held.qkv)).astype(bf16)
        keep = fold_core(times_transposed(after(stacked[0], across), held.qkv))
        gain_grads = jnp.stack([attn_gain_grad, mlp_gain_grad])
        grad_out = over_tokens(kept.context, branch_all)
        came = hook(LAST, after(swap_x(across), keep), grad_out, gain_grads)
        grad_qkv = by_half(kept.inputs_all, stacked)
        return (attn_in + keep + came.astype(f32)).astype(bf16), grad_qkv

    def scatter_rows(value):
        return lax.psum_scatter(value, FSDP, scatter_dimension=0, tiled=True)

    def sync(value, *others):
        return lax.optimization_barrier((value, *others))

    def fold(keep, came):
        return (keep.astype(f32) + came.astype(f32)).astype(bf16)

    def halves(grad):
        return grad[0], swap_y(grad[1])

    def out_halves(grad_out):
        size = width // 2
        keep = lax.dynamic_slice_in_dim(grad_out, y * size, size, 1)
        give = lax.dynamic_slice_in_dim(grad_out, (1 - y) * size, size, 1)
        return keep.reshape(2, LANES, size), swap_y(give.reshape(2, LANES, size))

    def out_pair(keep, came):
        out = jax.ShapeDtypeStruct((2, LANES, 2 * LANES), bf16)
        near, give = small_call(fold_out_kernel, chip_array, [keep, came], [out, out])
        return near, swap_x(give)

    def pack(keep, came, near, cross, gain_grads):
        out = jax.ShapeDtypeStruct((4 * (rows + 16), 4 * LANES), bf16)
        operands = [keep, came, near, cross, gain_grads]
        return small_call(pack_kernel, chip_array, operands, [out])[0]

    def spread_start(value, y_first):
        return value, (swap_y if y_first else swap_x)(value)

    def spread_end(pair, y_first):
        value, first = pair
        if y_first:
            return [value, swap_x(value), first, swap_x(first)]
        return [value, first, swap_y(value), swap_y(first)]

    def spread(value, y_first):
        return spread_end(spread_start(value, y_first), y_first)

    def reduce_plain(found):
        keep, came = out_halves(found.out)
        both = fold(keep, came[::-1])
        placed = jnp.zeros((4, 2, LANES, width // 2), bf16)
        placed = lax.dynamic_update_slice(placed, both[:1, None], (chip, core, 0, 0))
        placed = lax.dynamic_update_slice(placed, both[1:, None], (chip ^ 2, core, 0, 0))
        gain_rows = found.gains.reshape(2, fsdp_count, rows).transpose(1, 0, 2)
        gain_rows = gain_rows.reshape(fsdp_count, 1, 2 * rows).astype(bf16)
        gain_rows = jnp.pad(gain_rows, ((0, 0), (0, 15), (0, width // 2 - 2 * rows)))
        packed = jnp.concatenate([placed.reshape(fsdp_count, rows, width // 2), gain_rows], axis=1)
        return [
            spread(scatter_rows(fold(*halves(found.qkv))), False),
            spread(scatter_rows(packed.reshape(fsdp_count * (rows + 16), width // 2)), True),
            spread(scatter_rows(fold(*halves(found.up))), False),
            spread(scatter_rows(fold(*halves(found.down))), True),
        ]

    inputs = own_rows(tokens)
    of0, of1 = types.SimpleNamespace(), types.SimpleNamespace()
    state = types.SimpleNamespace(out_grads=own_rows(cotangent))
    if even:

        def hook_forward0(point, value):
            if point == ATTEND1:
                value, state.out_grads = sync(value, state.out_grads)
            elif point == NORM:
                value, up = sync(value, up_gathered[0])
                weights[0].up = with_far(up)
            elif point == FEED0:
                value, down = sync(value, down_gathered[0])
                weights[0].down = with_far(down)
            elif point == FEED1:
                value, packed = sync(value, packed_gathered)
                near = packed.reshape(4, rows + 16, 4 * LANES)[:, :rows, : 3 * LANES]
                far = swap_y(near.reshape(4 * rows, 3 * LANES))
                qkv, columns, gains[1] = place([packed], [far], depth_array, True)
                weights[1].qkv, weights[1].out = qkv, out_from_columns(columns)
            return value

        def hook_forward1(point, value):
            if point == ATTEND0:
                value, weights[1].out, up = sync(value, weights[1].out, up_gathered[1])
                weights[1].up = with_far(up)
            elif point == NORM:
                value, far, down = sync(value, weights[1].up[1], down_gathered[1])
                weights[1].up = weights[1].up[0], far
                weights[1].down = with_far(down)
            return value

        def hook_backward1(point, value, *grads):
            if point == NORM:
                value, *down = sync(value, *grads[0])
                of1.down = halves(down)
            elif point == ATTEND0:
                value, *up = sync(value, *grads[0])
                of1.up_grads = up
            elif point == ATTEND1:
                value, came, *outputs = sync(value, of1.down[1], *state.away)
                of1.down = scatter_rows(fold(of1.down[0], came))
                of1.up = halves(of1.up_grads)
                state.away = outputs
            elif point == LAST:
                value, came, out, of1.gains = sync(value, of1.up[1], *grads)
                of1.up = scatter_rows(fold(of1.up[0], came))
                of1.out = out_halves(out)
            return value

        def hook_backward0(point, value, *grads):
            if point == FEED0:
                value, down, *qkv = sync(value, of1.down, *of1.qkv)
                of1.qkv = halves(qkv)
                of1.down = spread_start(down, True)
            elif point == FEED1:
                value, came = sync(value, of1.out[1])
                of1.out = out_pair(of1.out[0], came)
            elif point == NORM:
                value, came, cross, up, hop, *down = sync(
                    value, of1.qkv[1], of1.out[1], of1.up, of1.down[1], *grads[0]
                )
                of1.packed = scatter_rows(
                    pack(of1.qkv[0], came, of1.out[0], cross, of1.gains)
                )
                of1.down = of1.down[0], hop
                of1.up = up
                of0.down = halves(down)
            elif point == ATTEND0:
                value, *up = sync(value, *grads[0])
                of0.up_grads = up
            elif point == ATTEND1:
                value, came = sync(value, of0.down[1])
                of0.down = scatter_rows(fold(of0.down[0], came))
                of0.up = halves(of0.up_grads)
                of1.up = spread_start(of1.up, False)
                of1.down = spread_end(of1.down, True)
            elif point == STACKED:
                value, hop, packed, *ends = sync(value, of1.up[1], of1.packed, *of1.down)
                of1.up = of1.up[0], hop
                of1.down = ends
                of1.packed = spread_start(packed, False)
            elif point == LAST:
                value, came, hop, down, away, out, of0.gains = sync(
                    value, of0.up[1], of1.packed[1], of0.down, state.in_away, *grads
                )
                of0.up = scatter_rows(fold(of0.up[0], came))
                of0.out = out_halves(out)
                of1.packed = of1.packed[0], hop
                of0.down = spread_start(down, True)
                of1.up = spread_end(of1.up, False)
                state.in_away = away
            return value

    else:

        def hook_forward0(point, value):
            return value

        hook_forward1 = hook_forward0

        def hook_plain(found):
            def hook(point, value, *grads):
                if point == NORM:
                    found.down = grads[0]
                elif point == ATTEND0:
                    found.up = grads[0]
                elif point == LAST:
                    found.out, found.gains = grads
                return value

            return hook

        hook_backward0, hook_backward1 = hook_plain(of0), hook_plain(of1)

    hidden0, saved0 = forward(inputs, 0, hook_forward0)
    hidden1, saved1 = forward(hidden0, 1, hook_forward1)
    state.away = [swap_y(hidden0[half:]), swap_y(hidden1[half:])]
    in_grads1, of1.qkv = backward(state.out_grads, saved1, 1, hook_backward1)
    state.in_away = swap_y(in_grads1[half:])
    in_grads0, of0.qkv = backward(in_grads1, saved0, 0, hook_backward0)
    if even:
        near, came = of0.out
        qkv_near, qkv_came = halves(of0.qkv)
        packed0 = pack(qkv_near, qkv_came, *out_pair(near, came), of0.gains)
        packed0 = scatter_rows(packed0)
        near1 = [spread_end(of1.packed, False), of1.up, of1.down]
        near0 = [
            spread(packed0, False),
            spread(of0.up, False),
            spread_end(of0.down, True),
        ]
    else:
        near1, near0 = reduce_plain(of1), reduce_plain(of0)

    def to_owner(layer0, layer1, away):
        pairs = [jnp.stack([runs[:half], far]) for runs, far in zip((layer0, layer1), away)]
        keep = jnp.where(first_core, pairs[0], pairs[1])
        take = swap_core(jnp.where(first_core, pairs[1], pairs[0]))
        both = flipped(~first_core, jnp.stack([keep, take], axis=1), 1)
        return flipped(~first_y, both, 0).reshape(2, block, width)

    hidden_out = to_owner(hidden0, hidden1, state.away)
    in_grads_out = to_owner(in_grads0, in_grads1, [swap_y(in_grads0[half:]), state.in_away])

    def natural(position):
        layers = jnp.stack(near0[position]), jnp.stack(near1[position])
        near = jnp.where(first_core, layers[0], layers[1])
        far = jnp.where(first_core, swap_core(layers[0]), swap_core(layers[1]))
        both = jnp.stack([near, far], axis=1)
        shape = both.shape
        both = both.reshape((2, 2, 2) + shape[2:])
        both = flipped(~first_y, flipped(~first_x, flipped(~first_core, both, 2), 1), 0)
        return both.reshape((8,) + shape[2:])

    rows_old = (row_qkv, row_out, row_up, row_down)
    if even:
        where = jnp.stack([at_eighth, core]).astype(jnp.int32)

        def build(position, kind, olds, shapes):
            return assemble(
                near0[position],
                near1[position],
                [swap_core(value) for value in near0[position]],
                [swap_core(value) for value in near1[position]],
                olds,
                where,
                kind,
                shapes,
            )

        def column(row):
            return row.reshape(-1, 1)

        down = build(2, ROWS, [column(row_down)], ((8 * unit, width),))
        up = build(1, COLUMNS, [column(row_up)], ((rows, hidden_width),))
        built = [None, None, up[:2], down[:2]]
        sums = {2: jnp.concatenate([up[2], down[2]], axis=1)}
        places = {2: (0, LANES), 3: (LANES + 2 * hidden_width, 2 * LANES + 2 * hidden_width)}
        places.update({0: (0, LANES), 1: (1, LANES + 6 * width)})

        def build_first(*tokens):
            first = build(
                0,
                PACKED,
                [after(column(row_qkv), *tokens), column(row_out)],
                ((rows, 3 * width), (rows, width)),
            )
            built[:2] = (first[0], first[2]), (first[1], first[3])
            sums[0] = first[5]
            return first[4].reshape(2, rows)

    else:
        qkv = natural(0).reshape(8, rows, 3, LANES).transpose(1, 2, 0, 3).reshape(rows, 3 * width)
        out = natural(1).reshape(2, 4, rows + 16, width // 2).astype(f32).sum(axis=1)
        gain_shard = out[:, rows].sum(axis=0)[: 2 * rows].reshape(2, rows)
        out = out[:, :rows].transpose(1, 0, 2).reshape(rows, width)
        up = natural(2).reshape(8, rows, fsdp_count, unit).transpose(1, 2, 0, 3)
        up = up.reshape(rows, hidden_width)
        down = natural(3).reshape(8 * unit, width)
        built, parts = [], []
        for gradient, row_old in zip((qkv, out, up, down), rows_old):
            gradient = gradient.astype(f32)
            square = gradient * gradient
            row_new = decay_rate * row_old.reshape(-1, 1) + (1.0 - decay_rate) * jnp.mean(
                square, axis=1, keepdims=True
            )
            built.append((gradient, row_new))
            total_new = jnp.pad(jnp.sum(row_new).reshape(1, 1), ((0, 0), (0, LANES - 1)))
            parts.append(
                [
                    total_new,
                    jnp.sum(square, axis=0, keepdims=True),
                    jnp.sum(square / row_new, axis=0, keepdims=True),
                ]
            )
        blank = jnp.zeros_like(parts[0][0])
        sums = {
            2: jnp.concatenate(parts[2] + parts[3], axis=1),
            0: jnp.concatenate([blank] + parts[0] + parts[1], axis=1),
        }
        places = {2: (0, LANES), 3: (LANES + 2 * hidden_width, 2 * LANES + 2 * hidden_width)}
        places.update(
            {0: (LANES, 2 * LANES), 1: (2 * LANES + 6 * width, 3 * LANES + 6 * width)}
        )

        def build_first(*tokens):
            return gain_shard

    def sum_line(value):
        if fsdp_count != 4:
            return lax.psum(value, FSDP)
        near, two, three = rotations(value)[1:]
        return (value + two) + (near + three)

    masters = (w_qkv[0], w_out[0], w_up[0], w_down[0])
    cols_old = (col_qkv, col_out, col_up, col_down)
    gain_masters = (gain_attn, gain_mlp)
    moments_old = (var_attn, var_mlp)

    def total(value):
        return jnp.sum(value).reshape(1, 1)

    new_rows, new_cols, ratios, new_masters = [None] * 4, [None] * 4, [None] * 4, [None] * 4

    def update(position, summed, weight_total):
        gradient, row_new = built[position]
        at_total, start = places[position]
        cols = gradient.shape[1]
        row_count = gradient.shape[0] * fsdp_count
        entry_count = row_count * cols
        col_all = summed[:, start : start + cols]
        ratio_all = summed[:, start + cols : start + 2 * cols]
        row_mean = summed[:, at_total : at_total + 1] / row_count
        new_rows[position] = row_new.reshape(1, -1)
        new_cols[position] = (
            decay_rate * cols_old[position] + (1.0 - decay_rate) * col_all / row_count
        )
        ratios[position] = jnp.sqrt(
            row_mean * total(ratio_all / new_cols[position]) / entry_count
        )
        weight_scale = jnp.sqrt(weight_total / entry_count + weight_eps)
        factor = step_rate * weight_scale / jnp.maximum(1.0, ratios[position] / clip_level)
        raw = gradient * lax.rsqrt(row_new * new_cols[position] / row_mean)
        new_masters[position] = masters[position] - factor * raw

    def lanes(values, start):
        lane = lax.broadcasted_iota(jnp.int32, (1, LANES), 1)
        return sum(jnp.where(lane == start + i, value, 0.0) for i, value in enumerate(values))

    def with_lanes(row, values):
        return jnp.concatenate([row[:, :LANES] + lanes(values, 2), row[:, LANES:]], axis=1)

    weight_totals = [total(master * master) for master in masters + gain_masters]
    summed = sum_line(with_lanes(sums[2], weight_totals))
    weight_all = [summed[:, 2 + i : 3 + i] for i in range(6)]
    for position in (2, 3):
        update(position, summed, weight_all[position])
    gain_shard = build_first(new_masters[2], new_masters[3])
    moments, gain_updates = [], []
    for gain_pos in range(2):
        grad = gain_shard[gain_pos : gain_pos + 1]
        moment = decay_rate * moments_old[gain_pos] + (1.0 - decay_rate) * grad * grad
        moments.append(moment)
        gain_updates.append(grad * lax.rsqrt(moment))
    summed = sum_line(with_lanes(sums[0], [total(step * step) for step in gain_updates]))
    for position in (0, 1):
        update(position, summed, weight_all[position])
    for gain_pos in range(2):
        clip_ratio = jnp.sqrt(summed[:, 2 + gain_pos : 3 + gain_pos] / width)
        weight_scale = jnp.sqrt(weight_all[4 + gain_pos] / width + weight_eps)
        factor = step_rate * weight_scale / jnp.maximum(1.0, clip_ratio / clip_level)
        new_masters.append(gain_masters[gain_pos] - factor * gain_updates[gain_pos])
        ratios.append(clip_ratio)
    return (
        hidden_out[None],
        in_grads_out[None],
        *[entry[0][None] for entry in built],
        gain_shard[:1],
        gain_shard[1:],
        *[master[None] for master in new_masters[:4]],
        new_masters[4],
        new_masters[5],
        new_rows[0],
        new_cols[0],
        new_rows[1],
        new_cols[1],
        new_rows[2],
        new_cols[2],
        new_rows[3],
        new_cols[3],
        moments[0],
        moments[1],
        jnp.concatenate(ratios, axis=1),
    )


def solution(mesh):
    in_specs = (
        P(FSDP, CTX, None),
        P(FSDP, CTX, None),
        P(FSDP, None),
        P(SECTION, FSDP, None),
        P(SECTION, FSDP, None),
        P(SECTION, FSDP, None),
        P(SECTION, FSDP, None),
        P(SECTION, FSDP),
        P(SECTION, FSDP),
        P(SECTION, FSDP),
        P(SECTION, None),
        P(SECTION, FSDP),
        P(SECTION, None),
        P(SECTION, FSDP),
        P(SECTION, None),
        P(SECTION, FSDP),
        P(SECTION, None),
        P(SECTION, FSDP),
        P(SECTION, FSDP),
    )
    out_specs = (
        P(SECTION, FSDP, CTX, None),
        P(SECTION, FSDP, CTX, None),
        P(SECTION, FSDP, None),
        P(SECTION, FSDP, None),
        P(SECTION, FSDP, None),
        P(SECTION, FSDP, None),
        P(SECTION, FSDP),
        P(SECTION, FSDP),
        P(SECTION, FSDP, None),
        P(SECTION, FSDP, None),
        P(SECTION, FSDP, None),
        P(SECTION, FSDP, None),
        P(SECTION, FSDP),
        P(SECTION, FSDP),
        P(SECTION, FSDP),
        P(SECTION, None),
        P(SECTION, FSDP),
        P(SECTION, None),
        P(SECTION, FSDP),
        P(SECTION, None),
        P(SECTION, FSDP),
        P(SECTION, None),
        P(SECTION, FSDP),
        P(SECTION, FSDP),
        P(SECTION, None),
    )
    return jax.shard_map(
        per_device, mesh=mesh, in_specs=in_specs, out_specs=out_specs, check_vma=False
    )
```

```python
import functools
import types

import jax
import jax.numpy as jnp
from jax import lax
from jax.experimental import pallas as pl
from jax.experimental.pallas import tpu as pltpu
from jax.sharding import PartitionSpec as P

HEADS = 16


decay_rate = 0.5
clip_level = 0.5
step_rate = 1.0
norm_eps = 1e-05
weight_eps = 1e-06
mask_fill = -1e30

bf16 = jnp.bfloat16
f32 = jnp.float32
LANES = 128
SECTION, CTX, FSDP = "section", "ctx", "fsdp"
ROWS, COLUMNS, PACKED = range(3)


def swap_core(value):
    return lax.ppermute(value, SECTION, [(0, 1), (1, 0)])


def swap_x(value):
    return lax.ppermute(value, CTX, [(i, i ^ 1) for i in range(4)])


def swap_y(value):
    return lax.ppermute(value, CTX, [(i, i ^ 2) for i in range(4)])


def dot(left, right):
    return jnp.dot(left, right, preferred_element_type=f32)


def times_transposed(left, right):
    return lax.dot_general(left, right, (((1,), (1,)), ((), ())), preferred_element_type=f32)


def rows_product(left, right):
    return lax.dot_general(left, right, (((0,), (0,)), ((), ())), preferred_element_type=f32)


def after(value, *tokens):
    return lax.optimization_barrier((value, *tokens))[0]


def with_core(value):
    return jnp.concatenate([value, swap_core(value)], axis=0)


def gather_tiles(value):
    return [with_core(value), with_core(swap_x(value))]


def fold_core(partial):
    rows = partial.shape[0] // 2
    partial = partial.astype(bf16)
    return partial[:rows].astype(f32) + swap_core(partial[rows:]).astype(f32)


(SEND, ATTEND0, ATTEND1, STACKED, LAST, NORM, FEED0, FEED1, OUT) = range(9)


def norm_parts(values):
    center = values - jnp.mean(values, axis=-1, keepdims=True)
    spread = jnp.mean(center * center, axis=-1, keepdims=True)
    scale = lax.rsqrt(spread + norm_eps)
    return center * scale, scale


def norm_back(out_grad, unit, scale, gain):
    scaled = out_grad * gain
    mean_scaled = jnp.mean(scaled, axis=-1, keepdims=True)
    mean_unit = jnp.mean(scaled * unit, axis=-1, keepdims=True)
    return scale * (scaled - mean_scaled - unit * mean_unit), jnp.sum(out_grad * unit, axis=0)


def nt(left, right):
    return lax.dot_general(left, right, (((1,), (1,)), ((), ())), preferred_element_type=f32)


def attention_kernel(q_ref, k_ref, v_ref, qid_ref, kid_ref, out_ref, lse_ref, *, scale):
    queries = q_ref[...] * jnp.asarray(scale, bf16)
    keys, values_t = k_ref[...], v_ref[...].T
    same = kid_ref[...] == qid_ref[...]
    first = lax.broadcasted_iota(jnp.int32, queries.shape, 1) < queries.shape[1] // 2
    parts = []
    for head in range(2):
        own = jnp.where(first if head == 0 else ~first, queries, jnp.zeros_like(queries))
        scores = jnp.where(same, nt(keys, own), mask_fill)
        peak = jnp.max(scores, axis=0, keepdims=True)
        weights = jnp.exp(scores - peak)
        total = jnp.sum(weights, axis=0, keepdims=True)
        lse_ref[0, head : head + 1, :] = peak + jnp.log(total)
        parts.append(dot(values_t, weights.astype(bf16)) * (1.0 / total))
    width = values_t.shape[0] // 2
    stacked = jnp.concatenate([parts[0][:width], parts[1][width:]], axis=0)
    out_ref[...] = stacked.T.astype(bf16)


def attention_forward(projected, keys_values, query_ids, key_ids, scale):
    rows, seq_len = projected.shape[0], keys_values.shape[0]
    tile = min(256, rows)
    elems = 4 * rows * seq_len
    return pl.pallas_call(
        functools.partial(attention_kernel, scale=scale),
        grid=(2, rows // tile),
        in_specs=[
            pl.BlockSpec((tile, LANES), lambda p, i: (i, 3 * p)),
            pl.BlockSpec((seq_len, LANES), lambda p, i: (0, 3 * p + 1)),
            pl.BlockSpec((seq_len, LANES), lambda p, i: (0, 3 * p + 2)),
            pl.BlockSpec((1, tile), lambda p, i: (0, i)),
            pl.BlockSpec((seq_len, 1), lambda p, i: (0, 0)),
        ],
        out_specs=[
            pl.BlockSpec((tile, LANES), lambda p, i: (i, p)),
            pl.BlockSpec((1, 2, tile), lambda p, i: (p, 0, i)),
        ],
        out_shape=[
            jax.ShapeDtypeStruct((rows, 2 * LANES), bf16),
            jax.ShapeDtypeStruct((2, 2, rows), f32),
        ],
        compiler_params=pltpu.CompilerParams(vmem_limit_bytes=32 << 20),
        cost_estimate=pl.CostEstimate(
            flops=elems * 4 * 128, bytes_accessed=4 << 20, transcendentals=elems
        ),
    )(projected, keys_values, keys_values, query_ids, key_ids)


def attention_back_kernel(
    q_ref, k_ref, v_ref, g_ref, lse_ref, qid_ref, kid_ref, *refs, scale, last
):
    queries = q_ref[...] * jnp.asarray(scale, bf16)
    keys, values, grads = k_ref[...], v_ref[...], g_ref[...]
    keys_t = keys.T
    same = kid_ref[...] == qid_ref[...]
    first = lax.broadcasted_iota(jnp.int32, queries.shape, 1) < queries.shape[1] // 2
    step = pl.program_id(1)
    if last:
        early_q, early_k, early_v, out_ref, dk_ref, dv_ref = refs
    else:
        dq_ref, dk_ref, dv_ref = refs

    @pl.when(step == 0)
    def _():
        dk_ref[...] = early_k[...] if last else jnp.zeros_like(dk_ref)
        dv_ref[...] = early_v[...] if last else jnp.zeros_like(dv_ref)

    parts = []
    for head in range(2):
        mine = first if head == 0 else ~first
        own = jnp.where(mine, queries, jnp.zeros_like(queries))
        own_grads = jnp.where(mine, grads, jnp.zeros_like(grads))
        scores = jnp.where(same, nt(keys, own), mask_fill)
        weights = jnp.exp(scores - lse_ref[0, head : head + 1, :])
        prob_grad = nt(values, own_grads)
        row_dot = jnp.sum(weights * prob_grad, axis=0, keepdims=True)
        score_grad = (weights * (prob_grad - row_dot)).astype(bf16)
        dv_ref[...] += dot(weights.astype(bf16), own_grads)
        dk_ref[...] += dot(score_grad, own)
        parts.append(dot(keys_t, score_grad))
    width = keys_t.shape[0] // 2
    stacked = jnp.concatenate([parts[0][:width], parts[1][width:]], axis=0)
    query_grad = (stacked.T * scale).astype(bf16)
    if not last:
        dq_ref[...] = query_grad
        return
    early, tile = early_q.shape[0], query_grad.shape[0]
    start = pl.multiple_of(early + step * tile, tile)
    out_ref[pl.ds(start, tile), :LANES] = query_grad

    @pl.when(step == pl.num_programs(1) - 1)
    def _():
        out_ref[:early, :LANES] = early_q[...]
        out_ref[:, LANES : 2 * LANES] = dk_ref[...].astype(bf16)
        out_ref[:, 2 * LANES :] = dv_ref[...].astype(bf16)


def attention_backward(projected, keys_values, grads, lse, query_ids, key_ids, scale, early=None):
    rows, seq_len = projected.shape[0], keys_values.shape[0]
    tile = min(256, rows)
    elems = 4 * rows * seq_len

    def column(size):
        return pl.BlockSpec((size, LANES), lambda p, i: (0, p))

    in_specs = [
        pl.BlockSpec((tile, LANES), lambda p, i: (i, 3 * p)),
        pl.BlockSpec((seq_len, LANES), lambda p, i: (0, 3 * p + 1)),
        pl.BlockSpec((seq_len, LANES), lambda p, i: (0, 3 * p + 2)),
        pl.BlockSpec((tile, LANES), lambda p, i: (i, p)),
        pl.BlockSpec((1, 2, tile), lambda p, i: (p, 0, i)),
        pl.BlockSpec((1, tile), lambda p, i: (0, i)),
        pl.BlockSpec((seq_len, 1), lambda p, i: (0, 0)),
    ]
    if early is None:
        out_specs = [pl.BlockSpec((tile, LANES), lambda p, i: (i, p))] + [column(seq_len)] * 2
        out_shape = [
            jax.ShapeDtypeStruct((rows, 2 * LANES), bf16),
            jax.ShapeDtypeStruct((seq_len, 2 * LANES), f32),
            jax.ShapeDtypeStruct((seq_len, 2 * LANES), f32),
        ]
        scratch = []
    else:
        in_specs += [column(early[0].shape[0]), column(seq_len), column(seq_len)]
        out_specs = pl.BlockSpec((seq_len, 3 * LANES), lambda p, i: (0, p))
        out_shape = jax.ShapeDtypeStruct((seq_len, 6 * LANES), bf16)
        scratch = [pltpu.VMEM((seq_len, LANES), f32)] * 2
    return pl.pallas_call(
        functools.partial(attention_back_kernel, scale=scale, last=early is not None),
        grid=(2, rows // tile),
        in_specs=in_specs,
        out_specs=out_specs,
        out_shape=out_shape,
        scratch_shapes=scratch,
        compiler_params=pltpu.CompilerParams(vmem_limit_bytes=32 << 20),
        cost_estimate=pl.CostEstimate(
            flops=elems * 10 * 128, bytes_accessed=6 << 20, transcendentals=elems
        ),
    )(projected, keys_values, keys_values, grads, lse, query_ids, key_ids, *(early or ()))


def weight_grad_kernel(*refs, lefts, rights):
    outs = refs[-lefts * rights :]
    for i in range(lefts):
        turned = [refs[2 * i + k][...].T for k in range(2)]
        for j in range(rights):
            at = 2 * lefts + 2 * j
            total = dot(turned[0], refs[at][...]) + dot(turned[1], refs[at + 1][...])
            outs[i * rights + j][...] = total.astype(bf16)


def weight_grad(lefts, rights):
    size = lefts[0][0].shape[1]
    depth = lefts[0][0].shape[0]
    tile = min(256, size)
    operands, specs, outs = [], [], []
    for pair in lefts:
        for value in pair:
            operands.append(value)
            specs.append(pl.BlockSpec((depth, tile), lambda i: (0, i)))
    for pair, cols, at in rights:
        for value, row in pair:
            operands.append(value)
            specs.append(pl.BlockSpec((depth, cols), lambda i, row=row, at=at: (row, at)))
    for _ in lefts:
        outs += [jax.ShapeDtypeStruct((size, cols), bf16) for _, cols, _ in rights]
    columns = sum(cols for _, cols, _ in rights)
    return pl.pallas_call(
        functools.partial(weight_grad_kernel, lefts=len(lefts), rights=len(rights)),
        grid=(size // tile,),
        in_specs=specs,
        out_specs=[pl.BlockSpec((tile, out.shape[1]), lambda i: (i, 0)) for out in outs],
        out_shape=outs,
        compiler_params=pltpu.CompilerParams(vmem_limit_bytes=32 << 20),
        cost_estimate=pl.CostEstimate(
            flops=4 * depth * size * len(lefts) * columns,
            bytes_accessed=4 * depth * (size * len(lefts) + columns),
            transcendentals=0,
        ),
    )(*operands)


def whole(shape):
    return pl.BlockSpec(shape, lambda *_: (0,) * len(shape))


def cut_kernel(_, *refs, width):
    first, up, down = refs[:16], refs[16:24], refs[24:26]
    packed, far, ups, downs = refs[26:28], refs[28:30], refs[30:32], refs[32:34]
    rows = first[0].shape[1]
    for core in range(2):
        for i in range(3):
            lanes = slice(LANES * i, LANES * (i + 1))
            packed[core][:rows, lanes] = first[3 * core + i][0].astype(bf16)
            far[core][:, lanes] = first[6 + 3 * core + i][0].astype(bf16)
        out = first[12 + core][0].astype(bf16)
        packed[core][:LANES, 3 * LANES :] = out[:, :LANES]
        packed[core][LANES:rows, 3 * LANES :] = out[:, LANES:]
        gains = jnp.concatenate([first[14][...], first[15][...]], axis=1)
        top = lax.broadcasted_iota(jnp.int32, (16, 2 * rows), 0) == 0
        gains = jnp.where(top, jnp.broadcast_to(gains, (16, 2 * rows)), 0.0)
        packed[core][rows:, :] = gains.astype(bf16)
        for i in range(4):
            ups[core][:, LANES * i : LANES * (i + 1)] = up[4 * core + i][0].astype(bf16)
        downs[core][...] = down[core][0].astype(bf16)


def cut_weights(w_qkv, w_out, w_up, w_down, gain_attn, gain_mlp, at_eighth):
    rows, width = w_qkv.shape[1], w_out.shape[2]

    def column(i, flip):
        return pl.BlockSpec((1, rows, LANES), lambda g, at: (0, 0, 8 * i + (at[0] ^ flip)))

    specs = [column(i, flip) for flip in (0, 1, 4, 5) for i in range(3)]
    specs += [
        pl.BlockSpec(
            (1, LANES, 2 * LANES), lambda g, at, c=core: (0, (at[0] & 1) ^ c, at[0] >> 1)
        )
        for core in range(2)
    ]
    specs += [whole(gain_attn.shape), whole(gain_mlp.shape)]
    specs += [column(i, core) for core in range(2) for i in range(4)]
    specs += [
        pl.BlockSpec((1, LANES, width), lambda g, at, c=core: (0, at[0] ^ c, 0))
        for core in range(2)
    ]
    outs = [
        jax.ShapeDtypeStruct(shape, bf16)
        for shape in (
            (rows + 16, 4 * LANES),
            (rows, 3 * LANES),
            (rows, 4 * LANES),
            (LANES, width),
        )
        for _ in range(2)
    ]
    operands = [w_qkv] * 12 + [w_out] * 2 + [gain_attn, gain_mlp] + [w_up] * 8 + [w_down] * 2
    return pl.pallas_call(
        functools.partial(cut_kernel, width=width),
        grid_spec=pltpu.PrefetchScalarGridSpec(
            num_scalar_prefetch=1,
            grid=(1,),
            in_specs=specs,
            out_specs=[whole(out.shape) for out in outs],
        ),
        out_shape=outs,
        compiler_params=pltpu.CompilerParams(vmem_limit_bytes=56 << 20),
    )(at_eighth, *operands)


def place_qkv_kernel(at, *refs, fixed):
    out_ref = refs[-1]
    rows, cols = refs[4].shape
    for k in range(4):
        slot = k if fixed else lax.rem(at[0] + 4 - k, 4)
        part = pl.ds(pl.multiple_of(slot * rows, rows), rows)
        out_ref[part, :cols] = refs[k][:rows, :cols]
        out_ref[part, cols:] = refs[4 + k][...]


def place_out_kernel(at, *refs, fixed):
    out_ref, gain_ref = refs[-2:]
    rows, cols = refs[0].shape[0] - 16, refs[0].shape[1] - LANES
    for k in range(4):
        slot = k if fixed else lax.rem(at[0] + 4 - k, 4)
        packed = refs[k]
        away = slot ^ at[1]
        away = 2 * (away & 1) + (away >> 1)
        out_ref[away, :, :LANES] = packed[:LANES, cols:]
        out_ref[away, :, LANES:] = packed[LANES:rows, cols:]
        part = pl.ds(pl.multiple_of(slot * rows, rows), rows)
        gains = packed[rows:, :].astype(f32)
        gain_ref[0:1, part] = gains[0:1, :rows]
        gain_ref[1:2, part] = gains[0:1, rows:]


def place(kernel, operands, shapes, outs, at, fixed):
    specs = [
        pl.BlockSpec(shape, (lambda g, at, k=k: (k, 0)) if fixed else (lambda g, at: (0, 0)))
        for shape in shapes
        for k in range(4)
    ]
    if fixed:
        operands = [value for value in operands for _ in range(4)]
    return pl.pallas_call(
        functools.partial(kernel, fixed=fixed),
        grid_spec=pltpu.PrefetchScalarGridSpec(
            num_scalar_prefetch=1,
            grid=(1,),
            in_specs=specs,
            out_specs=[whole(out.shape) for out in outs],
        ),
        out_shape=outs,
        compiler_params=pltpu.CompilerParams(vmem_limit_bytes=24 << 20),
    )(at, *operands)


def small_call(kernel, at, operands, outs, room=40):
    return pl.pallas_call(
        kernel,
        grid_spec=pltpu.PrefetchScalarGridSpec(
            num_scalar_prefetch=1,
            grid=(1,),
            in_specs=[whole(value.shape) for value in operands],
            out_specs=[whole(out.shape) for out in outs],
        ),
        out_shape=outs,
        compiler_params=pltpu.CompilerParams(vmem_limit_bytes=room << 20),
    )(at, *operands)


def join_out_kernel(at, keep, came, far_keep, far_came, out_ref):
    for b in range(2):
        rows = slice(LANES * b, LANES * (b + 1))
        for away, value in enumerate((keep[b], came[b], far_keep[1 - b], far_came[1 - b])):
            size = value.shape[1]
            start = pl.multiple_of((at[0] ^ away) * size, size)
            out_ref[rows, pl.ds(start, size)] = value


def fold_out_kernel(at, keep, came, near_ref, give_ref):
    size = near_ref.shape[2]
    first_x = (at[0] & 1) == 0
    for b in range(2):
        value = keep[b].astype(f32) + came[1 - b].astype(f32)
        low, high = value[:, :size], value[:, size:]
        near_ref[b] = jnp.where(first_x, low, high).astype(bf16)
        give_ref[b] = jnp.where(first_x, high, low).astype(bf16)


def pack_kernel(at, keep, came, near, cross, gains, out_ref):
    cols = keep.shape[1]
    rows = keep.shape[0] // 4
    top = lax.broadcasted_iota(jnp.int32, (16, 2 * rows), 0) == 0
    for f in range(4):
        base = f * (rows + 16)
        part = slice(rows * f, rows * (f + 1))
        out_ref[base : base + rows, :cols] = (
            keep[part, :].astype(f32) + came[part, :].astype(f32)
        ).astype(bf16)
        gain = jnp.concatenate([gains[0:1, part], gains[1:2, part]], axis=1)
        gain = jnp.where(top, jnp.broadcast_to(gain, (16, 2 * rows)), 0.0)
        out_ref[base + rows : base + rows + 16, :] = gain.astype(bf16)
    for away, value in enumerate((near[0], cross[0], near[1], cross[1])):
        base = (at[0] ^ away) * (rows + 16)
        for half in range(2):
            start = pl.multiple_of(base + LANES * half, 16)
            out_ref[pl.ds(start, LANES), cols:] = value[:, LANES * half : LANES * (half + 1)]


def assemble_kernel(at, *refs, kind, shapes):
    groups = [refs[4 * i : 4 * i + 4] for i in range(4)]
    rows_old = refs[16 : 16 + len(shapes)]
    extra = refs[16 + len(shapes)]
    outs = refs[17 + len(shapes) :]
    grads, rows_new, sums_ref = outs[: len(shapes)], outs[len(shapes) : 2 * len(shapes)], outs[-1]
    first_core = at[1] == 0
    gain = 0.0
    for core in range(2):
        for chip in range(4):
            eighth = (2 * chip + core) ^ at[0]
            value = jnp.where(first_core, groups[core][chip][...], groups[2 + core][chip][...])
            value = value.astype(f32)
            if kind == ROWS:
                rows = value.shape[0]
                grads[0][pl.ds(pl.multiple_of(eighth * rows, rows), rows), :] = value
            elif kind == COLUMNS:
                for i in range(value.shape[1] // LANES):
                    start = pl.multiple_of((8 * i + eighth) * LANES, LANES)
                    grads[0][:, pl.ds(start, LANES)] = value[:, LANES * i : LANES * (i + 1)]
            else:
                rows = shapes[0][0]
                for i in range(3):
                    start = pl.multiple_of((8 * i + eighth) * LANES, LANES)
                    grads[0][:, pl.ds(start, LANES)] = value[:rows, LANES * i : LANES * (i + 1)]
                part = pl.ds(pl.multiple_of((eighth & 1) * LANES, LANES), LANES)
                for half in range(2):
                    start = pl.multiple_of((2 * (eighth >> 1) + half) * LANES, LANES)
                    block = value[half * LANES : (half + 1) * LANES, 3 * LANES :]
                    grads[1][part, pl.ds(start, LANES)] = block
                gain = gain + value[rows : rows + 1, :]
    lane = lax.broadcasted_iota(jnp.int32, (1, LANES), 1)
    sums_ref[...] = jnp.zeros_like(sums_ref)
    if kind == PACKED:
        outs[-2][...] = gain
        moment = decay_rate * extra[...] + (1.0 - decay_rate) * gain * gain
        square = (gain * lax.rsqrt(moment)) ** 2
        middle = square.shape[1] // 2
        attn_total = jnp.sum(square[:, :middle], axis=1, keepdims=True)
        mlp_total = jnp.sum(square[:, middle:], axis=1, keepdims=True)
        sums_ref[:, :LANES] = jnp.where(lane == 2, attn_total, jnp.where(lane == 3, mlp_total, 0.0))
    else:
        sums_ref[:, :LANES] = extra[...]
    begin = LANES
    for index, (total_rows, cols) in enumerate(shapes):
        grad_ref, row_ref, new_ref = grads[index], rows_old[index], rows_new[index]
        col_part = slice(begin, begin + cols)
        ratio_part = slice(begin + cols, begin + 2 * cols)
        begin += 2 * cols

        def body(i, total):
            part = pl.ds(pl.multiple_of(i * 64, 64), 64)
            values = grad_ref[part, :]
            square = values * values
            row_new = decay_rate * row_ref[part, :] + (1.0 - decay_rate) * (
                jnp.sum(square, axis=1, keepdims=True) / cols
            )
            new_ref[part, :] = row_new
            sums_ref[:, col_part] += jnp.sum(square, axis=0, keepdims=True)
            sums_ref[:, ratio_part] += jnp.sum(square * (1.0 / row_new), axis=0, keepdims=True)
            return total + jnp.sum(row_new, axis=0, keepdims=True)

        total = lax.fori_loop(0, total_rows // 64, body, jnp.zeros((1, 1), f32))
        sums_ref[:, :LANES] += jnp.where(lane == index, total, 0.0)


def assemble(near0, near1, far0, far1, rows_old, extra, where, kind, shapes):
    outs = [jax.ShapeDtypeStruct(shape, f32) for shape in shapes]
    outs += [jax.ShapeDtypeStruct((shape[0], 1), f32) for shape in shapes]
    if kind == PACKED:
        outs.append(jax.ShapeDtypeStruct((1, near0[0].shape[1]), f32))
    outs.append(
        jax.ShapeDtypeStruct((1, LANES + 2 * sum(shape[1] for shape in shapes)), f32)
    )
    return small_call(
        functools.partial(assemble_kernel, kind=kind, shapes=shapes),
        where,
        [*near0, *far0, *near1, *far1, *rows_old, extra],
        outs,
        56,
    )


def per_device(
    tokens,
    cotangent,
    segment_ids,
    w_qkv,
    w_out,
    w_up,
    w_down,
    gain_attn,
    gain_mlp,
    row_qkv,
    col_qkv,
    row_out,
    col_out,
    row_up,
    col_up,
    row_down,
    col_down,
    var_attn,
    var_mlp,
):
    core = lax.axis_index(SECTION)
    chip = lax.axis_index(CTX)
    depth = lax.axis_index(FSDP)
    y, x = chip // 2, chip % 2
    fsdp_count = lax.axis_size(FSDP)
    assert lax.axis_size(SECTION) == 2 and lax.axis_size(CTX) == 4
    _, block, width = tokens.shape
    half = block // 2
    rows = w_qkv.shape[1]
    hidden_width = w_up.shape[2]
    unit = hidden_width // fsdp_count // 8
    scale = (width // HEADS) ** (-0.5)
    even = fsdp_count == 4 and rows == 2 * LANES and unit == LANES
    first_core, first_y, first_x = core == 0, y == 0, x == 0

    def flipped(when, value, axis=0):
        low, high = jnp.split(value, 2, axis)
        return jnp.where(when, jnp.concatenate([high, low], axis), value)

    at_eighth = 2 * chip + core

    def eighth(e):
        qkv = lax.dynamic_index_in_dim(w_qkv[0].reshape(rows, 3, 8, LANES), e, 2, keepdims=False)
        up = lax.dynamic_index_in_dim(
            w_up[0].reshape(rows, fsdp_count, 8, unit), e, 2, keepdims=False
        )
        down = lax.dynamic_slice_in_dim(w_down[0], e * unit, unit, 0)
        return [
            part.astype(bf16)
            for part in (qkv.reshape(rows, 3 * LANES), up.reshape(rows, fsdp_count * unit), down)
        ]

    def by_layer(mine, other):
        taken = swap_core(other)
        return jnp.where(first_core, mine, taken), jnp.where(first_core, taken, mine)

    def gather_rows(value):
        return lax.all_gather(value, FSDP, axis=0, tiled=True)

    def rotations(value):
        return [value] + [
            lax.ppermute(
                value, FSDP, [(i, (i + k) % fsdp_count) for i in range(fsdp_count)]
            )
            for k in range(1, fsdp_count)
        ]

    def with_far(value):
        return value, swap_y(value)

    chip_array = chip.reshape(1).astype(jnp.int32)

    def out_parts(columns):
        keep, came = columns[:2], swap_x(columns[2:])
        return [keep, came, swap_y(keep), swap_y(came)]

    def join_out(parts):
        out = jax.ShapeDtypeStruct((2 * LANES, width), bf16)
        return small_call(join_out_kernel, chip_array, parts, [out])[0]

    weights, gains = [types.SimpleNamespace(), types.SimpleNamespace()], [None, None]
    depth_array = jnp.stack([depth, chip]).astype(jnp.int32)
    if even:
        cuts = cut_weights(
            w_qkv, w_out, w_up, w_down, gain_attn, gain_mlp, at_eighth.reshape(1).astype(jnp.int32)
        )
        packed_parts = by_layer(*cuts[:2])
        far_parts = by_layer(*cuts[2:4])
        up_parts = by_layer(*cuts[4:6])
        down_parts = by_layer(*cuts[6:])
        turns = rotations(packed_parts[0])
        fars = [swap_y(value[:rows, : 3 * LANES]) for value in turns[1:]]

        def place_qkv(packed, far, fixed):
            shapes = ((rows + 16, 4 * LANES), (rows, 3 * LANES))
            out = jax.ShapeDtypeStruct((4 * rows, 6 * LANES), bf16)
            return place(place_qkv_kernel, [*packed, *far], shapes, [out], depth_array, fixed)[0]

        def place_out(packed, fixed):
            outs = [
                jax.ShapeDtypeStruct((4, LANES, 2 * LANES), bf16),
                jax.ShapeDtypeStruct((2, 4 * rows), f32),
            ]
            shapes = ((rows + 16, 4 * LANES),)
            columns, gain = place(place_out_kernel, packed, shapes, outs, depth_array, fixed)
            return out_parts(columns), gain

        weights[0].qkv = place_qkv(turns, [far_parts[0]] + fars, False)
        weights[0].out, gains[0] = place_out(turns, False)
        up_gathered = [gather_rows(after(up_parts[0], *turns[1:])), gather_rows(up_parts[1])]
        down_gathered = [gather_rows(after(down_parts[0], *turns[1:])), gather_rows(down_parts[1])]
        packed_gathered = gather_rows(packed_parts[1])
    else:
        mine_parts, other_parts = eighth(at_eighth), eighth(at_eighth ^ 1)
        qkv_parts, up_parts, down_parts = [by_layer(a, b) for a, b in zip(mine_parts, other_parts)]
        whole_out = gather_rows(w_out[0].astype(bf16))
        out_parts = by_layer(whole_out, whole_out)
        gains_own = lax.all_gather(
            jnp.concatenate([gain_attn, gain_mlp], axis=0).astype(bf16), FSDP, axis=1, tiled=True
        )
        gains = [part.astype(f32) for part in by_layer(gains_own, gains_own)]
        for layer in range(2):
            blocks = out_parts[layer].reshape(4, 2, LANES, width)
            blocks = lax.dynamic_index_in_dim(blocks, core, 1, keepdims=False)
            weights[layer] = types.SimpleNamespace(
                qkv=jnp.concatenate(with_far(gather_rows(qkv_parts[layer])), axis=1),
                out=jnp.concatenate(
                    [
                        lax.dynamic_index_in_dim(blocks, chip, 0, keepdims=False),
                        lax.dynamic_index_in_dim(blocks, chip ^ 2, 0, keepdims=False),
                    ],
                    axis=0,
                ),
                up=with_far(gather_rows(up_parts[layer])),
                down=with_far(gather_rows(down_parts[layer])),
            )

    def own_rows(value):
        near = lax.dynamic_slice(value, (y, core * half, 0), (1, half, width))[0]
        away = lax.dynamic_slice(value, (1 - y, core * half, 0), (1, half, width))[0]
        return jnp.concatenate([near, swap_y(away)], axis=0)

    ids = lax.dynamic_index_in_dim(segment_ids, y, 0, keepdims=False).reshape(2, 2, 2, half)
    ids = flipped(~first_y, flipped(~first_x, flipped(~first_core, ids, 2), 1), 0)
    ids = ids.transpose(1, 2, 0, 3)
    key_ids = ids.reshape(8 * half, 1)
    query_ids = [ids[k].reshape(1, 4 * half) for k in range(2)]

    def forward(inputs, layer, hook):
        held = weights[layer]
        attn_gain, mlp_gain = gains[layer][0], gains[layer][1]
        inputs_all = gather_tiles(inputs)
        projected = [dot(value, held.qkv).astype(bf16) for value in inputs_all]
        keys_values = jnp.concatenate(projected, axis=0)

        def attend(k, queries):
            context, lse = attention_forward(queries, keys_values, query_ids[k], key_ids, scale)
            context = hook(OUT, context) if k == 1 else context
            return context, lse, fold_core(dot(context, held.out))

        context1, lse1, across = attend(1, hook(ATTEND0, projected[1]))
        across = across.astype(bf16)
        context0, lse0, keep = attend(0, hook(ATTEND1, after(projected[0], across)))
        came = hook(NORM, after(swap_x(across), keep))
        unit_attn, scale_attn = norm_parts(inputs.astype(f32) + keep + came.astype(f32))
        normed = unit_attn * attn_gain
        normed_all = gather_tiles(normed.astype(bf16))

        def feed(value):
            activated, slope, partial = [], [], 0.0
            for half_up, half_down in zip(held.up, held.down):
                upward = dot(value, half_up)
                phi_whole = 0.5 * (1.0 + lax.erf(upward * (0.5**0.5)))
                activated.append((upward * phi_whole).astype(bf16))
                density = jnp.exp(-0.5 * upward * upward) * 0.3989422804014327
                slope.append((phi_whole + upward * density).astype(bf16))
                partial += dot(activated[-1], half_down)
            return activated, slope, fold_core(partial)

        activated0, slope0, keep = feed(hook(FEED0, normed_all[0]))
        activated1, slope1, across = feed(hook(FEED1, after(normed_all[1], keep)))
        came = hook(LAST, swap_x(hook(SEND, across.astype(bf16))))
        unit_mlp, scale_mlp = norm_parts(normed + keep + came.astype(f32))
        return (unit_mlp * mlp_gain).astype(bf16), types.SimpleNamespace(
            inputs_all=inputs_all,
            projected=projected,
            keys_values=keys_values,
            context=(context0, context1),
            lse=(lse0, lse1),
            unit_attn=unit_attn,
            scale_attn=scale_attn,
            normed_all=normed_all,
            activated=(activated0, activated1),
            slope=(slope0, slope1),
            unit_mlp=unit_mlp,
            scale_mlp=scale_mlp,
        )

    def backward(out_grads, kept, layer, hook):
        held = weights[layer]
        attn_gain, mlp_gain = gains[layer][0], gains[layer][1]

        def both(pair):
            return [(value, 0) for value in pair]

        mlp_in, mlp_gain_grad = norm_back(
            out_grads.astype(f32), kept.unit_mlp, kept.scale_mlp, mlp_gain
        )
        down_all = gather_tiles(mlp_in.astype(bf16))

        def feed_back(k, value):
            grads, partial = [], 0.0
            for half_up, half_down, slope in zip(held.up, held.down, kept.slope[k]):
                grad = times_transposed(value, half_down) * slope.astype(f32)
                grads.append(grad.astype(bf16))
                partial += times_transposed(grads[-1], half_up)
            return grads, fold_core(partial)

        upward0, keep = feed_back(0, hook(FEED0, down_all[0]))
        upward1, across = feed_back(1, hook(FEED1, after(down_all[1], keep)))
        grad_down = weight_grad(list(zip(*kept.activated)), [(both(down_all), width, 0)])
        came = hook(NORM, swap_x(across.astype(bf16)), grad_down)
        attn_in, attn_gain_grad = norm_back(
            mlp_in + keep + came.astype(f32), kept.unit_attn, kept.scale_attn, attn_gain
        )
        branch_all = gather_tiles(attn_in.astype(bf16))

        def attend_back(k, value, early=None):
            grads = times_transposed(value, held.out).astype(bf16)
            return attention_backward(
                kept.projected[k],
                kept.keys_values,
                grads,
                kept.lse[k],
                query_ids[k],
                key_ids,
                scale,
                early,
            )

        grad_up = weight_grad(
            [kept.normed_all],
            [(both(right), right[0].shape[1], 0) for right in zip(upward0, upward1)],
        )
        early = attend_back(0, hook(ATTEND0, branch_all[0], grad_up))
        stacked = attend_back(1, hook(ATTEND1, after(branch_all[1], early[0])), early)
        gain_grads = jnp.stack([attn_gain_grad, mlp_gain_grad])
        (grad_out,) = weight_grad([kept.context], [(both(branch_all), width, 0)])
        stacked = hook(STACKED, stacked, grad_out, gain_grads)
        tile = 4 * half
        across = fold_core(times_transposed(stacked[tile:], held.qkv)).astype(bf16)
        across = hook(SEND, across)
        keep = fold_core(times_transposed(after(stacked, across)[:tile], held.qkv))
        came = hook(LAST, after(swap_x(across), keep))
        tiles = [(stacked, 0), (stacked, 1)]
        grad_qkv = weight_grad([kept.inputs_all], [(tiles, 3 * LANES, at) for at in range(2)])
        return (attn_in + keep + came.astype(f32)).astype(bf16), grad_qkv

    def scatter_rows(value):
        return lax.psum_scatter(value, FSDP, scatter_dimension=0, tiled=True)

    def sync(value, *others):
        return lax.optimization_barrier((value, *others))

    def fold(keep, came):
        return (keep.astype(f32) + came.astype(f32)).astype(bf16)

    def halves(grad):
        return grad[0], swap_y(grad[1])

    def out_halves(grad_out):
        size = width // 2
        keep = lax.dynamic_slice_in_dim(grad_out, y * size, size, 1)
        give = lax.dynamic_slice_in_dim(grad_out, (1 - y) * size, size, 1)
        return keep.reshape(2, LANES, size), swap_y(give.reshape(2, LANES, size))

    def out_pair(keep, came):
        out = jax.ShapeDtypeStruct((2, LANES, 2 * LANES), bf16)
        near, give = small_call(fold_out_kernel, chip_array, [keep, came], [out, out])
        return near, swap_x(give)

    def pack(keep, came, near, cross, gain_grads):
        out = jax.ShapeDtypeStruct((4 * (rows + 16), 4 * LANES), bf16)
        operands = [keep, came, near, cross, gain_grads]
        return small_call(pack_kernel, chip_array, operands, [out])[0]

    def spread_start(value, y_first):
        return value, (swap_y if y_first else swap_x)(value)

    def spread_end(pair, y_first):
        value, first = pair
        if y_first:
            return [value, swap_x(value), first, swap_x(first)]
        return [value, first, swap_y(value), swap_y(first)]

    def spread(value, y_first):
        return spread_end(spread_start(value, y_first), y_first)

    def reduce_plain(found):
        keep, came = out_halves(found.out)
        both = fold(keep, came[::-1])
        placed = jnp.zeros((4, 2, LANES, width // 2), bf16)
        placed = lax.dynamic_update_slice(placed, both[:1, None], (chip, core, 0, 0))
        placed = lax.dynamic_update_slice(placed, both[1:, None], (chip ^ 2, core, 0, 0))
        gain_rows = found.gains.reshape(2, fsdp_count, rows).transpose(1, 0, 2)
        gain_rows = gain_rows.reshape(fsdp_count, 1, 2 * rows).astype(bf16)
        gain_rows = jnp.pad(gain_rows, ((0, 0), (0, 15), (0, width // 2 - 2 * rows)))
        packed = jnp.concatenate([placed.reshape(fsdp_count, rows, width // 2), gain_rows], axis=1)
        return [
            spread(scatter_rows(fold(*halves(found.qkv))), False),
            spread(scatter_rows(packed.reshape(fsdp_count * (rows + 16), width // 2)), True),
            spread(scatter_rows(fold(*halves(found.up))), False),
            spread(scatter_rows(fold(*halves(found.down))), True),
        ]

    inputs = own_rows(tokens)
    of0, of1 = types.SimpleNamespace(), types.SimpleNamespace()

    def total(value):
        return jnp.sum(value).reshape(1, 1)

    def lanes(values, start):
        lane = lax.broadcasted_iota(jnp.int32, (1, LANES), 1)
        return sum(jnp.where(lane == start + i, value, 0.0) for i, value in enumerate(values))

    def with_lanes(row, values):
        if even:
            return row
        return jnp.concatenate([row[:, :LANES] + values, row[:, LANES:]], axis=1)

    masters = (w_qkv[0], w_out[0], w_up[0], w_down[0])
    gain_masters = (gain_attn, gain_mlp)
    state = types.SimpleNamespace(
        out_grads=own_rows(cotangent),
        weight_totals=lanes([total(master * master) for master in masters + gain_masters], 2),
    )
    if even:

        def hook_forward0(point, value):
            if point == OUT:
                value, up, *parts = sync(value, up_gathered[0], *weights[0].out)
                weights[0].out = join_out(parts)
                weights[0].up = with_far(up)
            elif point == NORM:
                value, far, down = sync(value, weights[0].up[1], down_gathered[0])
                weights[0].up = weights[0].up[0], far
                weights[0].down = with_far(down)
            elif point == FEED0:
                value, far = sync(value, weights[0].down[1])
                weights[0].down = weights[0].down[0], far
            elif point == SEND:
                value, packed = sync(value, packed_gathered)
                near = packed.reshape(4, rows + 16, 4 * LANES)[:, :rows, : 3 * LANES]
                far = swap_y(near.reshape(4 * rows, 3 * LANES))
                weights[1].qkv = place_qkv([packed], [far], True)
                weights[1].out, gains[1] = place_out([packed], True)
            elif point == LAST:
                value, up = sync(value, up_gathered[1])
                weights[1].up = with_far(up)
            return value

        def hook_forward1(point, value):
            if point == OUT:
                value, down, *parts = sync(value, down_gathered[1], *weights[1].out)
                weights[1].out = join_out(parts)
                weights[1].down = with_far(down)
            elif point == NORM:
                value, far = sync(value, weights[1].up[1])
                weights[1].up = weights[1].up[0], far
            elif point == FEED0:
                value, far = sync(value, weights[1].down[1])
                weights[1].down = weights[1].down[0], far
            elif point == LAST:
                value, state.out_grads, state.weight_totals = sync(
                    value, state.out_grads, state.weight_totals
                )
            return value

        def hook_backward1(point, value, *grads):
            if point == NORM:
                value, *down = sync(value, *grads[0])
                of1.down = halves(down)
            elif point == ATTEND0:
                value, *up = sync(value, *grads[0])
                of1.up_grads = up
            elif point == ATTEND1:
                value, *outputs = sync(value, *state.away)
                state.away = outputs
            elif point == STACKED:
                value, came, out, of1.gains = sync(value, of1.down[1], *grads)
                of1.down = scatter_rows(fold(of1.down[0], came))
                of1.up = halves(of1.up_grads)
                of1.out = out
            return value

        def hook_backward0(point, value, *grads):
            if point == FEED0:
                value, came, *qkv = sync(value, of1.up[1], *of1.qkv)
                of1.up = scatter_rows(fold(of1.up[0], came))
                of1.qkv = halves(qkv)
                of1.out = out_halves(of1.out)
            elif point == NORM:
                value, came, out_came, down, *grad_down = sync(
                    value, of1.qkv[1], of1.out[1], of1.down, *grads[0]
                )
                of1.qkv = of1.qkv[0], came
                of1.out = out_pair(of1.out[0], out_came)
                of1.down = spread_start(down, True)
                of0.down = halves(grad_down)
            elif point == ATTEND0:
                value, cross, up, *up_grads = sync(value, of1.out[1], of1.up, *grads[0])
                of1.packed = scatter_rows(pack(*of1.qkv, of1.out[0], cross, of1.gains))
                of1.up = up
                of0.up_grads = up_grads
            elif point == ATTEND1:
                value, came, hop, state.in_away = sync(
                    value, of0.down[1], of1.down[1], state.in_away
                )
                of0.down = scatter_rows(fold(of0.down[0], came))
                of0.up = halves(of0.up_grads)
                of1.up = spread_start(of1.up, False)
                of1.down = spread_end((of1.down[0], hop), True)
            elif point == STACKED:
                value, came, hop, packed, out, of0.gains, *ends = sync(
                    value, of0.up[1], of1.up[1], of1.packed, *grads, *of1.down
                )
                of0.up = scatter_rows(fold(of0.up[0], came))
                of1.up = of1.up[0], hop
                of1.down = ends
                of1.packed = spread_start(packed, False)
                of0.out = out_halves(out)
            elif point == SEND:
                value, out_came, hop = sync(value, of0.out[1], of1.packed[1])
                of0.out = out_pair(of0.out[0], out_came)
                of1.packed = of1.packed[0], hop
            elif point == LAST:
                value, of0.down = sync(value, of0.down)
            return value

    else:

        def hook_forward0(point, value):
            return value

        hook_forward1 = hook_forward0

        def hook_plain(found):
            def hook(point, value, *grads):
                if point == NORM:
                    found.down = grads[0]
                elif point == ATTEND0:
                    found.up = grads[0]
                elif point == STACKED:
                    found.out, found.gains = grads
                return value

            return hook

        hook_backward0, hook_backward1 = hook_plain(of0), hook_plain(of1)

    hidden0, saved0 = forward(inputs, 0, hook_forward0)
    hidden1, saved1 = forward(hidden0, 1, hook_forward1)
    state.away = [swap_y(hidden0[half:]), swap_y(hidden1[half:])]
    in_grads1, of1.qkv = backward(state.out_grads, saved1, 1, hook_backward1)
    state.in_away = swap_y(in_grads1[half:])
    in_grads0, of0.qkv = backward(in_grads1, saved0, 0, hook_backward0)
    if even:
        qkv_near, qkv_came = halves(of0.qkv)
        packed0 = pack(qkv_near, qkv_came, *of0.out, of0.gains)
        packed0, of0.up, of0.down, *rest = sync(
            packed0, of0.up, of0.down, *of1.packed, *of1.up, hidden0, hidden1, in_grads0, in_grads1
        )
        of1.packed, of1.up = rest[:2], rest[2:4]
        hidden0, hidden1, in_grads0, in_grads1 = rest[4:]
        packed0 = scatter_rows(packed0)
        near0 = [None, spread(of0.up, False), spread(of0.down, True)]
        near1 = [spread_end(of1.packed, False), spread_end(of1.up, False), of1.down]
    else:
        near1, near0 = reduce_plain(of1), reduce_plain(of0)

    def to_owner(layer0, layer1, away):
        pairs = [jnp.stack([runs[:half], far]) for runs, far in zip((layer0, layer1), away)]
        keep = jnp.where(first_core, pairs[0], pairs[1])
        take = swap_core(jnp.where(first_core, pairs[1], pairs[0]))
        both = flipped(~first_core, jnp.stack([keep, take], axis=1), 1)
        return flipped(~first_y, both, 0).reshape(2, block, width)

    hidden_out = to_owner(hidden0, hidden1, state.away)
    in_grads_out = to_owner(in_grads0, in_grads1, [swap_y(in_grads0[half:]), state.in_away])

    def natural(position):
        layers = jnp.stack(near0[position]), jnp.stack(near1[position])
        near = jnp.where(first_core, layers[0], layers[1])
        far = jnp.where(first_core, swap_core(layers[0]), swap_core(layers[1]))
        both = jnp.stack([near, far], axis=1)
        shape = both.shape
        both = both.reshape((2, 2, 2) + shape[2:])
        both = flipped(~first_y, flipped(~first_x, flipped(~first_core, both, 2), 1), 0)
        return both.reshape((8,) + shape[2:])

    rows_old = (row_qkv, row_out, row_up, row_down)
    if even:
        where = jnp.stack([at_eighth, core]).astype(jnp.int32)

        def build(position, kind, olds, extra, shapes):
            return assemble(
                near0[position],
                near1[position],
                [swap_core(value) for value in near0[position]],
                [swap_core(value) for value in near1[position]],
                olds,
                extra,
                where,
                kind,
                shapes,
            )

        def column(row):
            return row.reshape(-1, 1)

        down = build(2, ROWS, [column(row_down)], jnp.zeros((1, LANES), f32), ((8 * unit, width),))
        up = build(
            1, COLUMNS, [column(row_up)], state.weight_totals, ((rows, hidden_width),)
        )
        near0[0] = spread(after(packed0, up[1], down[1]), False)
        built = [None, None, up[:2], down[:2]]
        sums = {2: jnp.concatenate([up[2], down[2]], axis=1)}
        places = {2: (0, LANES), 3: (LANES + 2 * hidden_width, 2 * LANES + 2 * hidden_width)}
        places.update({0: (0, LANES), 1: (1, LANES + 6 * width)})

        def build_first():
            first = build(
                0,
                PACKED,
                [after(column(row_qkv), sums[2]), column(row_out)],
                jnp.concatenate([var_attn, var_mlp], axis=1),
                ((rows, 3 * width), (rows, width)),
            )
            built[:2] = (first[0], first[2]), (first[1], first[3])
            sums[0] = first[5]
            return first[4].reshape(2, rows)

    else:
        qkv = natural(0).reshape(8, rows, 3, LANES).transpose(1, 2, 0, 3).reshape(rows, 3 * width)
        out = natural(1).reshape(2, 4, rows + 16, width // 2).astype(f32).sum(axis=1)
        gain_shard = out[:, rows].sum(axis=0)[: 2 * rows].reshape(2, rows)
        out = out[:, :rows].transpose(1, 0, 2).reshape(rows, width)
        up = natural(2).reshape(8, rows, fsdp_count, unit).transpose(1, 2, 0, 3)
        up = up.reshape(rows, hidden_width)
        down = natural(3).reshape(8 * unit, width)
        built, parts = [], []
        for gradient, row_old in zip((qkv, out, up, down), rows_old):
            gradient = gradient.astype(f32)
            square = gradient * gradient
            row_new = decay_rate * row_old.reshape(-1, 1) + (1.0 - decay_rate) * jnp.mean(
                square, axis=1, keepdims=True
            )
            built.append((gradient, row_new))
            total_new = jnp.pad(jnp.sum(row_new).reshape(1, 1), ((0, 0), (0, LANES - 1)))
            parts.append(
                [
                    total_new,
                    jnp.sum(square, axis=0, keepdims=True),
                    jnp.sum(square / row_new, axis=0, keepdims=True),
                ]
            )
        blank = jnp.zeros_like(parts[0][0])
        sums = {
            2: jnp.concatenate(parts[2] + parts[3], axis=1),
            0: jnp.concatenate([blank] + parts[0] + parts[1], axis=1),
        }
        places = {2: (0, LANES), 3: (LANES + 2 * hidden_width, 2 * LANES + 2 * hidden_width)}
        places.update(
            {0: (LANES, 2 * LANES), 1: (2 * LANES + 6 * width, 3 * LANES + 6 * width)}
        )

        def build_first():
            return gain_shard

    def sum_line(value):
        if fsdp_count != 4:
            return lax.psum(value, FSDP)
        near, two, three = rotations(value)[1:]
        return (value + two) + (near + three)

    cols_old = (col_qkv, col_out, col_up, col_down)
    moments_old = (var_attn, var_mlp)
    new_rows, new_cols, ratios, new_masters = [None] * 4, [None] * 4, [None] * 4, [None] * 4

    def update(position, summed, weight_total):
        gradient, row_new = built[position]
        at_total, start = places[position]
        cols = gradient.shape[1]
        row_count = gradient.shape[0] * fsdp_count
        entry_count = row_count * cols
        col_all = summed[:, start : start + cols]
        ratio_all = summed[:, start + cols : start + 2 * cols]
        row_mean = summed[:, at_total : at_total + 1] / row_count
        new_rows[position] = row_new.reshape(1, -1)
        new_cols[position] = (
            decay_rate * cols_old[position] + (1.0 - decay_rate) * col_all / row_count
        )
        ratios[position] = jnp.sqrt(
            row_mean * total(ratio_all / new_cols[position]) / entry_count
        )
        weight_scale = jnp.sqrt(weight_total / entry_count + weight_eps)
        factor = step_rate * weight_scale / jnp.maximum(1.0, ratios[position] / clip_level)
        raw = gradient * lax.rsqrt(row_new * new_cols[position] / row_mean)
        new_masters[position] = masters[position] - factor * raw

    early = sum_line(with_lanes(sums[2], state.weight_totals))
    gain_shard = build_first()
    moments, gain_updates = [], []
    for gain_pos in range(2):
        grad = gain_shard[gain_pos : gain_pos + 1]
        moment = decay_rate * moments_old[gain_pos] + (1.0 - decay_rate) * grad * grad
        moments.append(moment)
        gain_updates.append(grad * lax.rsqrt(moment))
    last = with_lanes(sums[0], lanes([total(step * step) for step in gain_updates], 2))
    summed, early = sum_line(last), after(early, last)
    weight_all = [early[:, 2 + i : 3 + i] for i in range(6)]
    for position in (2, 3):
        update(position, early, weight_all[position])
    for position in (0, 1):
        update(position, summed, weight_all[position])
    for gain_pos in range(2):
        clip_ratio = jnp.sqrt(summed[:, 2 + gain_pos : 3 + gain_pos] / width)
        weight_scale = jnp.sqrt(weight_all[4 + gain_pos] / width + weight_eps)
        factor = step_rate * weight_scale / jnp.maximum(1.0, clip_ratio / clip_level)
        new_masters.append(gain_masters[gain_pos] - factor * gain_updates[gain_pos])
        ratios.append(clip_ratio)
    return (
        hidden_out[None],
        in_grads_out[None],
        *[entry[0][None] for entry in built],
        gain_shard[:1],
        gain_shard[1:],
        *[master[None] for master in new_masters[:4]],
        new_masters[4],
        new_masters[5],
        new_rows[0],
        new_cols[0],
        new_rows[1],
        new_cols[1],
        new_rows[2],
        new_cols[2],
        new_rows[3],
        new_cols[3],
        moments[0],
        moments[1],
        jnp.concatenate(ratios, axis=1),
    )


def solution(mesh):
    in_specs = (
        P(FSDP, CTX, None),
        P(FSDP, CTX, None),
        P(FSDP, None),
        P(SECTION, FSDP, None),
        P(SECTION, FSDP, None),
        P(SECTION, FSDP, None),
        P(SECTION, FSDP, None),
        P(SECTION, FSDP),
        P(SECTION, FSDP),
        P(SECTION, FSDP),
        P(SECTION, None),
        P(SECTION, FSDP),
        P(SECTION, None),
        P(SECTION, FSDP),
        P(SECTION, None),
        P(SECTION, FSDP),
        P(SECTION, None),
        P(SECTION, FSDP),
        P(SECTION, FSDP),
    )
    out_specs = (
        P(SECTION, FSDP, CTX, None),
        P(SECTION, FSDP, CTX, None),
        P(SECTION, FSDP, None),
        P(SECTION, FSDP, None),
        P(SECTION, FSDP, None),
        P(SECTION, FSDP, None),
        P(SECTION, FSDP),
        P(SECTION, FSDP),
        P(SECTION, FSDP, None),
        P(SECTION, FSDP, None),
        P(SECTION, FSDP, None),
        P(SECTION, FSDP, None),
        P(SECTION, FSDP),
        P(SECTION, FSDP),
        P(SECTION, FSDP),
        P(SECTION, None),
        P(SECTION, FSDP),
        P(SECTION, None),
        P(SECTION, FSDP),
        P(SECTION, None),
        P(SECTION, FSDP),
        P(SECTION, None),
        P(SECTION, FSDP),
        P(SECTION, FSDP),
        P(SECTION, None),
    )
    return jax.shard_map(
        per_device, mesh=mesh, in_specs=in_specs, out_specs=out_specs, check_vma=False
    )
```

```python
import functools
import types

import jax
import jax.numpy as jnp
from jax import lax
from jax.experimental import pallas as pl
from jax.experimental.pallas import tpu as pltpu
from jax.sharding import PartitionSpec as P

HEADS = 16


decay_rate = 0.5
clip_level = 0.5
step_rate = 1.0
norm_eps = 1e-05
weight_eps = 1e-06
mask_fill = -1e30

bf16 = jnp.bfloat16
f32 = jnp.float32
LANES = 128
SECTION, CTX, FSDP = "section", "ctx", "fsdp"
ROWS, COLUMNS, PACKED = range(3)


def swap_core(value):
    return lax.ppermute(value, SECTION, [(0, 1), (1, 0)])


def swap_x(value):
    return lax.ppermute(value, CTX, [(i, i ^ 1) for i in range(4)])


def swap_y(value):
    return lax.ppermute(value, CTX, [(i, i ^ 2) for i in range(4)])


def dot(left, right):
    return jnp.dot(left, right, preferred_element_type=f32)


def times_transposed(left, right):
    return lax.dot_general(left, right, (((1,), (1,)), ((), ())), preferred_element_type=f32)


def rows_product(left, right):
    return lax.dot_general(left, right, (((0,), (0,)), ((), ())), preferred_element_type=f32)


def after(value, *tokens):
    return lax.optimization_barrier((value, *tokens))[0]


def with_core(value):
    return jnp.concatenate([value, swap_core(value)], axis=0)


def gather_tiles(value):
    return [with_core(value), with_core(swap_x(value))]


def fold_core(partial):
    rows = partial.shape[0] // 2
    partial = partial.astype(bf16)
    return partial[:rows].astype(f32) + swap_core(partial[rows:]).astype(f32)


(SEND, ATTEND0, ATTEND1, STACKED, LAST, NORM, FEED0, FEED1, OUT) = range(9)


def norm_parts(values):
    center = values - jnp.mean(values, axis=-1, keepdims=True)
    spread = jnp.mean(center * center, axis=-1, keepdims=True)
    scale = lax.rsqrt(spread + norm_eps)
    return center * scale, scale


def norm_back(out_grad, unit, scale, gain):
    scaled = out_grad * gain
    mean_scaled = jnp.mean(scaled, axis=-1, keepdims=True)
    mean_unit = jnp.mean(scaled * unit, axis=-1, keepdims=True)
    return scale * (scaled - mean_scaled - unit * mean_unit), jnp.sum(out_grad * unit, axis=0)


def nt(left, right):
    return lax.dot_general(left, right, (((1,), (1,)), ((), ())), preferred_element_type=f32)


def attention_kernel(q_ref, k_ref, v_ref, qid_ref, kid_ref, out_ref, lse_ref, *, scale):
    queries = q_ref[...] * jnp.asarray(scale, bf16)
    keys, values_t = k_ref[...], v_ref[...].T
    same = kid_ref[...] == qid_ref[...]
    first = lax.broadcasted_iota(jnp.int32, queries.shape, 1) < queries.shape[1] // 2
    parts = []
    for head in range(2):
        own = jnp.where(first if head == 0 else ~first, queries, jnp.zeros_like(queries))
        scores = jnp.where(same, nt(keys, own), mask_fill)
        peak = jnp.max(scores, axis=0, keepdims=True)
        weights = jnp.exp(scores - peak)
        total = jnp.sum(weights, axis=0, keepdims=True)
        lse_ref[0, head : head + 1, :] = peak + jnp.log(total)
        parts.append(dot(values_t, weights.astype(bf16)) * (1.0 / total))
    width = values_t.shape[0] // 2
    stacked = jnp.concatenate([parts[0][:width], parts[1][width:]], axis=0)
    out_ref[...] = stacked.T.astype(bf16)


def attention_forward(projected, keys_values, query_ids, key_ids, scale):
    rows, seq_len = projected.shape[0], keys_values.shape[0]
    tile = min(256, rows)
    elems = 4 * rows * seq_len
    return pl.pallas_call(
        functools.partial(attention_kernel, scale=scale),
        grid=(2, rows // tile),
        in_specs=[
            pl.BlockSpec((tile, LANES), lambda p, i: (i, 3 * p)),
            pl.BlockSpec((seq_len, LANES), lambda p, i: (0, 3 * p + 1)),
            pl.BlockSpec((seq_len, LANES), lambda p, i: (0, 3 * p + 2)),
            pl.BlockSpec((1, tile), lambda p, i: (0, i)),
            pl.BlockSpec((seq_len, 1), lambda p, i: (0, 0)),
        ],
        out_specs=[
            pl.BlockSpec((tile, LANES), lambda p, i: (i, p)),
            pl.BlockSpec((1, 2, tile), lambda p, i: (p, 0, i)),
        ],
        out_shape=[
            jax.ShapeDtypeStruct((rows, 2 * LANES), bf16),
            jax.ShapeDtypeStruct((2, 2, rows), f32),
        ],
        compiler_params=pltpu.CompilerParams(vmem_limit_bytes=32 << 20),
        cost_estimate=pl.CostEstimate(
            flops=elems * 4 * 128, bytes_accessed=4 << 20, transcendentals=elems
        ),
    )(projected, keys_values, keys_values, query_ids, key_ids)


def attention_back_kernel(
    q_ref, k_ref, v_ref, g_ref, lse_ref, qid_ref, kid_ref, *refs, scale, last
):
    queries = q_ref[...] * jnp.asarray(scale, bf16)
    keys, values, grads = k_ref[...], v_ref[...], g_ref[...]
    keys_t = keys.T
    same = kid_ref[...] == qid_ref[...]
    first = lax.broadcasted_iota(jnp.int32, queries.shape, 1) < queries.shape[1] // 2
    step = pl.program_id(1)
    if last:
        early_q, early_k, early_v, out_ref, dk_ref, dv_ref = refs
    else:
        dq_ref, dk_ref, dv_ref = refs

    @pl.when(step == 0)
    def _():
        dk_ref[...] = early_k[...] if last else jnp.zeros_like(dk_ref)
        dv_ref[...] = early_v[...] if last else jnp.zeros_like(dv_ref)

    parts = []
    for head in range(2):
        mine = first if head == 0 else ~first
        own = jnp.where(mine, queries, jnp.zeros_like(queries))
        own_grads = jnp.where(mine, grads, jnp.zeros_like(grads))
        scores = jnp.where(same, nt(keys, own), mask_fill)
        weights = jnp.exp(scores - lse_ref[0, head : head + 1, :])
        prob_grad = nt(values, own_grads)
        row_dot = jnp.sum(weights * prob_grad, axis=0, keepdims=True)
        score_grad = (weights * (prob_grad - row_dot)).astype(bf16)
        dv_ref[...] += dot(weights.astype(bf16), own_grads)
        dk_ref[...] += dot(score_grad, own)
        parts.append(dot(keys_t, score_grad))
    width = keys_t.shape[0] // 2
    stacked = jnp.concatenate([parts[0][:width], parts[1][width:]], axis=0)
    query_grad = (stacked.T * scale).astype(bf16)
    if not last:
        dq_ref[...] = query_grad
        return
    early, tile = early_q.shape[0], query_grad.shape[0]
    start = pl.multiple_of(early + step * tile, tile)
    out_ref[pl.ds(start, tile), :LANES] = query_grad

    @pl.when(step == pl.num_programs(1) - 1)
    def _():
        out_ref[:early, :LANES] = early_q[...]
        out_ref[:, LANES : 2 * LANES] = dk_ref[...].astype(bf16)
        out_ref[:, 2 * LANES :] = dv_ref[...].astype(bf16)


def attention_backward(projected, keys_values, grads, lse, query_ids, key_ids, scale, early=None):
    rows, seq_len = projected.shape[0], keys_values.shape[0]
    tile = min(256, rows)
    elems = 4 * rows * seq_len

    def column(size):
        return pl.BlockSpec((size, LANES), lambda p, i: (0, p))

    in_specs = [
        pl.BlockSpec((tile, LANES), lambda p, i: (i, 3 * p)),
        pl.BlockSpec((seq_len, LANES), lambda p, i: (0, 3 * p + 1)),
        pl.BlockSpec((seq_len, LANES), lambda p, i: (0, 3 * p + 2)),
        pl.BlockSpec((tile, LANES), lambda p, i: (i, p)),
        pl.BlockSpec((1, 2, tile), lambda p, i: (p, 0, i)),
        pl.BlockSpec((1, tile), lambda p, i: (0, i)),
        pl.BlockSpec((seq_len, 1), lambda p, i: (0, 0)),
    ]
    if early is None:
        out_specs = [pl.BlockSpec((tile, LANES), lambda p, i: (i, p))] + [column(seq_len)] * 2
        out_shape = [
            jax.ShapeDtypeStruct((rows, 2 * LANES), bf16),
            jax.ShapeDtypeStruct((seq_len, 2 * LANES), f32),
            jax.ShapeDtypeStruct((seq_len, 2 * LANES), f32),
        ]
        scratch = []
    else:
        in_specs += [column(early[0].shape[0]), column(seq_len), column(seq_len)]
        out_specs = pl.BlockSpec((seq_len, 3 * LANES), lambda p, i: (0, p))
        out_shape = jax.ShapeDtypeStruct((seq_len, 6 * LANES), bf16)
        scratch = [pltpu.VMEM((seq_len, LANES), f32)] * 2
    return pl.pallas_call(
        functools.partial(attention_back_kernel, scale=scale, last=early is not None),
        grid=(2, rows // tile),
        in_specs=in_specs,
        out_specs=out_specs,
        out_shape=out_shape,
        scratch_shapes=scratch,
        compiler_params=pltpu.CompilerParams(vmem_limit_bytes=32 << 20),
        cost_estimate=pl.CostEstimate(
            flops=elems * 10 * 128, bytes_accessed=6 << 20, transcendentals=elems
        ),
    )(projected, keys_values, keys_values, grads, lse, query_ids, key_ids, *(early or ()))


def weight_grad_kernel(*refs, lefts, rights):
    outs = refs[-lefts * rights :]
    for i in range(lefts):
        turned = [refs[2 * i + k][...].T for k in range(2)]
        for j in range(rights):
            at = 2 * lefts + 2 * j
            total = dot(turned[0], refs[at][...]) + dot(turned[1], refs[at + 1][...])
            outs[i * rights + j][...] = total.astype(bf16)


def weight_grad(lefts, rights):
    size = lefts[0][0].shape[1]
    depth = lefts[0][0].shape[0]
    tile = min(256, size)
    operands, specs, outs = [], [], []
    for pair in lefts:
        for value in pair:
            operands.append(value)
            specs.append(pl.BlockSpec((depth, tile), lambda i: (0, i)))
    for pair, cols, at in rights:
        for value, row in pair:
            operands.append(value)
            specs.append(pl.BlockSpec((depth, cols), lambda i, row=row, at=at: (row, at)))
    for _ in lefts:
        outs += [jax.ShapeDtypeStruct((size, cols), bf16) for _, cols, _ in rights]
    columns = sum(cols for _, cols, _ in rights)
    return pl.pallas_call(
        functools.partial(weight_grad_kernel, lefts=len(lefts), rights=len(rights)),
        grid=(size // tile,),
        in_specs=specs,
        out_specs=[pl.BlockSpec((tile, out.shape[1]), lambda i: (i, 0)) for out in outs],
        out_shape=outs,
        compiler_params=pltpu.CompilerParams(vmem_limit_bytes=32 << 20),
        cost_estimate=pl.CostEstimate(
            flops=4 * depth * size * len(lefts) * columns,
            bytes_accessed=4 * depth * (size * len(lefts) + columns),
            transcendentals=0,
        ),
    )(*operands)


def whole(shape):
    return pl.BlockSpec(shape, lambda *_: (0,) * len(shape))


def cut_kernel(_, *refs, width):
    first, up, down = refs[:16], refs[16:24], refs[24:26]
    packed, far, ups, downs = refs[26:28], refs[28:30], refs[30:32], refs[32:34]
    rows = first[0].shape[1]
    for core in range(2):
        for i in range(3):
            lanes = slice(LANES * i, LANES * (i + 1))
            packed[core][:rows, lanes] = first[3 * core + i][0].astype(bf16)
            far[core][:, lanes] = first[6 + 3 * core + i][0].astype(bf16)
        out = first[12 + core][0].astype(bf16)
        packed[core][:LANES, 3 * LANES :] = out[:, :LANES]
        packed[core][LANES:rows, 3 * LANES :] = out[:, LANES:]
        gains = jnp.concatenate([first[14][...], first[15][...]], axis=1)
        top = lax.broadcasted_iota(jnp.int32, (16, 2 * rows), 0) == 0
        gains = jnp.where(top, jnp.broadcast_to(gains, (16, 2 * rows)), 0.0)
        packed[core][rows:, :] = gains.astype(bf16)
        for i in range(4):
            ups[core][:, LANES * i : LANES * (i + 1)] = up[4 * core + i][0].astype(bf16)
        downs[core][...] = down[core][0].astype(bf16)


def cut_weights(w_qkv, w_out, w_up, w_down, gain_attn, gain_mlp, at_eighth):
    rows, width = w_qkv.shape[1], w_out.shape[2]

    def column(i, flip):
        return pl.BlockSpec((1, rows, LANES), lambda g, at: (0, 0, 8 * i + (at[0] ^ flip)))

    specs = [column(i, flip) for flip in (0, 1, 4, 5) for i in range(3)]
    specs += [
        pl.BlockSpec(
            (1, LANES, 2 * LANES), lambda g, at, c=core: (0, (at[0] & 1) ^ c, at[0] >> 1)
        )
        for core in range(2)
    ]
    specs += [whole(gain_attn.shape), whole(gain_mlp.shape)]
    specs += [column(i, core) for core in range(2) for i in range(4)]
    specs += [
        pl.BlockSpec((1, LANES, width), lambda g, at, c=core: (0, at[0] ^ c, 0))
        for core in range(2)
    ]
    outs = [
        jax.ShapeDtypeStruct(shape, bf16)
        for shape in (
            (rows + 16, 4 * LANES),
            (rows, 3 * LANES),
            (rows, 4 * LANES),
            (LANES, width),
        )
        for _ in range(2)
    ]
    operands = [w_qkv] * 12 + [w_out] * 2 + [gain_attn, gain_mlp] + [w_up] * 8 + [w_down] * 2
    return pl.pallas_call(
        functools.partial(cut_kernel, width=width),
        grid_spec=pltpu.PrefetchScalarGridSpec(
            num_scalar_prefetch=1,
            grid=(1,),
            in_specs=specs,
            out_specs=[whole(out.shape) for out in outs],
        ),
        out_shape=outs,
        compiler_params=pltpu.CompilerParams(vmem_limit_bytes=56 << 20),
    )(at_eighth, *operands)


def place_qkv_kernel(at, *refs, fixed):
    out_ref = refs[-1]
    rows, cols = refs[4].shape
    for k in range(4):
        slot = k if fixed else lax.rem(at[0] + 4 - k, 4)
        part = pl.ds(pl.multiple_of(slot * rows, rows), rows)
        out_ref[part, :cols] = refs[k][:rows, :cols]
        out_ref[part, cols:] = refs[4 + k][...]


def place_out_kernel(at, *refs, fixed):
    out_ref, gain_ref = refs[-2:]
    rows, cols = refs[0].shape[0] - 16, refs[0].shape[1] - LANES
    for k in range(4):
        slot = k if fixed else lax.rem(at[0] + 4 - k, 4)
        packed = refs[k]
        away = slot ^ at[1]
        away = 2 * (away & 1) + (away >> 1)
        out_ref[away, :, :LANES] = packed[:LANES, cols:]
        out_ref[away, :, LANES:] = packed[LANES:rows, cols:]
        part = pl.ds(pl.multiple_of(slot * rows, rows), rows)
        gains = packed[rows:, :].astype(f32)
        gain_ref[0:1, part] = gains[0:1, :rows]
        gain_ref[1:2, part] = gains[0:1, rows:]


def place(kernel, operands, shapes, outs, at, fixed):
    specs = [
        pl.BlockSpec(shape, (lambda g, at, k=k: (k, 0)) if fixed else (lambda g, at: (0, 0)))
        for shape in shapes
        for k in range(4)
    ]
    if fixed:
        operands = [value for value in operands for _ in range(4)]
    return pl.pallas_call(
        functools.partial(kernel, fixed=fixed),
        grid_spec=pltpu.PrefetchScalarGridSpec(
            num_scalar_prefetch=1,
            grid=(1,),
            in_specs=specs,
            out_specs=[whole(out.shape) for out in outs],
        ),
        out_shape=outs,
        compiler_params=pltpu.CompilerParams(vmem_limit_bytes=24 << 20),
    )(at, *operands)


def small_call(kernel, at, operands, outs, room=40):
    return pl.pallas_call(
        kernel,
        grid_spec=pltpu.PrefetchScalarGridSpec(
            num_scalar_prefetch=1,
            grid=(1,),
            in_specs=[whole(value.shape) for value in operands],
            out_specs=[whole(out.shape) for out in outs],
        ),
        out_shape=outs,
        compiler_params=pltpu.CompilerParams(vmem_limit_bytes=room << 20),
    )(at, *operands)


def join_out_kernel(at, keep, came, far_keep, far_came, out_ref):
    for b in range(2):
        rows = slice(LANES * b, LANES * (b + 1))
        for away, value in enumerate((keep[b], came[b], far_keep[1 - b], far_came[1 - b])):
            size = value.shape[1]
            start = pl.multiple_of((at[0] ^ away) * size, size)
            out_ref[rows, pl.ds(start, size)] = value


def fold_out_kernel(at, keep, came, near_ref, give_ref):
    size = near_ref.shape[2]
    first_x = (at[0] & 1) == 0
    for b in range(2):
        value = keep[b].astype(f32) + came[1 - b].astype(f32)
        low, high = value[:, :size], value[:, size:]
        near_ref[b] = jnp.where(first_x, low, high).astype(bf16)
        give_ref[b] = jnp.where(first_x, high, low).astype(bf16)


def pack_kernel(at, keep, came, near, cross, gains, out_ref):
    cols = keep.shape[1]
    rows = keep.shape[0] // 4
    top = lax.broadcasted_iota(jnp.int32, (16, 2 * rows), 0) == 0
    for f in range(4):
        base = f * (rows + 16)
        part = slice(rows * f, rows * (f + 1))
        out_ref[base : base + rows, :cols] = (
            keep[part, :].astype(f32) + came[part, :].astype(f32)
        ).astype(bf16)
        gain = jnp.concatenate([gains[0:1, part], gains[1:2, part]], axis=1)
        gain = jnp.where(top, jnp.broadcast_to(gain, (16, 2 * rows)), 0.0)
        out_ref[base + rows : base + rows + 16, :] = gain.astype(bf16)
    for away, value in enumerate((near[0], cross[0], near[1], cross[1])):
        base = (at[0] ^ away) * (rows + 16)
        for half in range(2):
            start = pl.multiple_of(base + LANES * half, 16)
            out_ref[pl.ds(start, LANES), cols:] = value[:, LANES * half : LANES * (half + 1)]


def assemble_kernel(at, *refs, kind, shapes):
    groups = [refs[4 * i : 4 * i + 4] for i in range(4)]
    rows_old = refs[16 : 16 + len(shapes)]
    extra = refs[16 + len(shapes)]
    outs = refs[17 + len(shapes) :]
    grads, rows_new, sums_ref = outs[: len(shapes)], outs[len(shapes) : 2 * len(shapes)], outs[-1]
    first_core = at[1] == 0
    gain = 0.0
    for core in range(2):
        for chip in range(4):
            eighth = (2 * chip + core) ^ at[0]
            value = jnp.where(first_core, groups[core][chip][...], groups[2 + core][chip][...])
            value = value.astype(f32)
            if kind == ROWS:
                rows = value.shape[0]
                grads[0][pl.ds(pl.multiple_of(eighth * rows, rows), rows), :] = value
            elif kind == COLUMNS:
                for i in range(value.shape[1] // LANES):
                    start = pl.multiple_of((8 * i + eighth) * LANES, LANES)
                    grads[0][:, pl.ds(start, LANES)] = value[:, LANES * i : LANES * (i + 1)]
            else:
                rows = shapes[0][0]
                for i in range(3):
                    start = pl.multiple_of((8 * i + eighth) * LANES, LANES)
                    grads[0][:, pl.ds(start, LANES)] = value[:rows, LANES * i : LANES * (i + 1)]
                part = pl.ds(pl.multiple_of((eighth & 1) * LANES, LANES), LANES)
                for half in range(2):
                    start = pl.multiple_of((2 * (eighth >> 1) + half) * LANES, LANES)
                    block = value[half * LANES : (half + 1) * LANES, 3 * LANES :]
                    grads[1][part, pl.ds(start, LANES)] = block
                gain = gain + value[rows : rows + 1, :]
    lane = lax.broadcasted_iota(jnp.int32, (1, LANES), 1)
    sums_ref[...] = jnp.zeros_like(sums_ref)
    if kind == PACKED:
        outs[-2][...] = gain
        moment = decay_rate * extra[...] + (1.0 - decay_rate) * gain * gain
        square = (gain * lax.rsqrt(moment)) ** 2
        middle = square.shape[1] // 2
        attn_total = jnp.sum(square[:, :middle], axis=1, keepdims=True)
        mlp_total = jnp.sum(square[:, middle:], axis=1, keepdims=True)
        sums_ref[:, :LANES] = jnp.where(lane == 2, attn_total, jnp.where(lane == 3, mlp_total, 0.0))
    else:
        sums_ref[:, :LANES] = extra[...]
    begin = LANES
    for index, (total_rows, cols) in enumerate(shapes):
        grad_ref, row_ref, new_ref = grads[index], rows_old[index], rows_new[index]
        col_part = slice(begin, begin + cols)
        ratio_part = slice(begin + cols, begin + 2 * cols)
        begin += 2 * cols

        def body(i, total):
            part = pl.ds(pl.multiple_of(i * 64, 64), 64)
            values = grad_ref[part, :]
            square = values * values
            row_new = decay_rate * row_ref[part, :] + (1.0 - decay_rate) * (
                jnp.sum(square, axis=1, keepdims=True) / cols
            )
            new_ref[part, :] = row_new
            sums_ref[:, col_part] += jnp.sum(square, axis=0, keepdims=True)
            sums_ref[:, ratio_part] += jnp.sum(square * (1.0 / row_new), axis=0, keepdims=True)
            return total + jnp.sum(row_new, axis=0, keepdims=True)

        total = lax.fori_loop(0, total_rows // 64, body, jnp.zeros((1, 1), f32))
        sums_ref[:, :LANES] += jnp.where(lane == index, total, 0.0)


def assemble(near0, near1, far0, far1, rows_old, extra, where, kind, shapes):
    outs = [jax.ShapeDtypeStruct(shape, f32) for shape in shapes]
    outs += [jax.ShapeDtypeStruct((shape[0], 1), f32) for shape in shapes]
    if kind == PACKED:
        outs.append(jax.ShapeDtypeStruct((1, near0[0].shape[1]), f32))
    outs.append(
        jax.ShapeDtypeStruct((1, LANES + 2 * sum(shape[1] for shape in shapes)), f32)
    )
    return small_call(
        functools.partial(assemble_kernel, kind=kind, shapes=shapes),
        where,
        [*near0, *far0, *near1, *far1, *rows_old, extra],
        outs,
        56,
    )


def per_device(
    tokens,
    cotangent,
    segment_ids,
    w_qkv,
    w_out,
    w_up,
    w_down,
    gain_attn,
    gain_mlp,
    row_qkv,
    col_qkv,
    row_out,
    col_out,
    row_up,
    col_up,
    row_down,
    col_down,
    var_attn,
    var_mlp,
):
    core = lax.axis_index(SECTION)
    chip = lax.axis_index(CTX)
    depth = lax.axis_index(FSDP)
    y, x = chip // 2, chip % 2
    fsdp_count = lax.axis_size(FSDP)
    assert lax.axis_size(SECTION) == 2 and lax.axis_size(CTX) == 4
    _, block, width = tokens.shape
    half = block // 2
    rows = w_qkv.shape[1]
    hidden_width = w_up.shape[2]
    unit = hidden_width // fsdp_count // 8
    scale = (width // HEADS) ** (-0.5)
    even = fsdp_count == 4 and rows == 2 * LANES and unit == LANES
    first_core, first_y, first_x = core == 0, y == 0, x == 0

    def flipped(when, value, axis=0):
        low, high = jnp.split(value, 2, axis)
        return jnp.where(when, jnp.concatenate([high, low], axis), value)

    at_eighth = 2 * chip + core

    def eighth(e):
        qkv = lax.dynamic_index_in_dim(w_qkv[0].reshape(rows, 3, 8, LANES), e, 2, keepdims=False)
        up = lax.dynamic_index_in_dim(
            w_up[0].reshape(rows, fsdp_count, 8, unit), e, 2, keepdims=False
        )
        down = lax.dynamic_slice_in_dim(w_down[0], e * unit, unit, 0)
        return [
            part.astype(bf16)
            for part in (qkv.reshape(rows, 3 * LANES), up.reshape(rows, fsdp_count * unit), down)
        ]

    def by_layer(mine, other):
        taken = swap_core(other)
        return jnp.where(first_core, mine, taken), jnp.where(first_core, taken, mine)

    def gather_rows(value):
        return lax.all_gather(value, FSDP, axis=0, tiled=True)

    def rotations(value):
        return [value] + [
            lax.ppermute(
                value, FSDP, [(i, (i + k) % fsdp_count) for i in range(fsdp_count)]
            )
            for k in range(1, fsdp_count)
        ]

    def with_far(value):
        return value, swap_y(value)

    chip_array = chip.reshape(1).astype(jnp.int32)

    def out_parts(columns):
        keep, came = columns[:2], swap_x(columns[2:])
        return [keep, came, swap_y(keep), swap_y(came)]

    def join_out(parts):
        out = jax.ShapeDtypeStruct((2 * LANES, width), bf16)
        return small_call(join_out_kernel, chip_array, parts, [out])[0]

    weights, gains = [types.SimpleNamespace(), types.SimpleNamespace()], [None, None]
    depth_array = jnp.stack([depth, chip]).astype(jnp.int32)
    if even:
        cuts = cut_weights(
            w_qkv, w_out, w_up, w_down, gain_attn, gain_mlp, at_eighth.reshape(1).astype(jnp.int32)
        )
        packed_parts = by_layer(*cuts[:2])
        far_parts = by_layer(*cuts[2:4])
        up_parts = by_layer(*cuts[4:6])
        down_parts = by_layer(*cuts[6:])
        turns = rotations(packed_parts[0])
        fars = [swap_y(value[:rows, : 3 * LANES]) for value in turns[1:]]

        def place_qkv(packed, far, fixed):
            shapes = ((rows + 16, 4 * LANES), (rows, 3 * LANES))
            out = jax.ShapeDtypeStruct((4 * rows, 6 * LANES), bf16)
            return place(place_qkv_kernel, [*packed, *far], shapes, [out], depth_array, fixed)[0]

        def place_out(packed, fixed):
            outs = [
                jax.ShapeDtypeStruct((4, LANES, 2 * LANES), bf16),
                jax.ShapeDtypeStruct((2, 4 * rows), f32),
            ]
            shapes = ((rows + 16, 4 * LANES),)
            columns, gain = place(place_out_kernel, packed, shapes, outs, depth_array, fixed)
            return out_parts(columns), gain

        weights[0].qkv = place_qkv(turns, [far_parts[0]] + fars, False)
        weights[0].out, gains[0] = place_out(turns, False)
        up_gathered = [gather_rows(after(up_parts[0], *turns[1:])), gather_rows(up_parts[1])]
        down_gathered = [gather_rows(after(down_parts[0], *turns[1:])), gather_rows(down_parts[1])]
        packed_gathered = gather_rows(packed_parts[1])
    else:
        mine_parts, other_parts = eighth(at_eighth), eighth(at_eighth ^ 1)
        qkv_parts, up_parts, down_parts = [by_layer(a, b) for a, b in zip(mine_parts, other_parts)]
        whole_out = gather_rows(w_out[0].astype(bf16))
        out_parts = by_layer(whole_out, whole_out)
        gains_own = lax.all_gather(
            jnp.concatenate([gain_attn, gain_mlp], axis=0).astype(bf16), FSDP, axis=1, tiled=True
        )
        gains = [part.astype(f32) for part in by_layer(gains_own, gains_own)]
        for layer in range(2):
            blocks = out_parts[layer].reshape(4, 2, LANES, width)
            blocks = lax.dynamic_index_in_dim(blocks, core, 1, keepdims=False)
            weights[layer] = types.SimpleNamespace(
                qkv=jnp.concatenate(with_far(gather_rows(qkv_parts[layer])), axis=1),
                out=jnp.concatenate(
                    [
                        lax.dynamic_index_in_dim(blocks, chip, 0, keepdims=False),
                        lax.dynamic_index_in_dim(blocks, chip ^ 2, 0, keepdims=False),
                    ],
                    axis=0,
                ),
                up=with_far(gather_rows(up_parts[layer])),
                down=with_far(gather_rows(down_parts[layer])),
            )

    def own_rows(value):
        near = lax.dynamic_slice(value, (y, core * half, 0), (1, half, width))[0]
        away = lax.dynamic_slice(value, (1 - y, core * half, 0), (1, half, width))[0]
        return jnp.concatenate([near, swap_y(away)], axis=0)

    ids = lax.dynamic_index_in_dim(segment_ids, y, 0, keepdims=False).reshape(2, 2, 2, half)
    ids = flipped(~first_y, flipped(~first_x, flipped(~first_core, ids, 2), 1), 0)
    ids = ids.transpose(1, 2, 0, 3)
    key_ids = ids.reshape(8 * half, 1)
    query_ids = [ids[k].reshape(1, 4 * half) for k in range(2)]

    def forward(inputs, layer, hook):
        held = weights[layer]
        attn_gain, mlp_gain = gains[layer][0], gains[layer][1]
        inputs_all = gather_tiles(inputs)
        projected = [dot(value, held.qkv).astype(bf16) for value in inputs_all]
        keys_values = jnp.concatenate(projected, axis=0)

        def attend(k, queries):
            context, lse = attention_forward(queries, keys_values, query_ids[k], key_ids, scale)
            context = hook(OUT, context) if k == 1 else context
            return context, lse, fold_core(dot(context, held.out))

        context1, lse1, across = attend(1, hook(ATTEND0, projected[1]))
        across = across.astype(bf16)
        context0, lse0, keep = attend(0, hook(ATTEND1, after(projected[0], across)))
        came = hook(NORM, after(swap_x(across), keep))
        unit_attn, scale_attn = norm_parts(inputs.astype(f32) + keep + came.astype(f32))
        normed = unit_attn * attn_gain
        normed_all = gather_tiles(normed.astype(bf16))

        def feed(value):
            activated, slope, partial = [], [], 0.0
            for half_up, half_down in zip(held.up, held.down):
                upward = dot(value, half_up)
                phi_whole = 0.5 * (1.0 + lax.erf(upward * (0.5**0.5)))
                activated.append((upward * phi_whole).astype(bf16))
                density = jnp.exp(-0.5 * upward * upward) * 0.3989422804014327
                slope.append((phi_whole + upward * density).astype(bf16))
                partial += dot(activated[-1], half_down)
            return activated, slope, fold_core(partial)

        activated0, slope0, keep = feed(hook(FEED0, normed_all[0]))
        activated1, slope1, across = feed(hook(FEED1, after(normed_all[1], keep)))
        came = hook(LAST, swap_x(hook(SEND, across.astype(bf16))))
        unit_mlp, scale_mlp = norm_parts(normed + keep + came.astype(f32))
        return (unit_mlp * mlp_gain).astype(bf16), types.SimpleNamespace(
            inputs_all=inputs_all,
            projected=projected,
            keys_values=keys_values,
            context=(context0, context1),
            lse=(lse0, lse1),
            unit_attn=unit_attn,
            scale_attn=scale_attn,
            normed_all=normed_all,
            activated=(activated0, activated1),
            slope=(slope0, slope1),
            unit_mlp=unit_mlp,
            scale_mlp=scale_mlp,
        )

    def backward(out_grads, kept, layer, hook):
        held = weights[layer]
        attn_gain, mlp_gain = gains[layer][0], gains[layer][1]

        def both(pair):
            return [(value, 0) for value in pair]

        mlp_in, mlp_gain_grad = norm_back(
            out_grads.astype(f32), kept.unit_mlp, kept.scale_mlp, mlp_gain
        )
        down_all = gather_tiles(mlp_in.astype(bf16))

        def feed_back(k, value):
            grads, partial = [], 0.0
            for half_up, half_down, slope in zip(held.up, held.down, kept.slope[k]):
                grad = times_transposed(value, half_down) * slope.astype(f32)
                grads.append(grad.astype(bf16))
                partial += times_transposed(grads[-1], half_up)
            return grads, fold_core(partial)

        upward0, keep = feed_back(0, hook(FEED0, down_all[0]))
        upward1, across = feed_back(1, hook(FEED1, after(down_all[1], keep)))
        grad_down = weight_grad(list(zip(*kept.activated)), [(both(down_all), width, 0)])
        came = hook(NORM, swap_x(across.astype(bf16)), grad_down)
        attn_in, attn_gain_grad = norm_back(
            mlp_in + keep + came.astype(f32), kept.unit_attn, kept.scale_attn, attn_gain
        )
        branch_all = gather_tiles(attn_in.astype(bf16))

        def attend_back(k, value, early=None):
            grads = times_transposed(value, held.out).astype(bf16)
            return attention_backward(
                kept.projected[k],
                kept.keys_values,
                grads,
                kept.lse[k],
                query_ids[k],
                key_ids,
                scale,
                early,
            )

        grad_up = weight_grad(
            [kept.normed_all],
            [(both(right), right[0].shape[1], 0) for right in zip(upward0, upward1)],
        )
        early = attend_back(0, hook(ATTEND0, branch_all[0], grad_up))
        stacked = attend_back(1, hook(ATTEND1, after(branch_all[1], early[0])), early)
        gain_grads = jnp.stack([attn_gain_grad, mlp_gain_grad])
        (grad_out,) = weight_grad([kept.context], [(both(branch_all), width, 0)])
        stacked = hook(STACKED, stacked, grad_out, gain_grads)
        tile = 4 * half
        across = fold_core(times_transposed(stacked[tile:], held.qkv)).astype(bf16)
        across = hook(SEND, across)
        keep = fold_core(times_transposed(after(stacked, across)[:tile], held.qkv))
        came = hook(LAST, after(swap_x(across), keep))
        tiles = [(stacked, 0), (stacked, 1)]
        grad_qkv = weight_grad([kept.inputs_all], [(tiles, 3 * LANES, at) for at in range(2)])
        return (attn_in + keep + came.astype(f32)).astype(bf16), grad_qkv

    def scatter_rows(value):
        return lax.psum_scatter(value, FSDP, scatter_dimension=0, tiled=True)

    def sync(value, *others):
        return lax.optimization_barrier((value, *others))

    def fold(keep, came):
        return (keep.astype(f32) + came.astype(f32)).astype(bf16)

    def halves(grad):
        return grad[0], swap_y(grad[1])

    def out_halves(grad_out):
        size = width // 2
        keep = lax.dynamic_slice_in_dim(grad_out, y * size, size, 1)
        give = lax.dynamic_slice_in_dim(grad_out, (1 - y) * size, size, 1)
        return keep.reshape(2, LANES, size), swap_y(give.reshape(2, LANES, size))

    def out_pair(keep, came):
        out = jax.ShapeDtypeStruct((2, LANES, 2 * LANES), bf16)
        near, give = small_call(fold_out_kernel, chip_array, [keep, came], [out, out])
        return near, swap_x(give)

    def pack(keep, came, near, cross, gain_grads):
        out = jax.ShapeDtypeStruct((4 * (rows + 16), 4 * LANES), bf16)
        operands = [keep, came, near, cross, gain_grads]
        return small_call(pack_kernel, chip_array, operands, [out])[0]

    def spread_start(value, y_first):
        return value, (swap_y if y_first else swap_x)(value)

    def spread_end(pair, y_first):
        value, first = pair
        if y_first:
            return [value, swap_x(value), first, swap_x(first)]
        return [value, first, swap_y(value), swap_y(first)]

    def spread(value, y_first):
        return spread_end(spread_start(value, y_first), y_first)

    def reduce_plain(found):
        keep, came = out_halves(found.out)
        both = fold(keep, came[::-1])
        placed = jnp.zeros((4, 2, LANES, width // 2), bf16)
        placed = lax.dynamic_update_slice(placed, both[:1, None], (chip, core, 0, 0))
        placed = lax.dynamic_update_slice(placed, both[1:, None], (chip ^ 2, core, 0, 0))
        gain_rows = found.gains.reshape(2, fsdp_count, rows).transpose(1, 0, 2)
        gain_rows = gain_rows.reshape(fsdp_count, 1, 2 * rows).astype(bf16)
        gain_rows = jnp.pad(gain_rows, ((0, 0), (0, 15), (0, width // 2 - 2 * rows)))
        packed = jnp.concatenate([placed.reshape(fsdp_count, rows, width // 2), gain_rows], axis=1)
        return [
            spread(scatter_rows(fold(*halves(found.qkv))), False),
            spread(scatter_rows(packed.reshape(fsdp_count * (rows + 16), width // 2)), True),
            spread(scatter_rows(fold(*halves(found.up))), False),
            spread(scatter_rows(fold(*halves(found.down))), True),
        ]

    inputs, out_grads = sync(own_rows(tokens), own_rows(cotangent))
    of0, of1 = types.SimpleNamespace(), types.SimpleNamespace()

    def total(value):
        return jnp.sum(value).reshape(1, 1)

    def lanes(values, start):
        lane = lax.broadcasted_iota(jnp.int32, (1, LANES), 1)
        return sum(jnp.where(lane == start + i, value, 0.0) for i, value in enumerate(values))

    def with_lanes(row, values):
        if even:
            return row
        return jnp.concatenate([row[:, :LANES] + values, row[:, LANES:]], axis=1)

    masters = (w_qkv[0], w_out[0], w_up[0], w_down[0])
    gain_masters = (gain_attn, gain_mlp)
    state = types.SimpleNamespace(
        out_grads=out_grads,
        weight_totals=lanes([total(master * master) for master in masters + gain_masters], 2),
    )
    if even:

        def hook_forward0(point, value):
            if point == OUT:
                value, up, *parts = sync(value, up_gathered[0], *weights[0].out)
                weights[0].out = join_out(parts)
                weights[0].up = with_far(up)
            elif point == NORM:
                value, far, down = sync(value, weights[0].up[1], down_gathered[0])
                weights[0].up = weights[0].up[0], far
                weights[0].down = with_far(down)
            elif point == FEED0:
                value, far = sync(value, weights[0].down[1])
                weights[0].down = weights[0].down[0], far
            elif point == SEND:
                value, packed = sync(value, packed_gathered)
                near = packed.reshape(4, rows + 16, 4 * LANES)[:, :rows, : 3 * LANES]
                far = swap_y(near.reshape(4 * rows, 3 * LANES))
                weights[1].qkv = place_qkv([packed], [far], True)
                weights[1].out, gains[1] = place_out([packed], True)
            elif point == LAST:
                value, up = sync(value, up_gathered[1])
                weights[1].up = with_far(up)
            return value

        def hook_forward1(point, value):
            if point == OUT:
                value, down, *parts = sync(value, down_gathered[1], *weights[1].out)
                weights[1].out = join_out(parts)
                weights[1].down = with_far(down)
            elif point == NORM:
                value, far = sync(value, weights[1].up[1])
                weights[1].up = weights[1].up[0], far
            elif point == FEED0:
                value, far = sync(value, weights[1].down[1])
                weights[1].down = weights[1].down[0], far
            elif point == LAST:
                value, state.weight_totals = sync(value, state.weight_totals)
            return value

        def hook_backward1(point, value, *grads):
            if point == NORM:
                value, *down = sync(value, *grads[0])
                of1.down = halves(down)
            elif point == ATTEND0:
                value, *up = sync(value, *grads[0])
                of1.up_grads = up
            elif point == ATTEND1:
                value, *outputs = sync(value, *state.away)
                state.away = outputs
            elif point == STACKED:
                value, came, out, of1.gains = sync(value, of1.down[1], *grads)
                of1.down = scatter_rows(fold(of1.down[0], came))
                of1.up = halves(of1.up_grads)
                of1.out = out
            return value

        def hook_backward0(point, value, *grads):
            if point == FEED0:
                value, came, *qkv = sync(value, of1.up[1], *of1.qkv)
                of1.up = scatter_rows(fold(of1.up[0], came))
                of1.qkv = halves(qkv)
                of1.out = out_halves(of1.out)
            elif point == NORM:
                value, came, out_came, down, *grad_down = sync(
                    value, of1.qkv[1], of1.out[1], of1.down, *grads[0]
                )
                of1.qkv = of1.qkv[0], came
                of1.out = out_pair(of1.out[0], out_came)
                of1.down = spread_start(down, True)
                of0.down = halves(grad_down)
            elif point == ATTEND0:
                value, cross, up, *up_grads = sync(value, of1.out[1], of1.up, *grads[0])
                of1.packed = scatter_rows(pack(*of1.qkv, of1.out[0], cross, of1.gains))
                of1.up = up
                of0.up_grads = up_grads
            elif point == ATTEND1:
                value, came, hop, state.in_away = sync(
                    value, of0.down[1], of1.down[1], state.in_away
                )
                of0.down = scatter_rows(fold(of0.down[0], came))
                of0.up = halves(of0.up_grads)
                of1.up = spread_start(of1.up, False)
                of1.down = spread_end((of1.down[0], hop), True)
            elif point == STACKED:
                value, came, hop, packed, out, of0.gains, *ends = sync(
                    value, of0.up[1], of1.up[1], of1.packed, *grads, *of1.down
                )
                of0.up = scatter_rows(fold(of0.up[0], came))
                of1.up = of1.up[0], hop
                of1.down = ends
                of1.packed = spread_start(packed, False)
                of0.out = out_halves(out)
            elif point == SEND:
                value, out_came, hop = sync(value, of0.out[1], of1.packed[1])
                of0.out = out_pair(of0.out[0], out_came)
                of1.packed = of1.packed[0], hop
            elif point == LAST:
                value, of0.down = sync(value, of0.down)
            return value

    else:

        def hook_forward0(point, value):
            return value

        hook_forward1 = hook_forward0

        def hook_plain(found):
            def hook(point, value, *grads):
                if point == NORM:
                    found.down = grads[0]
                elif point == ATTEND0:
                    found.up = grads[0]
                elif point == STACKED:
                    found.out, found.gains = grads
                return value

            return hook

        hook_backward0, hook_backward1 = hook_plain(of0), hook_plain(of1)

    hidden0, saved0 = forward(inputs, 0, hook_forward0)
    hidden1, saved1 = forward(hidden0, 1, hook_forward1)
    state.away = [swap_y(hidden0[half:]), swap_y(hidden1[half:])]
    in_grads1, of1.qkv = backward(state.out_grads, saved1, 1, hook_backward1)
    state.in_away = swap_y(in_grads1[half:])
    in_grads0, of0.qkv = backward(in_grads1, saved0, 0, hook_backward0)
    if even:
        qkv_near, qkv_came = halves(of0.qkv)
        packed0 = pack(qkv_near, qkv_came, *of0.out, of0.gains)
        packed0, of0.up, of0.down = sync(packed0, of0.up, of0.down)
        packed0 = scatter_rows(packed0)
        of0.down, of0.up = spread_start(of0.down, True), spread_start(of0.up, False)
        down_hop, up_hop, *rest = sync(
            of0.down[1],
            of0.up[1],
            *of1.packed,
            *of1.up,
            hidden0,
            hidden1,
            in_grads0,
            in_grads1,
        )
        of1.packed, of1.up = rest[:2], rest[2:4]
        hidden0, hidden1, in_grads0, in_grads1 = rest[4:]
        near0 = [
            None,
            spread_end((of0.up[0], up_hop), False),
            spread_end((of0.down[0], down_hop), True),
        ]
        near1 = [spread_end(of1.packed, False), spread_end(of1.up, False), of1.down]
    else:
        near1, near0 = reduce_plain(of1), reduce_plain(of0)

    def to_owner(layer0, layer1, away):
        pairs = [jnp.stack([runs[:half], far]) for runs, far in zip((layer0, layer1), away)]
        keep = jnp.where(first_core, pairs[0], pairs[1])
        take = swap_core(jnp.where(first_core, pairs[1], pairs[0]))
        both = flipped(~first_core, jnp.stack([keep, take], axis=1), 1)
        return flipped(~first_y, both, 0).reshape(2, block, width)

    hidden_out = to_owner(hidden0, hidden1, state.away)
    in_grads_out = to_owner(in_grads0, in_grads1, [swap_y(in_grads0[half:]), state.in_away])

    def natural(position):
        layers = jnp.stack(near0[position]), jnp.stack(near1[position])
        near = jnp.where(first_core, layers[0], layers[1])
        far = jnp.where(first_core, swap_core(layers[0]), swap_core(layers[1]))
        both = jnp.stack([near, far], axis=1)
        shape = both.shape
        both = both.reshape((2, 2, 2) + shape[2:])
        both = flipped(~first_y, flipped(~first_x, flipped(~first_core, both, 2), 1), 0)
        return both.reshape((8,) + shape[2:])

    rows_old = (row_qkv, row_out, row_up, row_down)
    if even:
        where = jnp.stack([at_eighth, core]).astype(jnp.int32)

        def build(position, kind, olds, extra, shapes):
            return assemble(
                near0[position],
                near1[position],
                [swap_core(value) for value in near0[position]],
                [swap_core(value) for value in near1[position]],
                olds,
                extra,
                where,
                kind,
                shapes,
            )

        def column(row):
            return row.reshape(-1, 1)

        down = build(2, ROWS, [column(row_down)], jnp.zeros((1, LANES), f32), ((8 * unit, width),))
        up = build(
            1, COLUMNS, [column(row_up)], state.weight_totals, ((rows, hidden_width),)
        )
        near0[0] = spread(after(packed0, up[1], down[1]), False)
        built = [None, None, up[:2], down[:2]]
        sums = {2: jnp.concatenate([up[2], down[2]], axis=1)}
        places = {2: (0, LANES), 3: (LANES + 2 * hidden_width, 2 * LANES + 2 * hidden_width)}
        places.update({0: (0, LANES), 1: (1, LANES + 6 * width)})

        def build_first():
            first = build(
                0,
                PACKED,
                [after(column(row_qkv), sums[2]), column(row_out)],
                jnp.concatenate([var_attn, var_mlp], axis=1),
                ((rows, 3 * width), (rows, width)),
            )
            built[:2] = (first[0], first[2]), (first[1], first[3])
            sums[0] = first[5]
            return first[4].reshape(2, rows)

    else:
        qkv = natural(0).reshape(8, rows, 3, LANES).transpose(1, 2, 0, 3).reshape(rows, 3 * width)
        out = natural(1).reshape(2, 4, rows + 16, width // 2).astype(f32).sum(axis=1)
        gain_shard = out[:, rows].sum(axis=0)[: 2 * rows].reshape(2, rows)
        out = out[:, :rows].transpose(1, 0, 2).reshape(rows, width)
        up = natural(2).reshape(8, rows, fsdp_count, unit).transpose(1, 2, 0, 3)
        up = up.reshape(rows, hidden_width)
        down = natural(3).reshape(8 * unit, width)
        built, parts = [], []
        for gradient, row_old in zip((qkv, out, up, down), rows_old):
            gradient = gradient.astype(f32)
            square = gradient * gradient
            row_new = decay_rate * row_old.reshape(-1, 1) + (1.0 - decay_rate) * jnp.mean(
                square, axis=1, keepdims=True
            )
            built.append((gradient, row_new))
            total_new = jnp.pad(jnp.sum(row_new).reshape(1, 1), ((0, 0), (0, LANES - 1)))
            parts.append(
                [
                    total_new,
                    jnp.sum(square, axis=0, keepdims=True),
                    jnp.sum(square / row_new, axis=0, keepdims=True),
                ]
            )
        blank = jnp.zeros_like(parts[0][0])
        sums = {
            2: jnp.concatenate(parts[2] + parts[3], axis=1),
            0: jnp.concatenate([blank] + parts[0] + parts[1], axis=1),
        }
        places = {2: (0, LANES), 3: (LANES + 2 * hidden_width, 2 * LANES + 2 * hidden_width)}
        places.update(
            {0: (LANES, 2 * LANES), 1: (2 * LANES + 6 * width, 3 * LANES + 6 * width)}
        )

        def build_first():
            return gain_shard

    def sum_line(value):
        if fsdp_count != 4:
            return lax.psum(value, FSDP)
        near, two, three = rotations(value)[1:]
        return (value + two) + (near + three)

    cols_old = (col_qkv, col_out, col_up, col_down)
    moments_old = (var_attn, var_mlp)
    new_rows, new_cols, ratios, new_masters = [None] * 4, [None] * 4, [None] * 4, [None] * 4

    def update(position, summed, weight_total):
        gradient, row_new = built[position]
        at_total, start = places[position]
        cols = gradient.shape[1]
        row_count = gradient.shape[0] * fsdp_count
        entry_count = row_count * cols
        col_all = summed[:, start : start + cols]
        ratio_all = summed[:, start + cols : start + 2 * cols]
        row_mean = summed[:, at_total : at_total + 1] / row_count
        new_rows[position] = row_new.reshape(1, -1)
        new_cols[position] = (
            decay_rate * cols_old[position] + (1.0 - decay_rate) * col_all / row_count
        )
        ratios[position] = jnp.sqrt(
            row_mean * total(ratio_all / new_cols[position]) / entry_count
        )
        weight_scale = jnp.sqrt(weight_total / entry_count + weight_eps)
        factor = step_rate * weight_scale / jnp.maximum(1.0, ratios[position] / clip_level)
        raw = gradient * lax.rsqrt(row_new * new_cols[position] / row_mean)
        new_masters[position] = masters[position] - factor * raw

    early = sum_line(with_lanes(sums[2], state.weight_totals))
    gain_shard = build_first()
    moments, gain_updates = [], []
    for gain_pos in range(2):
        grad = gain_shard[gain_pos : gain_pos + 1]
        moment = decay_rate * moments_old[gain_pos] + (1.0 - decay_rate) * grad * grad
        moments.append(moment)
        gain_updates.append(grad * lax.rsqrt(moment))
    last = with_lanes(sums[0], lanes([total(step * step) for step in gain_updates], 2))
    summed, early = sum_line(last), after(early, last)
    weight_all = [early[:, 2 + i : 3 + i] for i in range(6)]
    for position in (2, 3):
        update(position, early, weight_all[position])
    for position in (0, 1):
        update(position, summed, weight_all[position])
    for gain_pos in range(2):
        clip_ratio = jnp.sqrt(summed[:, 2 + gain_pos : 3 + gain_pos] / width)
        weight_scale = jnp.sqrt(weight_all[4 + gain_pos] / width + weight_eps)
        factor = step_rate * weight_scale / jnp.maximum(1.0, clip_ratio / clip_level)
        new_masters.append(gain_masters[gain_pos] - factor * gain_updates[gain_pos])
        ratios.append(clip_ratio)
    return (
        hidden_out[None],
        in_grads_out[None],
        *[entry[0][None] for entry in built],
        gain_shard[:1],
        gain_shard[1:],
        *[master[None] for master in new_masters[:4]],
        new_masters[4],
        new_masters[5],
        new_rows[0],
        new_cols[0],
        new_rows[1],
        new_cols[1],
        new_rows[2],
        new_cols[2],
        new_rows[3],
        new_cols[3],
        moments[0],
        moments[1],
        jnp.concatenate(ratios, axis=1),
    )


def solution(mesh):
    in_specs = (
        P(FSDP, CTX, None),
        P(FSDP, CTX, None),
        P(FSDP, None),
        P(SECTION, FSDP, None),
        P(SECTION, FSDP, None),
        P(SECTION, FSDP, None),
        P(SECTION, FSDP, None),
        P(SECTION, FSDP),
        P(SECTION, FSDP),
        P(SECTION, FSDP),
        P(SECTION, None),
        P(SECTION, FSDP),
        P(SECTION, None),
        P(SECTION, FSDP),
        P(SECTION, None),
        P(SECTION, FSDP),
        P(SECTION, None),
        P(SECTION, FSDP),
        P(SECTION, FSDP),
    )
    out_specs = (
        P(SECTION, FSDP, CTX, None),
        P(SECTION, FSDP, CTX, None),
        P(SECTION, FSDP, None),
        P(SECTION, FSDP, None),
        P(SECTION, FSDP, None),
        P(SECTION, FSDP, None),
        P(SECTION, FSDP),
        P(SECTION, FSDP),
        P(SECTION, FSDP, None),
        P(SECTION, FSDP, None),
        P(SECTION, FSDP, None),
        P(SECTION, FSDP, None),
        P(SECTION, FSDP),
        P(SECTION, FSDP),
        P(SECTION, FSDP),
        P(SECTION, None),
        P(SECTION, FSDP),
        P(SECTION, None),
        P(SECTION, FSDP),
        P(SECTION, None),
        P(SECTION, FSDP),
        P(SECTION, None),
        P(SECTION, FSDP),
        P(SECTION, FSDP),
        P(SECTION, None),
    )
    return jax.shard_map(
        per_device, mesh=mesh, in_specs=in_specs, out_specs=out_specs, check_vma=False
    )
```

```python
import functools
import types

import jax
import jax.numpy as jnp
from jax import lax
from jax.experimental import pallas as pl
from jax.experimental.pallas import tpu as pltpu
from jax.sharding import PartitionSpec as P

HEADS = 16


decay_rate = 0.5
clip_level = 0.5
step_rate = 1.0
norm_eps = 1e-05
weight_eps = 1e-06
mask_fill = -1e30

bf16 = jnp.bfloat16
f32 = jnp.float32
LANES = 128
SECTION, CTX, FSDP = "section", "ctx", "fsdp"
ROWS, COLUMNS, PACKED = range(3)


def swap_core(value):
    return lax.ppermute(value, SECTION, [(0, 1), (1, 0)])


def swap_x(value):
    return lax.ppermute(value, CTX, [(i, i ^ 1) for i in range(4)])


def swap_y(value):
    return lax.ppermute(value, CTX, [(i, i ^ 2) for i in range(4)])


def dot(left, right):
    return jnp.dot(left, right, preferred_element_type=f32)


def times_transposed(left, right):
    return lax.dot_general(left, right, (((1,), (1,)), ((), ())), preferred_element_type=f32)


def rows_product(left, right):
    return lax.dot_general(left, right, (((0,), (0,)), ((), ())), preferred_element_type=f32)


def after(value, *tokens):
    return lax.optimization_barrier((value, *tokens))[0]


def with_core(value):
    return jnp.concatenate([value, swap_core(value)], axis=0)


def gather_tiles(value):
    return [with_core(value), with_core(swap_x(value))]


def fold_core(partial):
    rows = partial.shape[0] // 2
    partial = partial.astype(bf16)
    return partial[:rows].astype(f32) + swap_core(partial[rows:]).astype(f32)


(SEND, ATTEND0, ATTEND1, STACKED, LAST, NORM, FEED0, FEED1, OUT) = range(9)


def norm_parts(values):
    center = values - jnp.mean(values, axis=-1, keepdims=True)
    spread = jnp.mean(center * center, axis=-1, keepdims=True)
    scale = lax.rsqrt(spread + norm_eps)
    return center * scale, scale


def norm_back(out_grad, unit, scale, gain):
    scaled = out_grad * gain
    mean_scaled = jnp.mean(scaled, axis=-1, keepdims=True)
    mean_unit = jnp.mean(scaled * unit, axis=-1, keepdims=True)
    return scale * (scaled - mean_scaled - unit * mean_unit), jnp.sum(out_grad * unit, axis=0)


def nt(left, right):
    return lax.dot_general(left, right, (((1,), (1,)), ((), ())), preferred_element_type=f32)


def attention_kernel(q_ref, k_ref, v_ref, qid_ref, kid_ref, out_ref, lse_ref, *, scale):
    queries = q_ref[...] * jnp.asarray(scale, bf16)
    keys, values_t = k_ref[...], v_ref[...].T
    same = kid_ref[...] == qid_ref[...]
    first = lax.broadcasted_iota(jnp.int32, queries.shape, 1) < queries.shape[1] // 2
    parts = []
    for head in range(2):
        own = jnp.where(first if head == 0 else ~first, queries, jnp.zeros_like(queries))
        scores = jnp.where(same, nt(keys, own), mask_fill)
        peak = jnp.max(scores, axis=0, keepdims=True)
        weights = jnp.exp(scores - peak)
        total = jnp.sum(weights, axis=0, keepdims=True)
        lse_ref[0, head : head + 1, :] = peak + jnp.log(total)
        parts.append(dot(values_t, weights.astype(bf16)) * (1.0 / total))
    width = values_t.shape[0] // 2
    stacked = jnp.concatenate([parts[0][:width], parts[1][width:]], axis=0)
    out_ref[...] = stacked.T.astype(bf16)


def attention_forward(projected, keys_values, query_ids, key_ids, scale):
    rows, seq_len = projected.shape[0], keys_values.shape[0]
    tile = min(256, rows)
    elems = 4 * rows * seq_len
    return pl.pallas_call(
        functools.partial(attention_kernel, scale=scale),
        grid=(2, rows // tile),
        in_specs=[
            pl.BlockSpec((tile, LANES), lambda p, i: (i, 3 * p)),
            pl.BlockSpec((seq_len, LANES), lambda p, i: (0, 3 * p + 1)),
            pl.BlockSpec((seq_len, LANES), lambda p, i: (0, 3 * p + 2)),
            pl.BlockSpec((1, tile), lambda p, i: (0, i)),
            pl.BlockSpec((seq_len, 1), lambda p, i: (0, 0)),
        ],
        out_specs=[
            pl.BlockSpec((tile, LANES), lambda p, i: (i, p)),
            pl.BlockSpec((1, 2, tile), lambda p, i: (p, 0, i)),
        ],
        out_shape=[
            jax.ShapeDtypeStruct((rows, 2 * LANES), bf16),
            jax.ShapeDtypeStruct((2, 2, rows), f32),
        ],
        compiler_params=pltpu.CompilerParams(vmem_limit_bytes=32 << 20),
        cost_estimate=pl.CostEstimate(
            flops=elems * 4 * 128, bytes_accessed=4 << 20, transcendentals=elems
        ),
    )(projected, keys_values, keys_values, query_ids, key_ids)


def attention_back_kernel(
    q_ref, k_ref, v_ref, g_ref, lse_ref, qid_ref, kid_ref, *refs, scale, last
):
    queries = q_ref[...] * jnp.asarray(scale, bf16)
    keys, values, grads = k_ref[...], v_ref[...], g_ref[...]
    keys_t = keys.T
    same = kid_ref[...] == qid_ref[...]
    first = lax.broadcasted_iota(jnp.int32, queries.shape, 1) < queries.shape[1] // 2
    step = pl.program_id(1)
    if last:
        early_q, early_k, early_v, out_ref, dk_ref, dv_ref = refs
    else:
        dq_ref, dk_ref, dv_ref = refs

    @pl.when(step == 0)
    def _():
        dk_ref[...] = early_k[...] if last else jnp.zeros_like(dk_ref)
        dv_ref[...] = early_v[...] if last else jnp.zeros_like(dv_ref)

    parts = []
    for head in range(2):
        mine = first if head == 0 else ~first
        own = jnp.where(mine, queries, jnp.zeros_like(queries))
        own_grads = jnp.where(mine, grads, jnp.zeros_like(grads))
        scores = jnp.where(same, nt(keys, own), mask_fill)
        weights = jnp.exp(scores - lse_ref[0, head : head + 1, :])
        prob_grad = nt(values, own_grads)
        row_dot = jnp.sum(weights * prob_grad, axis=0, keepdims=True)
        score_grad = (weights * (prob_grad - row_dot)).astype(bf16)
        dv_ref[...] += dot(weights.astype(bf16), own_grads)
        dk_ref[...] += dot(score_grad, own)
        parts.append(dot(keys_t, score_grad))
    width = keys_t.shape[0] // 2
    stacked = jnp.concatenate([parts[0][:width], parts[1][width:]], axis=0)
    query_grad = (stacked.T * scale).astype(bf16)
    if not last:
        dq_ref[...] = query_grad
        return
    early, tile = early_q.shape[0], query_grad.shape[0]
    start = pl.multiple_of(early + step * tile, tile)
    out_ref[pl.ds(start, tile), :LANES] = query_grad

    @pl.when(step == pl.num_programs(1) - 1)
    def _():
        out_ref[:early, :LANES] = early_q[...]
        out_ref[:, LANES : 2 * LANES] = dk_ref[...].astype(bf16)
        out_ref[:, 2 * LANES :] = dv_ref[...].astype(bf16)


def attention_backward(projected, keys_values, grads, lse, query_ids, key_ids, scale, early=None):
    rows, seq_len = projected.shape[0], keys_values.shape[0]
    tile = min(256, rows)
    elems = 4 * rows * seq_len

    def column(size):
        return pl.BlockSpec((size, LANES), lambda p, i: (0, p))

    in_specs = [
        pl.BlockSpec((tile, LANES), lambda p, i: (i, 3 * p)),
        pl.BlockSpec((seq_len, LANES), lambda p, i: (0, 3 * p + 1)),
        pl.BlockSpec((seq_len, LANES), lambda p, i: (0, 3 * p + 2)),
        pl.BlockSpec((tile, LANES), lambda p, i: (i, p)),
        pl.BlockSpec((1, 2, tile), lambda p, i: (p, 0, i)),
        pl.BlockSpec((1, tile), lambda p, i: (0, i)),
        pl.BlockSpec((seq_len, 1), lambda p, i: (0, 0)),
    ]
    if early is None:
        out_specs = [pl.BlockSpec((tile, LANES), lambda p, i: (i, p))] + [column(seq_len)] * 2
        out_shape = [
            jax.ShapeDtypeStruct((rows, 2 * LANES), bf16),
            jax.ShapeDtypeStruct((seq_len, 2 * LANES), f32),
            jax.ShapeDtypeStruct((seq_len, 2 * LANES), f32),
        ]
        scratch = []
    else:
        in_specs += [column(early[0].shape[0]), column(seq_len), column(seq_len)]
        out_specs = pl.BlockSpec((seq_len, 3 * LANES), lambda p, i: (0, p))
        out_shape = jax.ShapeDtypeStruct((seq_len, 6 * LANES), bf16)
        scratch = [pltpu.VMEM((seq_len, LANES), f32)] * 2
    return pl.pallas_call(
        functools.partial(attention_back_kernel, scale=scale, last=early is not None),
        grid=(2, rows // tile),
        in_specs=in_specs,
        out_specs=out_specs,
        out_shape=out_shape,
        scratch_shapes=scratch,
        compiler_params=pltpu.CompilerParams(vmem_limit_bytes=32 << 20),
        cost_estimate=pl.CostEstimate(
            flops=elems * 10 * 128, bytes_accessed=6 << 20, transcendentals=elems
        ),
    )(projected, keys_values, keys_values, grads, lse, query_ids, key_ids, *(early or ()))


def weight_grad_kernel(*refs, lefts, rights):
    outs = refs[-lefts * rights :]
    for i in range(lefts):
        turned = [refs[2 * i + k][...].T for k in range(2)]
        for j in range(rights):
            at = 2 * lefts + 2 * j
            total = dot(turned[0], refs[at][...]) + dot(turned[1], refs[at + 1][...])
            outs[i * rights + j][...] = total.astype(bf16)


def weight_grad(lefts, rights):
    size = lefts[0][0].shape[1]
    depth = lefts[0][0].shape[0]
    tile = min(256, size)
    operands, specs, outs = [], [], []
    for pair in lefts:
        for value in pair:
            operands.append(value)
            specs.append(pl.BlockSpec((depth, tile), lambda i: (0, i)))
    for pair, cols, at in rights:
        for value, row in pair:
            operands.append(value)
            specs.append(pl.BlockSpec((depth, cols), lambda i, row=row, at=at: (row, at)))
    for _ in lefts:
        outs += [jax.ShapeDtypeStruct((size, cols), bf16) for _, cols, _ in rights]
    columns = sum(cols for _, cols, _ in rights)
    return pl.pallas_call(
        functools.partial(weight_grad_kernel, lefts=len(lefts), rights=len(rights)),
        grid=(size // tile,),
        in_specs=specs,
        out_specs=[pl.BlockSpec((tile, out.shape[1]), lambda i: (i, 0)) for out in outs],
        out_shape=outs,
        compiler_params=pltpu.CompilerParams(vmem_limit_bytes=32 << 20),
        cost_estimate=pl.CostEstimate(
            flops=4 * depth * size * len(lefts) * columns,
            bytes_accessed=4 * depth * (size * len(lefts) + columns),
            transcendentals=0,
        ),
    )(*operands)


def whole(shape):
    return pl.BlockSpec(shape, lambda *_: (0,) * len(shape))


def cut_kernel(_, *refs, width):
    first, up, down = refs[:16], refs[16:24], refs[24:26]
    packed, far, ups, downs = refs[26:28], refs[28:30], refs[30:32], refs[32:34]
    rows = first[0].shape[1]
    for core in range(2):
        for i in range(3):
            lanes = slice(LANES * i, LANES * (i + 1))
            packed[core][:rows, lanes] = first[3 * core + i][0].astype(bf16)
            far[core][:, lanes] = first[6 + 3 * core + i][0].astype(bf16)
        out = first[12 + core][0].astype(bf16)
        packed[core][:LANES, 3 * LANES :] = out[:, :LANES]
        packed[core][LANES:rows, 3 * LANES :] = out[:, LANES:]
        gains = jnp.concatenate([first[14][...], first[15][...]], axis=1)
        top = lax.broadcasted_iota(jnp.int32, (16, 2 * rows), 0) == 0
        gains = jnp.where(top, jnp.broadcast_to(gains, (16, 2 * rows)), 0.0)
        packed[core][rows:, :] = gains.astype(bf16)
        for i in range(4):
            ups[core][:, LANES * i : LANES * (i + 1)] = up[4 * core + i][0].astype(bf16)
        downs[core][...] = down[core][0].astype(bf16)


def cut_weights(w_qkv, w_out, w_up, w_down, gain_attn, gain_mlp, at_eighth):
    rows, width = w_qkv.shape[1], w_out.shape[2]

    def column(i, flip):
        return pl.BlockSpec((1, rows, LANES), lambda g, at: (0, 0, 8 * i + (at[0] ^ flip)))

    specs = [column(i, flip) for flip in (0, 1, 4, 5) for i in range(3)]
    specs += [
        pl.BlockSpec(
            (1, LANES, 2 * LANES), lambda g, at, c=core: (0, (at[0] & 1) ^ c, at[0] >> 1)
        )
        for core in range(2)
    ]
    specs += [whole(gain_attn.shape), whole(gain_mlp.shape)]
    specs += [column(i, core) for core in range(2) for i in range(4)]
    specs += [
        pl.BlockSpec((1, LANES, width), lambda g, at, c=core: (0, at[0] ^ c, 0))
        for core in range(2)
    ]
    outs = [
        jax.ShapeDtypeStruct(shape, bf16)
        for shape in (
            (rows + 16, 4 * LANES),
            (rows, 3 * LANES),
            (rows, 4 * LANES),
            (LANES, width),
        )
        for _ in range(2)
    ]
    operands = [w_qkv] * 12 + [w_out] * 2 + [gain_attn, gain_mlp] + [w_up] * 8 + [w_down] * 2
    return pl.pallas_call(
        functools.partial(cut_kernel, width=width),
        grid_spec=pltpu.PrefetchScalarGridSpec(
            num_scalar_prefetch=1,
            grid=(1,),
            in_specs=specs,
            out_specs=[whole(out.shape) for out in outs],
        ),
        out_shape=outs,
        compiler_params=pltpu.CompilerParams(vmem_limit_bytes=56 << 20),
    )(at_eighth, *operands)


def place_qkv_kernel(at, *refs, fixed):
    out_ref = refs[-1]
    rows, cols = refs[4].shape
    for k in range(4):
        slot = k if fixed else lax.rem(at[0] + 4 - k, 4)
        part = pl.ds(pl.multiple_of(slot * rows, rows), rows)
        out_ref[part, :cols] = refs[k][:rows, :cols]
        out_ref[part, cols:] = refs[4 + k][...]


def place_out_kernel(at, *refs, fixed):
    out_ref, gain_ref = refs[-2:]
    rows, cols = refs[0].shape[0] - 16, refs[0].shape[1] - LANES
    for k in range(4):
        slot = k if fixed else lax.rem(at[0] + 4 - k, 4)
        packed = refs[k]
        away = slot ^ at[1]
        away = 2 * (away & 1) + (away >> 1)
        out_ref[away, :, :LANES] = packed[:LANES, cols:]
        out_ref[away, :, LANES:] = packed[LANES:rows, cols:]
        part = pl.ds(pl.multiple_of(slot * rows, rows), rows)
        gains = packed[rows:, :].astype(f32)
        gain_ref[0:1, part] = gains[0:1, :rows]
        gain_ref[1:2, part] = gains[0:1, rows:]


def place(kernel, operands, shapes, outs, at, fixed):
    specs = [
        pl.BlockSpec(shape, (lambda g, at, k=k: (k, 0)) if fixed else (lambda g, at: (0, 0)))
        for shape in shapes
        for k in range(4)
    ]
    if fixed:
        operands = [value for value in operands for _ in range(4)]
    return pl.pallas_call(
        functools.partial(kernel, fixed=fixed),
        grid_spec=pltpu.PrefetchScalarGridSpec(
            num_scalar_prefetch=1,
            grid=(1,),
            in_specs=specs,
            out_specs=[whole(out.shape) for out in outs],
        ),
        out_shape=outs,
        compiler_params=pltpu.CompilerParams(vmem_limit_bytes=24 << 20),
    )(at, *operands)


def small_call(kernel, at, operands, outs, room=40):
    return pl.pallas_call(
        kernel,
        grid_spec=pltpu.PrefetchScalarGridSpec(
            num_scalar_prefetch=1,
            grid=(1,),
            in_specs=[whole(value.shape) for value in operands],
            out_specs=[whole(out.shape) for out in outs],
        ),
        out_shape=outs,
        compiler_params=pltpu.CompilerParams(vmem_limit_bytes=room << 20),
    )(at, *operands)


def join_out_kernel(at, keep, came, far_keep, far_came, out_ref):
    for b in range(2):
        rows = slice(LANES * b, LANES * (b + 1))
        for away, value in enumerate((keep[b], came[b], far_keep[1 - b], far_came[1 - b])):
            size = value.shape[1]
            start = pl.multiple_of((at[0] ^ away) * size, size)
            out_ref[rows, pl.ds(start, size)] = value


def fold_out_kernel(at, keep, came, near_ref, give_ref):
    size = near_ref.shape[2]
    first_x = (at[0] & 1) == 0
    for b in range(2):
        value = keep[b].astype(f32) + came[1 - b].astype(f32)
        low, high = value[:, :size], value[:, size:]
        near_ref[b] = jnp.where(first_x, low, high).astype(bf16)
        give_ref[b] = jnp.where(first_x, high, low).astype(bf16)


def pack_kernel(at, keep, came, near, cross, gains, out_ref):
    cols = keep.shape[1]
    rows = keep.shape[0] // 4
    top = lax.broadcasted_iota(jnp.int32, (16, 2 * rows), 0) == 0
    for f in range(4):
        base = f * (rows + 16)
        part = slice(rows * f, rows * (f + 1))
        out_ref[base : base + rows, :cols] = (
            keep[part, :].astype(f32) + came[part, :].astype(f32)
        ).astype(bf16)
        gain = jnp.concatenate([gains[0:1, part], gains[1:2, part]], axis=1)
        gain = jnp.where(top, jnp.broadcast_to(gain, (16, 2 * rows)), 0.0)
        out_ref[base + rows : base + rows + 16, :] = gain.astype(bf16)
    for away, value in enumerate((near[0], cross[0], near[1], cross[1])):
        base = (at[0] ^ away) * (rows + 16)
        for half in range(2):
            start = pl.multiple_of(base + LANES * half, 16)
            out_ref[pl.ds(start, LANES), cols:] = value[:, LANES * half : LANES * (half + 1)]


def assemble_kernel(at, *refs, kind, shapes):
    groups = [refs[4 * i : 4 * i + 4] for i in range(4)]
    rows_old = refs[16 : 16 + len(shapes)]
    extra = refs[16 + len(shapes)]
    outs = refs[17 + len(shapes) :]
    grads, rows_new, sums_ref = outs[: len(shapes)], outs[len(shapes) : 2 * len(shapes)], outs[-1]
    first_core = at[1] == 0
    gain = 0.0
    for core in range(2):
        for chip in range(4):
            eighth = (2 * chip + core) ^ at[0]
            value = jnp.where(first_core, groups[core][chip][...], groups[2 + core][chip][...])
            value = value.astype(f32)
            if kind == ROWS:
                rows = value.shape[0]
                grads[0][pl.ds(pl.multiple_of(eighth * rows, rows), rows), :] = value
            elif kind == COLUMNS:
                for i in range(value.shape[1] // LANES):
                    start = pl.multiple_of((8 * i + eighth) * LANES, LANES)
                    grads[0][:, pl.ds(start, LANES)] = value[:, LANES * i : LANES * (i + 1)]
            else:
                rows = shapes[0][0]
                for i in range(3):
                    start = pl.multiple_of((8 * i + eighth) * LANES, LANES)
                    grads[0][:, pl.ds(start, LANES)] = value[:rows, LANES * i : LANES * (i + 1)]
                part = pl.ds(pl.multiple_of((eighth & 1) * LANES, LANES), LANES)
                for half in range(2):
                    start = pl.multiple_of((2 * (eighth >> 1) + half) * LANES, LANES)
                    block = value[half * LANES : (half + 1) * LANES, 3 * LANES :]
                    grads[1][part, pl.ds(start, LANES)] = block
                gain = gain + value[rows : rows + 1, :]
    lane = lax.broadcasted_iota(jnp.int32, (1, LANES), 1)
    sums_ref[...] = jnp.zeros_like(sums_ref)
    if kind == PACKED:
        outs[-2][...] = gain
        moment = decay_rate * extra[...] + (1.0 - decay_rate) * gain * gain
        square = (gain * lax.rsqrt(moment)) ** 2
        middle = square.shape[1] // 2
        attn_total = jnp.sum(square[:, :middle], axis=1, keepdims=True)
        mlp_total = jnp.sum(square[:, middle:], axis=1, keepdims=True)
        sums_ref[:, :LANES] = jnp.where(lane == 2, attn_total, jnp.where(lane == 3, mlp_total, 0.0))
    else:
        sums_ref[:, :LANES] = extra[...]
    begin = LANES
    for index, (total_rows, cols) in enumerate(shapes):
        grad_ref, row_ref, new_ref = grads[index], rows_old[index], rows_new[index]
        col_part = slice(begin, begin + cols)
        ratio_part = slice(begin + cols, begin + 2 * cols)
        begin += 2 * cols

        def body(i, total):
            part = pl.ds(pl.multiple_of(i * 64, 64), 64)
            values = grad_ref[part, :]
            square = values * values
            row_new = decay_rate * row_ref[part, :] + (1.0 - decay_rate) * (
                jnp.sum(square, axis=1, keepdims=True) / cols
            )
            new_ref[part, :] = row_new
            sums_ref[:, col_part] += jnp.sum(square, axis=0, keepdims=True)
            sums_ref[:, ratio_part] += jnp.sum(square * (1.0 / row_new), axis=0, keepdims=True)
            return total + jnp.sum(row_new, axis=0, keepdims=True)

        total = lax.fori_loop(0, total_rows // 64, body, jnp.zeros((1, 1), f32))
        sums_ref[:, :LANES] += jnp.where(lane == index, total, 0.0)


def assemble(near0, near1, far0, far1, rows_old, extra, where, kind, shapes):
    outs = [jax.ShapeDtypeStruct(shape, f32) for shape in shapes]
    outs += [jax.ShapeDtypeStruct((shape[0], 1), f32) for shape in shapes]
    if kind == PACKED:
        outs.append(jax.ShapeDtypeStruct((1, near0[0].shape[1]), f32))
    outs.append(
        jax.ShapeDtypeStruct((1, LANES + 2 * sum(shape[1] for shape in shapes)), f32)
    )
    return small_call(
        functools.partial(assemble_kernel, kind=kind, shapes=shapes),
        where,
        [*near0, *far0, *near1, *far1, *rows_old, extra],
        outs,
        56,
    )


def per_device(
    tokens,
    cotangent,
    segment_ids,
    w_qkv,
    w_out,
    w_up,
    w_down,
    gain_attn,
    gain_mlp,
    row_qkv,
    col_qkv,
    row_out,
    col_out,
    row_up,
    col_up,
    row_down,
    col_down,
    var_attn,
    var_mlp,
):
    core = lax.axis_index(SECTION)
    chip = lax.axis_index(CTX)
    depth = lax.axis_index(FSDP)
    y, x = chip // 2, chip % 2
    fsdp_count = lax.axis_size(FSDP)
    assert lax.axis_size(SECTION) == 2 and lax.axis_size(CTX) == 4
    _, block, width = tokens.shape
    half = block // 2
    rows = w_qkv.shape[1]
    hidden_width = w_up.shape[2]
    unit = hidden_width // fsdp_count // 8
    scale = (width // HEADS) ** (-0.5)
    even = fsdp_count == 4 and rows == 2 * LANES and unit == LANES
    first_core, first_y, first_x = core == 0, y == 0, x == 0

    def flipped(when, value, axis=0):
        low, high = jnp.split(value, 2, axis)
        return jnp.where(when, jnp.concatenate([high, low], axis), value)

    at_eighth = 2 * chip + core

    def eighth(e):
        qkv = lax.dynamic_index_in_dim(w_qkv[0].reshape(rows, 3, 8, LANES), e, 2, keepdims=False)
        up = lax.dynamic_index_in_dim(
            w_up[0].reshape(rows, fsdp_count, 8, unit), e, 2, keepdims=False
        )
        down = lax.dynamic_slice_in_dim(w_down[0], e * unit, unit, 0)
        return [
            part.astype(bf16)
            for part in (qkv.reshape(rows, 3 * LANES), up.reshape(rows, fsdp_count * unit), down)
        ]

    def by_layer(mine, other):
        taken = swap_core(other)
        return jnp.where(first_core, mine, taken), jnp.where(first_core, taken, mine)

    def gather_rows(value):
        return lax.all_gather(value, FSDP, axis=0, tiled=True)

    def rotations(value):
        return [value] + [
            lax.ppermute(
                value, FSDP, [(i, (i + k) % fsdp_count) for i in range(fsdp_count)]
            )
            for k in range(1, fsdp_count)
        ]

    def with_far(value):
        return value, swap_y(value)

    chip_array = chip.reshape(1).astype(jnp.int32)

    def out_parts(columns):
        keep, came = columns[:2], swap_x(columns[2:])
        return [keep, came, swap_y(keep), swap_y(came)]

    def join_out(parts):
        out = jax.ShapeDtypeStruct((2 * LANES, width), bf16)
        return small_call(join_out_kernel, chip_array, parts, [out])[0]

    weights, gains = [types.SimpleNamespace(), types.SimpleNamespace()], [None, None]
    depth_array = jnp.stack([depth, chip]).astype(jnp.int32)
    if even:
        cuts = cut_weights(
            w_qkv, w_out, w_up, w_down, gain_attn, gain_mlp, at_eighth.reshape(1).astype(jnp.int32)
        )
        packed_parts = by_layer(*cuts[:2])
        far_parts = by_layer(*cuts[2:4])
        up_parts = by_layer(*cuts[4:6])
        down_parts = by_layer(*cuts[6:])
        turns = rotations(packed_parts[0])
        fars = [swap_y(value[:rows, : 3 * LANES]) for value in turns[1:]]

        def place_qkv(packed, far, fixed):
            shapes = ((rows + 16, 4 * LANES), (rows, 3 * LANES))
            out = jax.ShapeDtypeStruct((4 * rows, 6 * LANES), bf16)
            return place(place_qkv_kernel, [*packed, *far], shapes, [out], depth_array, fixed)[0]

        def place_out(packed, fixed):
            outs = [
                jax.ShapeDtypeStruct((4, LANES, 2 * LANES), bf16),
                jax.ShapeDtypeStruct((2, 4 * rows), f32),
            ]
            shapes = ((rows + 16, 4 * LANES),)
            columns, gain = place(place_out_kernel, packed, shapes, outs, depth_array, fixed)
            return out_parts(columns), gain

        weights[0].qkv = place_qkv(turns, [far_parts[0]] + fars, False)
        weights[0].out, gains[0] = place_out(turns, False)
        up_gathered = [gather_rows(after(up_parts[0], *turns[1:])), gather_rows(up_parts[1])]
        down_gathered = [gather_rows(after(down_parts[0], *turns[1:])), gather_rows(down_parts[1])]
        packed_gathered = gather_rows(packed_parts[1])
    else:
        mine_parts, other_parts = eighth(at_eighth), eighth(at_eighth ^ 1)
        qkv_parts, up_parts, down_parts = [by_layer(a, b) for a, b in zip(mine_parts, other_parts)]
        whole_out = gather_rows(w_out[0].astype(bf16))
        out_parts = by_layer(whole_out, whole_out)
        gains_own = lax.all_gather(
            jnp.concatenate([gain_attn, gain_mlp], axis=0).astype(bf16), FSDP, axis=1, tiled=True
        )
        gains = [part.astype(f32) for part in by_layer(gains_own, gains_own)]
        for layer in range(2):
            blocks = out_parts[layer].reshape(4, 2, LANES, width)
            blocks = lax.dynamic_index_in_dim(blocks, core, 1, keepdims=False)
            weights[layer] = types.SimpleNamespace(
                qkv=jnp.concatenate(with_far(gather_rows(qkv_parts[layer])), axis=1),
                out=jnp.concatenate(
                    [
                        lax.dynamic_index_in_dim(blocks, chip, 0, keepdims=False),
                        lax.dynamic_index_in_dim(blocks, chip ^ 2, 0, keepdims=False),
                    ],
                    axis=0,
                ),
                up=with_far(gather_rows(up_parts[layer])),
                down=with_far(gather_rows(down_parts[layer])),
            )

    def own_rows(value):
        near = lax.dynamic_slice(value, (y, core * half, 0), (1, half, width))[0]
        away = lax.dynamic_slice(value, (1 - y, core * half, 0), (1, half, width))[0]
        return jnp.concatenate([near, swap_y(away)], axis=0)

    ids = lax.dynamic_index_in_dim(segment_ids, y, 0, keepdims=False).reshape(2, 2, 2, half)
    ids = flipped(~first_y, flipped(~first_x, flipped(~first_core, ids, 2), 1), 0)
    ids = ids.transpose(1, 2, 0, 3)
    key_ids = ids.reshape(8 * half, 1)
    query_ids = [ids[k].reshape(1, 4 * half) for k in range(2)]

    def forward(inputs, layer, hook):
        held = weights[layer]
        attn_gain, mlp_gain = gains[layer][0], gains[layer][1]
        inputs_all = gather_tiles(inputs)
        projected = [dot(value, held.qkv).astype(bf16) for value in inputs_all]
        keys_values = jnp.concatenate(projected, axis=0)

        def attend(k, queries):
            context, lse = attention_forward(queries, keys_values, query_ids[k], key_ids, scale)
            context = hook(OUT, context) if k == 1 else context
            return context, lse, fold_core(dot(context, held.out))

        context1, lse1, across = attend(1, hook(ATTEND0, projected[1]))
        across = across.astype(bf16)
        context0, lse0, keep = attend(0, hook(ATTEND1, after(projected[0], across)))
        came = hook(NORM, after(swap_x(across), keep))
        unit_attn, scale_attn = norm_parts(inputs.astype(f32) + keep + came.astype(f32))
        normed = unit_attn * attn_gain
        normed_all = gather_tiles(normed.astype(bf16))

        def feed(value):
            activated, slope, partial = [], [], 0.0
            for half_up, half_down in zip(held.up, held.down):
                upward = dot(value, half_up)
                phi_whole = 0.5 * (1.0 + lax.erf(upward * (0.5**0.5)))
                activated.append((upward * phi_whole).astype(bf16))
                density = jnp.exp(-0.5 * upward * upward) * 0.3989422804014327
                slope.append((phi_whole + upward * density).astype(bf16))
                partial += dot(activated[-1], half_down)
            return activated, slope, fold_core(partial)

        activated0, slope0, keep = feed(hook(FEED0, normed_all[0]))
        activated1, slope1, across = feed(hook(FEED1, after(normed_all[1], keep)))
        came = hook(LAST, swap_x(hook(SEND, across.astype(bf16))))
        unit_mlp, scale_mlp = norm_parts(normed + keep + came.astype(f32))
        return (unit_mlp * mlp_gain).astype(bf16), types.SimpleNamespace(
            inputs_all=inputs_all,
            projected=projected,
            keys_values=keys_values,
            context=(context0, context1),
            lse=(lse0, lse1),
            unit_attn=unit_attn,
            scale_attn=scale_attn,
            normed_all=normed_all,
            activated=(activated0, activated1),
            slope=(slope0, slope1),
            unit_mlp=unit_mlp,
            scale_mlp=scale_mlp,
        )

    def backward(out_grads, kept, layer, hook):
        held = weights[layer]
        attn_gain, mlp_gain = gains[layer][0], gains[layer][1]

        def both(pair):
            return [(value, 0) for value in pair]

        mlp_in, mlp_gain_grad = norm_back(
            out_grads.astype(f32), kept.unit_mlp, kept.scale_mlp, mlp_gain
        )
        down_all = gather_tiles(mlp_in.astype(bf16))

        def feed_back(k, value):
            grads, partial = [], 0.0
            for half_up, half_down, slope in zip(held.up, held.down, kept.slope[k]):
                grad = times_transposed(value, half_down) * slope.astype(f32)
                grads.append(grad.astype(bf16))
                partial += times_transposed(grads[-1], half_up)
            return grads, fold_core(partial)

        upward0, keep = feed_back(0, hook(FEED0, down_all[0]))
        upward1, across = feed_back(1, hook(FEED1, after(down_all[1], keep)))
        grad_down = weight_grad(list(zip(*kept.activated)), [(both(down_all), width, 0)])
        came = hook(NORM, swap_x(across.astype(bf16)), grad_down)
        attn_in, attn_gain_grad = norm_back(
            mlp_in + keep + came.astype(f32), kept.unit_attn, kept.scale_attn, attn_gain
        )
        branch_all = gather_tiles(attn_in.astype(bf16))

        def attend_back(k, value, early=None):
            grads = times_transposed(value, held.out).astype(bf16)
            return attention_backward(
                kept.projected[k],
                kept.keys_values,
                grads,
                kept.lse[k],
                query_ids[k],
                key_ids,
                scale,
                early,
            )

        grad_up = weight_grad(
            [kept.normed_all],
            [(both(right), right[0].shape[1], 0) for right in zip(upward0, upward1)],
        )
        early = attend_back(0, hook(ATTEND0, branch_all[0], grad_up))
        stacked = attend_back(1, hook(ATTEND1, after(branch_all[1], early[0])), early)
        gain_grads = jnp.stack([attn_gain_grad, mlp_gain_grad])
        (grad_out,) = weight_grad([kept.context], [(both(branch_all), width, 0)])
        stacked = hook(STACKED, stacked, grad_out, gain_grads)
        tile = 4 * half
        across = fold_core(times_transposed(stacked[tile:], held.qkv)).astype(bf16)
        across = hook(SEND, across)
        keep = fold_core(times_transposed(after(stacked, across)[:tile], held.qkv))
        came = hook(LAST, after(swap_x(across), keep))
        tiles = [(stacked, 0), (stacked, 1)]
        grad_qkv = weight_grad([kept.inputs_all], [(tiles, 3 * LANES, at) for at in range(2)])
        return (attn_in + keep + came.astype(f32)).astype(bf16), grad_qkv

    def scatter_rows(value):
        return lax.psum_scatter(value, FSDP, scatter_dimension=0, tiled=True)

    def sync(value, *others):
        return lax.optimization_barrier((value, *others))

    def fold(keep, came):
        return (keep.astype(f32) + came.astype(f32)).astype(bf16)

    def halves(grad):
        return grad[0], swap_y(grad[1])

    def out_halves(grad_out):
        size = width // 2
        keep = lax.dynamic_slice_in_dim(grad_out, y * size, size, 1)
        give = lax.dynamic_slice_in_dim(grad_out, (1 - y) * size, size, 1)
        return keep.reshape(2, LANES, size), swap_y(give.reshape(2, LANES, size))

    def out_pair(keep, came):
        out = jax.ShapeDtypeStruct((2, LANES, 2 * LANES), bf16)
        near, give = small_call(fold_out_kernel, chip_array, [keep, came], [out, out])
        return near, swap_x(give)

    def pack(keep, came, near, cross, gain_grads):
        out = jax.ShapeDtypeStruct((4 * (rows + 16), 4 * LANES), bf16)
        operands = [keep, came, near, cross, gain_grads]
        return small_call(pack_kernel, chip_array, operands, [out])[0]

    def spread_start(value, y_first):
        return value, (swap_y if y_first else swap_x)(value)

    def spread_end(pair, y_first):
        value, first = pair
        if y_first:
            return [value, swap_x(value), first, swap_x(first)]
        return [value, first, swap_y(value), swap_y(first)]

    def spread(value, y_first):
        return spread_end(spread_start(value, y_first), y_first)

    def reduce_plain(found):
        keep, came = out_halves(found.out)
        both = fold(keep, came[::-1])
        placed = jnp.zeros((4, 2, LANES, width // 2), bf16)
        placed = lax.dynamic_update_slice(placed, both[:1, None], (chip, core, 0, 0))
        placed = lax.dynamic_update_slice(placed, both[1:, None], (chip ^ 2, core, 0, 0))
        gain_rows = found.gains.reshape(2, fsdp_count, rows).transpose(1, 0, 2)
        gain_rows = gain_rows.reshape(fsdp_count, 1, 2 * rows).astype(bf16)
        gain_rows = jnp.pad(gain_rows, ((0, 0), (0, 15), (0, width // 2 - 2 * rows)))
        packed = jnp.concatenate([placed.reshape(fsdp_count, rows, width // 2), gain_rows], axis=1)
        return [
            spread(scatter_rows(fold(*halves(found.qkv))), False),
            spread(scatter_rows(packed.reshape(fsdp_count * (rows + 16), width // 2)), True),
            spread(scatter_rows(fold(*halves(found.up))), False),
            spread(scatter_rows(fold(*halves(found.down))), True),
        ]

    inputs, out_grads = sync(own_rows(tokens), own_rows(cotangent))
    of0, of1 = types.SimpleNamespace(), types.SimpleNamespace()

    def total(value):
        return jnp.sum(value).reshape(1, 1)

    def lanes(values, start):
        lane = lax.broadcasted_iota(jnp.int32, (1, LANES), 1)
        return sum(jnp.where(lane == start + i, value, 0.0) for i, value in enumerate(values))

    def with_lanes(row, values):
        if even:
            return row
        return jnp.concatenate([row[:, :LANES] + values, row[:, LANES:]], axis=1)

    masters = (w_qkv[0], w_out[0], w_up[0], w_down[0])
    gain_masters = (gain_attn, gain_mlp)
    state = types.SimpleNamespace(
        out_grads=out_grads,
        weight_totals=lanes([total(master * master) for master in masters + gain_masters], 2),
    )
    if even:

        def hook_forward0(point, value):
            if point == OUT:
                value, up, *parts = sync(value, up_gathered[0], *weights[0].out)
                weights[0].out = join_out(parts)
                weights[0].up = with_far(up)
            elif point == NORM:
                value, down = sync(value, down_gathered[0])
                weights[0].down = with_far(down)
            elif point == FEED0:
                value, far = sync(value, weights[0].up[1])
                weights[0].up = weights[0].up[0], far
            elif point == SEND:
                value, packed = sync(value, packed_gathered)
                near = packed.reshape(4, rows + 16, 4 * LANES)[:, :rows, : 3 * LANES]
                far = swap_y(near.reshape(4 * rows, 3 * LANES))
                weights[1].qkv = place_qkv([packed], [far], True)
                weights[1].out, gains[1] = place_out([packed], True)
            elif point == LAST:
                value, up = sync(value, up_gathered[1])
                weights[1].up = with_far(up)
            return value

        def hook_forward1(point, value):
            if point == OUT:
                value, down, *parts = sync(value, down_gathered[1], *weights[1].out)
                weights[1].out = join_out(parts)
                weights[1].down = with_far(down)
            elif point == NORM:
                value, far = sync(value, weights[1].up[1])
                weights[1].up = weights[1].up[0], far
            elif point == FEED0:
                value, far = sync(value, weights[1].down[1])
                weights[1].down = weights[1].down[0], far
            elif point == LAST:
                value, state.weight_totals = sync(value, state.weight_totals)
            return value

        def hook_backward1(point, value, *grads):
            if point == NORM:
                value, *down = sync(value, *grads[0])
                of1.down = halves(down)
            elif point == ATTEND0:
                value, *up = sync(value, *grads[0])
                of1.up_grads = up
            elif point == ATTEND1:
                value, *outputs = sync(value, *state.away)
                state.away = outputs
            elif point == STACKED:
                value, came, out, of1.gains = sync(value, of1.down[1], *grads)
                of1.down = scatter_rows(fold(of1.down[0], came))
                of1.up = halves(of1.up_grads)
                of1.out = out
            return value

        def hook_backward0(point, value, *grads):
            if point == FEED0:
                value, came, *qkv = sync(value, of1.up[1], *of1.qkv)
                of1.up = scatter_rows(fold(of1.up[0], came))
                of1.qkv = halves(qkv)
                of1.out = out_halves(of1.out)
            elif point == NORM:
                value, came, out_came, down, *grad_down = sync(
                    value, of1.qkv[1], of1.out[1], of1.down, *grads[0]
                )
                of1.qkv = of1.qkv[0], came
                of1.out = out_pair(of1.out[0], out_came)
                of1.down = spread_start(down, True)
                of0.down = halves(grad_down)
            elif point == ATTEND0:
                value, cross, up, *up_grads = sync(value, of1.out[1], of1.up, *grads[0])
                of1.packed = scatter_rows(pack(*of1.qkv, of1.out[0], cross, of1.gains))
                of1.up = up
                of0.up_grads = up_grads
            elif point == ATTEND1:
                value, came, hop, state.in_away = sync(
                    value, of0.down[1], of1.down[1], state.in_away
                )
                of0.down = scatter_rows(fold(of0.down[0], came))
                of0.up = halves(of0.up_grads)
                of1.up = spread_start(of1.up, False)
                of1.down = spread_end((of1.down[0], hop), True)
            elif point == STACKED:
                value, came, hop, packed, out, of0.gains, *ends = sync(
                    value, of0.up[1], of1.up[1], of1.packed, *grads, *of1.down
                )
                of0.up = scatter_rows(fold(of0.up[0], came))
                of1.up = of1.up[0], hop
                of1.down = ends
                of1.packed = spread_start(packed, False)
                of0.out = out_halves(out)
            elif point == SEND:
                value, out_came, hop = sync(value, of0.out[1], of1.packed[1])
                of0.out = out_pair(of0.out[0], out_came)
                of1.packed = of1.packed[0], hop
            elif point == LAST:
                value, of0.down = sync(value, of0.down)
            return value

    else:

        def hook_forward0(point, value):
            return value

        hook_forward1 = hook_forward0

        def hook_plain(found):
            def hook(point, value, *grads):
                if point == NORM:
                    found.down = grads[0]
                elif point == ATTEND0:
                    found.up = grads[0]
                elif point == STACKED:
                    found.out, found.gains = grads
                return value

            return hook

        hook_backward0, hook_backward1 = hook_plain(of0), hook_plain(of1)

    hidden0, saved0 = forward(inputs, 0, hook_forward0)
    hidden1, saved1 = forward(hidden0, 1, hook_forward1)
    state.away = [swap_y(hidden0[half:]), swap_y(hidden1[half:])]
    in_grads1, of1.qkv = backward(state.out_grads, saved1, 1, hook_backward1)
    state.in_away = swap_y(in_grads1[half:])
    in_grads0, of0.qkv = backward(in_grads1, saved0, 0, hook_backward0)
    if even:
        qkv_near, qkv_came = halves(of0.qkv)
        packed0 = pack(qkv_near, qkv_came, *of0.out, of0.gains)
        packed0, of0.up, of0.down = sync(packed0, of0.up, of0.down)
        packed0 = scatter_rows(packed0)
        of0.down, of0.up = spread_start(of0.down, True), spread_start(of0.up, False)
        down_hop, up_hop, *rest = sync(
            of0.down[1],
            of0.up[1],
            *of1.packed,
            *of1.up,
            hidden0,
            hidden1,
            in_grads0,
            in_grads1,
        )
        of1.packed, of1.up = rest[:2], rest[2:4]
        hidden0, hidden1, in_grads0, in_grads1 = rest[4:]
        near0 = [
            None,
            spread_end((of0.up[0], up_hop), False),
            spread_end((of0.down[0], down_hop), True),
        ]
        near1 = [spread_end(of1.packed, False), spread_end(of1.up, False), of1.down]
    else:
        near1, near0 = reduce_plain(of1), reduce_plain(of0)

    def to_owner(layer0, layer1, away):
        pairs = [jnp.stack([runs[:half], far]) for runs, far in zip((layer0, layer1), away)]
        keep = jnp.where(first_core, pairs[0], pairs[1])
        take = swap_core(jnp.where(first_core, pairs[1], pairs[0]))
        both = flipped(~first_core, jnp.stack([keep, take], axis=1), 1)
        return flipped(~first_y, both, 0).reshape(2, block, width)

    hidden_out = to_owner(hidden0, hidden1, state.away)
    in_grads_out = to_owner(in_grads0, in_grads1, [swap_y(in_grads0[half:]), state.in_away])

    def natural(position):
        layers = jnp.stack(near0[position]), jnp.stack(near1[position])
        near = jnp.where(first_core, layers[0], layers[1])
        far = jnp.where(first_core, swap_core(layers[0]), swap_core(layers[1]))
        both = jnp.stack([near, far], axis=1)
        shape = both.shape
        both = both.reshape((2, 2, 2) + shape[2:])
        both = flipped(~first_y, flipped(~first_x, flipped(~first_core, both, 2), 1), 0)
        return both.reshape((8,) + shape[2:])

    rows_old = (row_qkv, row_out, row_up, row_down)
    if even:
        where = jnp.stack([at_eighth, core]).astype(jnp.int32)

        def build(position, kind, olds, extra, shapes):
            return assemble(
                near0[position],
                near1[position],
                [swap_core(value) for value in near0[position]],
                [swap_core(value) for value in near1[position]],
                olds,
                extra,
                where,
                kind,
                shapes,
            )

        def column(row):
            return row.reshape(-1, 1)

        down = build(2, ROWS, [column(row_down)], jnp.zeros((1, LANES), f32), ((8 * unit, width),))
        up = build(
            1, COLUMNS, [column(row_up)], state.weight_totals, ((rows, hidden_width),)
        )
        near0[0] = spread(after(packed0, up[1], down[1]), False)
        built = [None, None, up[:2], down[:2]]
        sums = {2: jnp.concatenate([up[2], down[2]], axis=1)}
        places = {2: (0, LANES), 3: (LANES + 2 * hidden_width, 2 * LANES + 2 * hidden_width)}
        places.update({0: (0, LANES), 1: (1, LANES + 6 * width)})

        def build_first():
            first = build(
                0,
                PACKED,
                [after(column(row_qkv), sums[2]), column(row_out)],
                jnp.concatenate([var_attn, var_mlp], axis=1),
                ((rows, 3 * width), (rows, width)),
            )
            built[:2] = (first[0], first[2]), (first[1], first[3])
            sums[0] = first[5]
            return first[4].reshape(2, rows)

    else:
        qkv = natural(0).reshape(8, rows, 3, LANES).transpose(1, 2, 0, 3).reshape(rows, 3 * width)
        out = natural(1).reshape(2, 4, rows + 16, width // 2).astype(f32).sum(axis=1)
        gain_shard = out[:, rows].sum(axis=0)[: 2 * rows].reshape(2, rows)
        out = out[:, :rows].transpose(1, 0, 2).reshape(rows, width)
        up = natural(2).reshape(8, rows, fsdp_count, unit).transpose(1, 2, 0, 3)
        up = up.reshape(rows, hidden_width)
        down = natural(3).reshape(8 * unit, width)
        built, parts = [], []
        for gradient, row_old in zip((qkv, out, up, down), rows_old):
            gradient = gradient.astype(f32)
            square = gradient * gradient
            row_new = decay_rate * row_old.reshape(-1, 1) + (1.0 - decay_rate) * jnp.mean(
                square, axis=1, keepdims=True
            )
            built.append((gradient, row_new))
            total_new = jnp.pad(jnp.sum(row_new).reshape(1, 1), ((0, 0), (0, LANES - 1)))
            parts.append(
                [
                    total_new,
                    jnp.sum(square, axis=0, keepdims=True),
                    jnp.sum(square / row_new, axis=0, keepdims=True),
                ]
            )
        blank = jnp.zeros_like(parts[0][0])
        sums = {
            2: jnp.concatenate(parts[2] + parts[3], axis=1),
            0: jnp.concatenate([blank] + parts[0] + parts[1], axis=1),
        }
        places = {2: (0, LANES), 3: (LANES + 2 * hidden_width, 2 * LANES + 2 * hidden_width)}
        places.update(
            {0: (LANES, 2 * LANES), 1: (2 * LANES + 6 * width, 3 * LANES + 6 * width)}
        )

        def build_first():
            return gain_shard

    def sum_line(value):
        if fsdp_count != 4:
            return lax.psum(value, FSDP)
        near, two, three = rotations(value)[1:]
        return (value + two) + (near + three)

    cols_old = (col_qkv, col_out, col_up, col_down)
    moments_old = (var_attn, var_mlp)
    new_rows, new_cols, ratios, new_masters = [None] * 4, [None] * 4, [None] * 4, [None] * 4

    def update(position, summed, weight_total):
        gradient, row_new = built[position]
        at_total, start = places[position]
        cols = gradient.shape[1]
        row_count = gradient.shape[0] * fsdp_count
        entry_count = row_count * cols
        col_all = summed[:, start : start + cols]
        ratio_all = summed[:, start + cols : start + 2 * cols]
        row_mean = summed[:, at_total : at_total + 1] / row_count
        new_rows[position] = row_new.reshape(1, -1)
        new_cols[position] = (
            decay_rate * cols_old[position] + (1.0 - decay_rate) * col_all / row_count
        )
        ratios[position] = jnp.sqrt(
            row_mean * total(ratio_all / new_cols[position]) / entry_count
        )
        weight_scale = jnp.sqrt(weight_total / entry_count + weight_eps)
        factor = step_rate * weight_scale / jnp.maximum(1.0, ratios[position] / clip_level)
        raw = gradient * lax.rsqrt(row_new * new_cols[position] / row_mean)
        new_masters[position] = masters[position] - factor * raw

    early = sum_line(with_lanes(sums[2], state.weight_totals))
    gain_shard = build_first()
    moments, gain_updates = [], []
    for gain_pos in range(2):
        grad = gain_shard[gain_pos : gain_pos + 1]
        moment = decay_rate * moments_old[gain_pos] + (1.0 - decay_rate) * grad * grad
        moments.append(moment)
        gain_updates.append(grad * lax.rsqrt(moment))
    last = with_lanes(sums[0], lanes([total(step * step) for step in gain_updates], 2))
    summed, early = sum_line(last), after(early, last)
    weight_all = [early[:, 2 + i : 3 + i] for i in range(6)]
    for position in (2, 3):
        update(position, early, weight_all[position])
    for position in (0, 1):
        update(position, summed, weight_all[position])
    for gain_pos in range(2):
        clip_ratio = jnp.sqrt(summed[:, 2 + gain_pos : 3 + gain_pos] / width)
        weight_scale = jnp.sqrt(weight_all[4 + gain_pos] / width + weight_eps)
        factor = step_rate * weight_scale / jnp.maximum(1.0, clip_ratio / clip_level)
        new_masters.append(gain_masters[gain_pos] - factor * gain_updates[gain_pos])
        ratios.append(clip_ratio)
    return (
        hidden_out[None],
        in_grads_out[None],
        *[entry[0][None] for entry in built],
        gain_shard[:1],
        gain_shard[1:],
        *[master[None] for master in new_masters[:4]],
        new_masters[4],
        new_masters[5],
        new_rows[0],
        new_cols[0],
        new_rows[1],
        new_cols[1],
        new_rows[2],
        new_cols[2],
        new_rows[3],
        new_cols[3],
        moments[0],
        moments[1],
        jnp.concatenate(ratios, axis=1),
    )


def solution(mesh):
    in_specs = (
        P(FSDP, CTX, None),
        P(FSDP, CTX, None),
        P(FSDP, None),
        P(SECTION, FSDP, None),
        P(SECTION, FSDP, None),
        P(SECTION, FSDP, None),
        P(SECTION, FSDP, None),
        P(SECTION, FSDP),
        P(SECTION, FSDP),
        P(SECTION, FSDP),
        P(SECTION, None),
        P(SECTION, FSDP),
        P(SECTION, None),
        P(SECTION, FSDP),
        P(SECTION, None),
        P(SECTION, FSDP),
        P(SECTION, None),
        P(SECTION, FSDP),
        P(SECTION, FSDP),
    )
    out_specs = (
        P(SECTION, FSDP, CTX, None),
        P(SECTION, FSDP, CTX, None),
        P(SECTION, FSDP, None),
        P(SECTION, FSDP, None),
        P(SECTION, FSDP, None),
        P(SECTION, FSDP, None),
        P(SECTION, FSDP),
        P(SECTION, FSDP),
        P(SECTION, FSDP, None),
        P(SECTION, FSDP, None),
        P(SECTION, FSDP, None),
        P(SECTION, FSDP, None),
        P(SECTION, FSDP),
        P(SECTION, FSDP),
        P(SECTION, FSDP),
        P(SECTION, None),
        P(SECTION, FSDP),
        P(SECTION, None),
        P(SECTION, FSDP),
        P(SECTION, None),
        P(SECTION, FSDP),
        P(SECTION, None),
        P(SECTION, FSDP),
        P(SECTION, FSDP),
        P(SECTION, None),
    )
    return jax.shard_map(
        per_device, mesh=mesh, in_specs=in_specs, out_specs=out_specs, check_vma=False
    )
```
